32 devices in a mesh: sub: 8 (over z, y), rep: 4 (over x, core).
Axes of the slice: x: 2, y: 2, z: 4, core: 2. Of those that a mesh axis runs over, the one named last changes fastest.
Arguments:
- regions: bfloat16 [512, 128, 256], P('rep', 'sub'), may hold values from -6 to 6
- leaf_map: int32 [128], P('sub'), may hold values from 0 to 15, as said below
- leaf_bond_weight: bfloat16 [32, 4, 256, 1024], P(('sub', 'rep')), may hold values from -0.375 to 0.375
- mid_weight: bfloat16 [8, 4, 1024, 1024], P('sub', 'rep'), may hold values from -0.1875 to 0.1875
- upper_weight: bfloat16 [8, 1024, 2, 1024], P('sub'), may hold values from -0.1875 to 0.1875
- head_cotangent: float32 [512, 1024], P('rep', 'sub'), may hold values from -0.75 to 0.75
Outputs:
- leaf_grad: bfloat16 [32, 4, 256, 1024], P(('sub', 'rep'))
- middle_weight_gradient: bfloat16 [8, 4, 1024, 1024], P('sub', 'rep')
- upper_grad: bfloat16 [8, 1024, 2, 1024], P('sub', 'rep')
The draws below stay inside these ranges and needn't reach their ends.
Inputs may be any that keep to these rules, and one draw needn't show every extreme that they name: `leaf_map`: each aligned block of 16 entries is a permutation of 0 .. 15.
All inputs are finite; a program needn't handle non-finite values.
Results may differ from the reference program's by a relative error of at most 0.04.
Values may be sent and summed in bfloat16 or wider, within the bound.
No kernel may reach another device: no remote copies, remote signals or barrier semaphores. Data moves between devices by JAX's collectives and lax.ppermute only.
A program may use at most 128 MiB of HBM per device.

```python
import jax
import jax.numpy as jnp
from jax import lax

D = 1024
F = 256
REG_DEV = 16
BATCH = 512
REGIONS = 128
LEAF_NODES = 32
LEVELS = 3
N_SUB = 8


def draw_leaf_map(key, part):
    streams = jax.random.split(key, N_SUB)
    shuffles = jax.vmap(lambda stream: jax.random.permutation(stream, REG_DEV))(streams)
    return shuffles.reshape(N_SUB * REG_DEV).astype(jnp.int32)


def steps_of(rng, shape, pieces, least, largest):
    def one(dim, shards_of):
        steps = jax.random.uniform(jax.random.fold_in(jax.random.fold_in(rng, 6), dim), (shards_of,), jnp.float32, least / len(pieces), largest / len(pieces))
        return jnp.repeat(jnp.exp(steps), shape[dim] // shards_of).reshape((-1,) + (1,) * (len(shape) - dim - 1))

    level = one(*pieces[0])
    for cut in pieces[1:]:
        level = level * one(*cut)
    return level


def normal_values(stream_key, extent, deviation, bound, pieces=(), kind=jnp.bfloat16):
    values = jax.random.normal(stream_key, extent, jnp.float32) * deviation
    if len(pieces) > 0:
        values = steps_of(stream_key, extent, pieces, -0.22, 0.18) * values
    return jnp.clip(values, min=-bound, max=bound).astype(kind)


def setup_inputs(seed: int = 0) -> dict:
    splits = jax.random.split(jax.random.key(seed), 7)
    return {
        "regions": normal_values(splits[0], (BATCH, REGIONS, F), 1.0, 6.0, ((0, 4), (1, 8))),
        "leaf_map": draw_leaf_map(jax.random.fold_in(splits[6], 71), 0),
        "leaf_bond_weight": normal_values(splits[2], (LEAF_NODES, 4, F, D), F ** -0.5, 0.375, ((0, 32),)),
        "mid_weight": normal_values(splits[3], (N_SUB, 4, D, D), D ** -0.5, 0.1875, ((0, 8), (1, 4))),
        "upper_weight": normal_values(splits[4], (N_SUB, D, 2, D), D ** -0.5, 0.1875, ((0, 8),)),
        "head_cotangent": normal_values(splits[5], (BATCH, D), 0.05, 0.75, ((0, 4), (1, 8)), jnp.float32),
    }


EPSILON = 1e-06

def widen(array):
    return array.astype(jnp.float32)

def tensor_contraction(formula, left_arr, right_arr):
    return jnp.einsum(formula, widen(left_arr), widen(right_arr), precision=lax.Precision.HIGHEST)

def rms_factor(values):
    return lax.rsqrt(lax.optimization_barrier(jnp.mean(values * values, axis=-1, keepdims=True)) + EPSILON)

def norm_back(gradient, normed, factor):
    return factor * (gradient - normed * lax.optimization_barrier(jnp.mean(gradient * normed, axis=-1, keepdims=True)))

def product_of(factors):
    running = factors[..., 0, :]
    for position in range(1, factors.shape[-2]):
        running = running * factors[..., position, :]
    return running

def leave_one(factors):
    how_many = factors.shape[-2]
    results = []
    for position in range(how_many):
        remaining = [factors[..., partner_idx, :] for partner_idx in range(how_many) if partner_idx != position]
        running = remaining[0]
        for factor in remaining[1:]:
            running = running * factor
        results.append(running)
    return jnp.stack(results, axis=-2)

def subtree_parts(region_x, slot_map, leaf_w, middle_weight):
    batch_rows = region_x.shape[0]
    placed = jnp.take(region_x, slot_map, axis=1).reshape(batch_rows, 4, 4, F)
    leaf_terms = tensor_contraction('bnkf,nkfd->bnkd', placed, leaf_w)
    leaf_prod = product_of(1.0 + leaf_terms)
    leaf_scale = rms_factor(leaf_prod)
    leaf_norm = leaf_prod * leaf_scale
    leaf_message_rows = leaf_norm.astype(jnp.bfloat16)
    middle_node_terms = tensor_contraction('zpc,pci->zpi', leaf_message_rows, middle_weight).astype(jnp.bfloat16)
    mid_factors = 1.0 + widen(middle_node_terms)
    mid_prod = product_of(mid_factors)
    mid_scale = rms_factor(mid_prod)
    mid_norm = mid_prod * mid_scale
    sub_msg = mid_norm.astype(jnp.bfloat16)
    return (placed, leaf_terms, leaf_scale, leaf_norm, leaf_message_rows, mid_factors, mid_scale, mid_norm, sub_msg)

def subtree_grads(region_x, slot_map, leaf_w, middle_weight, sub_grad_in):
    placed, leaf_terms, leaf_scale, leaf_norm, leaf_message_rows, mid_factors, mid_scale, mid_norm, sub_msg = subtree_parts(region_x, slot_map, leaf_w, middle_weight)
    mid_back = norm_back(sub_grad_in, mid_norm, mid_scale)
    middle_gradient_list = (mid_back[:, None, :] * leave_one(mid_factors)).astype(jnp.bfloat16)
    middle_weight_gradient = tensor_contraction('sax,sav->axv', leaf_message_rows, middle_gradient_list).astype(jnp.bfloat16)
    leaf_backward_pass = tensor_contraction('xym,yam->xya', middle_gradient_list, middle_weight)
    node_back = norm_back(leaf_backward_pass, leaf_norm, leaf_scale)
    leaf_weight_gradients = (node_back[:, :, None, :] * leave_one(1.0 + leaf_terms)).astype(jnp.bfloat16)
    leaf_grad = tensor_contraction('bnkf,bnkd->nkfd', placed, leaf_weight_gradients).astype(jnp.bfloat16)
    return (leaf_grad, middle_weight_gradient)

def reference(regions, leaf_map, leaf_bond_weight, mid_weight, upper_weight, head_cotangent):
    batch_rows = regions.shape[0]
    region_sets = jnp.transpose(regions.reshape(batch_rows, N_SUB, REG_DEV, F), (1, 0, 2, 3))
    slot_maps = leaf_map.reshape(N_SUB, REG_DEV).astype(jnp.int32)
    leaf_sets = leaf_bond_weight.reshape(N_SUB, 4, 4, F, D)
    messages = lax.map(lambda packed: subtree_parts(*packed)[-1], (region_sets, slot_maps, leaf_sets, mid_weight))
    records = []
    for tier_level in range(LEVELS):
        group_size = 2 ** (tier_level + 1)
        block_width = D // group_size
        first_col = D - 2 * block_width
        groups = N_SUB // group_size
        block = upper_weight[:, :, :, first_col:first_col + block_width].reshape(groups, group_size, D, 2, block_width)
        weights = jnp.transpose(block, (0, 2, 3, 1, 4)).reshape(groups, D, 2, D)
        left_msg = messages[0::2]
        right_msg = messages[1::2]
        up_left = tensor_contraction('gbi,gio->gbo', left_msg, weights[:, :, 0, :])
        up_right = tensor_contraction('gbi,gio->gbo', right_msg, weights[:, :, 1, :])
        joined = (1.0 + up_left) * (1.0 + up_right)
        scaling = rms_factor(joined)
        messages = (joined * scaling).astype(jnp.bfloat16)
        records.append((group_size, block_width, groups, weights, left_msg, right_msg, up_left, up_right, scaling))
    root_msg = messages[0]
    head_width = D // N_SUB
    head_maps = jnp.transpose(upper_weight[:, :, :, D - head_width:], (1, 2, 0, 3)).reshape(D, 2, D)
    head_left = head_maps[:, 0, :]
    head_right = head_maps[:, 1, :]
    head_value = tensor_contraction('bi,io->bo', root_msg, head_left)
    head_gate = tensor_contraction('bi,io->bo', root_msg, head_right)
    gating = jax.nn.sigmoid(head_gate)
    grad_value = (head_cotangent * gating).astype(jnp.bfloat16)
    grad_gate = (head_cotangent * head_value * gating * (1.0 - gating)).astype(jnp.bfloat16)
    root_grad_msg = tensor_contraction('bo,io->bi', grad_value, head_left) + tensor_contraction('bo,io->bi', grad_gate, head_right)
    head_full = jnp.stack([tensor_contraction('bi,bo->io', root_msg, grad_value), tensor_contraction('bi,bo->io', root_msg, grad_gate)], axis=1)
    head_piece = jnp.transpose(head_full.reshape(D, 2, N_SUB, head_width), (2, 0, 1, 3))
    level_pieces = [None] * LEVELS
    grad_msgs = root_grad_msg[None]
    for tier_level in reversed(range(LEVELS)):
        group_size, block_width, groups, weights, left_msg, right_msg, up_left, up_right, scaling = records[tier_level]
        normed = (1.0 + up_left) * (1.0 + up_right) * scaling
        joined_grad = norm_back(grad_msgs, normed, scaling)
        grad_left = (joined_grad * (1.0 + up_right)).astype(jnp.bfloat16)
        grad_right = (joined_grad * (1.0 + up_left)).astype(jnp.bfloat16)
        node_grad = jnp.stack([tensor_contraction('gbi,gbo->gio', left_msg, grad_left), tensor_contraction('gbi,gbo->gio', right_msg, grad_right)], axis=2)
        node_piece = jnp.transpose(node_grad.reshape(groups, D, 2, group_size, block_width), (0, 3, 1, 2, 4)).reshape(N_SUB, D, 2, block_width)
        level_pieces[tier_level] = node_piece
        to_left = tensor_contraction('gbo,gio->gbi', grad_left, weights[:, :, 0, :])
        to_right = tensor_contraction('gbo,gio->gbi', grad_right, weights[:, :, 1, :])
        grad_msgs = jnp.stack([to_left, to_right], axis=1).reshape(2 * groups, batch_rows, D)
    upper_sum = jnp.concatenate(level_pieces + [head_piece], axis=-1)
    leaf_weight_gradients, middle_gradient_list = lax.map(lambda packed: subtree_grads(*packed), (region_sets, slot_maps, leaf_sets, mid_weight, grad_msgs))
    leaf_grad = leaf_weight_gradients.reshape(N_SUB * 4, 4, F, D)
    return (leaf_grad, middle_gradient_list, upper_sum.astype(jnp.bfloat16))
```

```python
import functools

import jax
import jax.numpy as jnp
from jax import lax
from jax.experimental import pallas as pl
from jax.experimental.pallas import tpu as pltpu
from jax.sharding import PartitionSpec as P

EPSILON = 1e-06
CHILDREN = 4
MIB = 1024 * 1024


def partner(value, axis, offset):
    return lax.ppermute(value, axis, [(i, i ^ offset) for i in range(lax.axis_size(axis))])


def rms_factor(values):
    return lax.rsqrt(jnp.mean(values * values, axis=-1, keepdims=True) + EPSILON)


def norm_back(gradient, normed, factor):
    return factor * (gradient - normed * jnp.mean(gradient * normed, axis=-1, keepdims=True))


def matmul(left_arr, right_arr):
    return jnp.dot(left_arr, right_arr, preferred_element_type=jnp.float32)


def matmul_t(left_arr, right_arr):
    return lax.dot_general(
        left_arr, right_arr, (((1,), (1,)), ((), ())), preferred_element_type=jnp.float32
    )


def inner_t(left_arr, right_arr):
    return lax.dot_general(
        left_arr, right_arr, (((0,), (0,)), ((), ())), preferred_element_type=jnp.float32
    )


def bf16(value):
    return value.astype(jnp.bfloat16)


def f32(value):
    return value.astype(jnp.float32)


def join_rows(first, second, axis):
    if axis == 0 and first.ndim > 2 or first.shape[axis] % 16 == 0:
        return jnp.concatenate([first, second], axis=axis)
    first, second = lax.optimization_barrier((f32(first), f32(second)))
    return bf16(lax.optimization_barrier(jnp.concatenate([first, second], axis=axis)))


def whole_block():
    return pl.BlockSpec(memory_space=pltpu.VMEM)


def place_kernel(slots, ids_ref, map_ref, regions_ref, *rest):
    outs, wide = rest[:CHILDREN], rest[CHILDREN]
    rows = regions_ref.shape[0] // slots
    parts = wide.shape[0]
    for part in range(parts):
        wide[part] = regions_ref[:, part * 128 : (part + 1) * 128].astype(jnp.float32)
    row = lax.broadcasted_iota(jnp.int32, (rows, rows), 0)
    col = lax.broadcasted_iota(jnp.int32, (rows, rows), 1)
    select = (jnp.bitwise_xor(row, ids_ref[1]) == col).astype(jnp.bfloat16)
    for offset in range(CHILDREN):
        node = jnp.bitwise_xor(ids_ref[0], offset)
        for child in range(CHILDREN):
            region = map_ref[node * CHILDREN + child]
            for part in range(parts):
                values = wide[part, pl.ds(region, rows, stride=slots), :].astype(jnp.bfloat16)
                outs[offset][child, :, part * 128 : (part + 1) * 128] = matmul(
                    select, values
                ).astype(jnp.bfloat16)


def place(regions, leaf_map, ids):
    rows, slots, feats = regions.shape
    flat = regions.reshape(rows * slots, feats)
    smem = pl.BlockSpec(memory_space=pltpu.SMEM)
    return pl.pallas_call(
        functools.partial(place_kernel, slots),
        out_shape=[jax.ShapeDtypeStruct((CHILDREN, rows, feats), jnp.bfloat16)] * CHILDREN,
        in_specs=[smem, smem, whole_block()],
        out_specs=[whole_block()] * CHILDREN,
        scratch_shapes=[pltpu.VMEM((feats // 128, rows * slots, 128), jnp.float32)],
        compiler_params=pltpu.CompilerParams(vmem_limit_bytes=16 * MIB),
        name="place",
    )(ids, leaf_map, flat)


def leaf_forward_kernel(count, *refs):
    placed, leaf_w, mid_w = refs[:count], refs[count], refs[count + 1]
    msgs, terms = refs[count + 2 : 2 * count + 2], refs[2 * count + 2 :]
    rows = placed[0].shape[1]
    product = None
    for child in range(CHILDREN):
        values = jnp.concatenate([ref[child] for ref in placed], axis=0)
        factor = 1.0 + matmul(values, leaf_w[child])
        product = factor if product is None else product * factor
    message = bf16(product * rms_factor(product))
    out = bf16(matmul(message, mid_w[...]))
    for i in range(count):
        msgs[i][...] = message[i * rows : (i + 1) * rows]
        terms[i][...] = out[i * rows : (i + 1) * rows]


def leaf_forward(placed, leaf_w, mid_w):
    count = len(placed)
    rows = placed[0].shape[1]
    width = mid_w.shape[0]
    return pl.pallas_call(
        functools.partial(leaf_forward_kernel, count),
        out_shape=[jax.ShapeDtypeStruct((rows, width), jnp.bfloat16)] * (2 * count),
        in_specs=[whole_block()] * (count + 2),
        out_specs=[whole_block()] * (2 * count),
        compiler_params=pltpu.CompilerParams(vmem_limit_bytes=24 * MIB),
        name="leaf_forward",
    )(*placed, leaf_w, mid_w)


def leaf_backward_kernel(*refs):
    placed, msgs, grads = refs[0:4], refs[4:8], refs[8:12]
    leaf_w, mid_w, leaf_out, mid_out, cot = refs[12:17]
    rows = placed[0].shape[1]
    for pair in range(2):
        chunk = [2 * pair, 2 * pair + 1]
        factors = [
            1.0 + matmul(jnp.concatenate([placed[c][child] for c in chunk], axis=0), leaf_w[child])
            for child in range(CHILDREN)
        ]
        low = factors[0] * factors[1]
        high = factors[2] * factors[3]
        product = low * high
        scale = rms_factor(product)
        back = matmul_t(jnp.concatenate([grads[c][...] for c in chunk], axis=0), mid_w[...])
        node = norm_back(back, product * scale, scale)
        node_high = node * high
        node_low = node * low
        where = slice(pair * 2 * rows, (pair + 1) * 2 * rows)
        cot[0, where] = bf16(node_high * factors[1])
        cot[1, where] = bf16(node_high * factors[0])
        cot[2, where] = bf16(node_low * factors[3])
        cot[3, where] = bf16(node_low * factors[2])
    all_grads = jnp.concatenate([ref[...] for ref in grads], axis=0)
    all_msgs = jnp.concatenate([ref[...] for ref in msgs], axis=0)
    mid_out[...] = bf16(inner_t(all_msgs, all_grads))
    for child in range(CHILDREN):
        values = jnp.concatenate([ref[child] for ref in placed], axis=0)
        leaf_out[child] = bf16(inner_t(values, cot[child]))


def leaf_backward(placed, msgs, grads, leaf_w, mid_w):
    rows = placed[0].shape[1]
    return pl.pallas_call(
        leaf_backward_kernel,
        out_shape=[
            jax.ShapeDtypeStruct(leaf_w.shape, jnp.bfloat16),
            jax.ShapeDtypeStruct(mid_w.shape, jnp.bfloat16),
        ],
        in_specs=[whole_block()] * 14,
        out_specs=[whole_block()] * 2,
        scratch_shapes=[pltpu.VMEM((CHILDREN, 4 * rows, mid_w.shape[0]), jnp.bfloat16)],
        compiler_params=pltpu.CompilerParams(vmem_limit_bytes=48 * MIB),
        name="leaf_backward",
    )(*placed, *msgs, *grads, leaf_w, mid_w)


def swap_blocks(array, size, axis):
    count = array.shape[axis] // size
    parts = [lax.slice_in_dim(array, i * size, (i + 1) * size, axis=axis) for i in range(count)]
    return jnp.concatenate([parts[i ^ 1] for i in range(count)], axis=axis)


def reverse_bits(value, count):
    out = 0
    for i in range(count):
        out = out * 2 + (value >> i) % 2
    return out


def assemble_kernel(group_bits, ids_ref, mine_ref, other_ref, out_ref):
    half, width = mine_ref.shape
    size = width >> group_bits
    for ref, core in ((mine_ref, ids_ref[0]), (other_ref, 1 - ids_ref[0])):
        rows = pl.ds(pl.multiple_of(core * half, half), half)
        for position in range(1 << group_bits):
            block = jnp.bitwise_xor(ids_ref[1], reverse_bits(position, group_bits))
            cols = pl.ds(pl.multiple_of(block * size, size), size)
            out_ref[rows, cols] = ref[:, position * size : (position + 1) * size]


def assemble(mine, other, core, block, group_bits):
    half, width = mine.shape
    size = width >> group_bits
    if size % 128 == 0:
        ids = jnp.stack([core, block]).astype(jnp.int32)
        return pl.pallas_call(
            functools.partial(assemble_kernel, group_bits),
            out_shape=jax.ShapeDtypeStruct((2 * half, width), mine.dtype),
            in_specs=[pl.BlockSpec(memory_space=pltpu.SMEM), whole_block(), whole_block()],
            out_specs=whole_block(),
            compiler_params=pltpu.CompilerParams(vmem_limit_bytes=16 * MIB),
            name="assemble",
        )(ids, mine, other)
    full = jnp.where(
        core == 1, jnp.concatenate([other, mine], axis=0), jnp.concatenate([mine, other], axis=0)
    )
    for i in range(group_bits):
        span = width >> (i + 1)
        full = jnp.where((block >> i) % 2 == 1, swap_blocks(full, span, 1), full)
    order = [reverse_bits(i, group_bits) for i in range(1 << group_bits)]
    return jnp.concatenate([full[:, i * size : (i + 1) * size] for i in order], axis=1)


def gather_maps(maps, sub_index, core, depth):
    width = maps.shape[1]
    half = width // 2
    own_rows = lax.dynamic_slice_in_dim(maps, core * half, half, 1)
    state = [None] * depth
    for stage in reversed(range(depth)):
        span = width >> (stage + 1)
        first = width - 2 * span
        side = (sub_index >> stage) % 2
        block = own_rows[:, :, first : first + span]
        mine = jnp.where(side == 1, block[1], block[0])
        send = jnp.where(side == 1, block[0], block[1])
        if stage > 0:
            for level in range(stage + 1, depth):
                send = jnp.concatenate([send, state[level]], axis=1)
            got = partner(send, "sub", 1 << stage)
            state[stage] = jnp.concatenate([mine, got[:, :span]], axis=1)
            at = span
            for level in range(stage + 1, depth):
                size = state[level].shape[1]
                state[level] = jnp.concatenate([state[level], got[:, at : at + size]], axis=1)
                at += size
        else:
            state[0] = jnp.concatenate([mine, partner(send, "sub", 1)], axis=1)
    if depth > 1:
        merged = jnp.concatenate(state[1:], axis=1)
        got = partner(merged, "sub", 1)
        at = 0
        for level in range(1, depth):
            size = state[level].shape[1]
            state[level] = jnp.concatenate([state[level], got[:, at : at + size]], axis=1)
            at += size
    others = [partner(state[0], "rep", 1)]
    if depth > 1:
        got = partner(jnp.stack(state[1:]), "rep", 1)
        others += [got[i] for i in range(depth - 1)]
    return [
        assemble(state[level], others[level], core, sub_index % (2 << level), level + 1)
        for level in range(depth)
    ]


def on_device(regions, leaf_map, leaf_bond_weight, mid_weight, upper_weight, head_cotangent):
    rows = regions.shape[0]
    width = upper_weight.shape[1]
    sub_count = lax.axis_size("sub")
    depth = sub_count.bit_length() - 1
    sub_index = lax.axis_index("sub")
    rep_index = lax.axis_index("rep")
    core = rep_index % 2
    far = rep_index // 2
    bits = [(sub_index >> level) % 2 == 1 for level in range(depth)]
    flip = sum(((sub_index >> level) % 2) * (rows >> (level + 1)) for level in range(depth))
    leaf_w = leaf_bond_weight[0]
    mid_w = mid_weight[0, 0]

    ids = jnp.stack([rep_index, flip]).astype(jnp.int32)
    sent = place(regions, leaf_map, ids)
    far_both = partner(sent[3], "rep", 3)
    far_one = partner(sent[2], "rep", 2)
    near = partner(sent[1], "rep", 1)
    placed = [sent[0], near, far_one, far_both]

    maps = jnp.transpose(upper_weight[0], (1, 0, 2))
    cotangent = head_cotangent
    for level in range(depth):
        cotangent = jnp.where(
            bits[level], swap_blocks(cotangent, rows >> (level + 1), 0), cotangent
        )
    weights = gather_maps(maps, sub_index, core, depth)

    msg0, msg1, term0, term1 = leaf_forward(placed[:2], leaf_w, mid_w)
    near0 = f32(partner(term1, "rep", 1))
    msg2, msg3, term2, term3 = leaf_forward(placed[2:], leaf_w, mid_w)
    near2 = f32(partner(term3, "rep", 1))
    own0, own2 = 1.0 + f32(term0), 1.0 + f32(term2)
    near0, near2 = 1.0 + near0, 1.0 + near2
    pair0 = own0 * near0
    far_pair0 = f32(partner(bf16(own2 * near2), "rep", 2))
    mid_prod = pair0 * far_pair0
    mid_scale = rms_factor(mid_prod)
    mid_norm = mid_prod * mid_scale
    message = bf16(mid_norm)

    saved = []
    for level in range(depth):
        keep = rows >> (level + 1)
        own_up = matmul(message, weights[level])
        other_up = 1.0 + f32(partner(bf16(own_up[keep:]), "sub", 1 << level))
        own_up = 1.0 + own_up[:keep]
        joined = own_up * other_up
        scaling = rms_factor(joined)
        saved.append((message, own_up, other_up, joined * scaling, scaling))
        message = bf16(joined * scaling)

    root = message
    for level in reversed(range(depth)):
        root = join_rows(root, partner(root, "sub", 1 << level), 0)
    head_width = width // sub_count
    head_col = width - head_width
    head_left = maps[0, :, head_col:]
    head_right = maps[1, :, head_col:]
    head_value = matmul(root, head_left)
    gating = jax.nn.sigmoid(matmul(root, head_right))
    grad_value = bf16(cotangent * gating)
    grad_gate = bf16(cotangent * head_value * gating * (1.0 - gating))
    grad_msg = matmul_t(grad_value, head_left) + matmul_t(grad_gate, head_right)
    for level in range(depth):
        keep = rows >> (level + 1)
        grad_msg = grad_msg[:keep] + f32(partner(bf16(grad_msg[keep:]), "sub", 1 << level))

    grads = [None] * depth
    for level in reversed(range(depth)):
        _, own_up, other_up, normed, scaling = saved[level]
        joined_grad = norm_back(grad_msg, normed, scaling)
        other_grad = partner(bf16(joined_grad * own_up), "sub", 1 << level)
        grads[level] = join_rows(bf16(joined_grad * other_up), other_grad, 0)
        grad_msg = matmul_t(grads[level], weights[level])

    sub_back = norm_back(grad_msg, mid_norm, mid_scale)
    pair_back2 = f32(partner(bf16(sub_back * pair0), "rep", 2))
    pair_back0 = sub_back * far_pair0
    back0, back2 = bf16(pair_back0 * near0), bf16(pair_back2 * near2)
    back1 = partner(bf16(pair_back0 * own0), "rep", 1)
    back3 = partner(bf16(pair_back2 * own2), "rep", 1)
    leaf_grad, mid_grad = leaf_backward(
        placed, [msg0, msg1, msg2, msg3], [back0, back1, back2, back3], leaf_w, mid_w
    )

    inputs = [entry[0][None] for entry in saved]
    for stage in reversed(range(depth)):
        levels = list(range(stage, depth))
        sizes = [inputs[i].shape[0] * inputs[i].shape[1] for i in levels]
        send = jnp.concatenate([inputs[i].reshape(-1, width) for i in levels], axis=0)
        got = partner(send, "sub", 1 << stage)
        at = 0
        for i, size in zip(levels, sizes):
            part = got[at : at + size].reshape(inputs[i].shape)
            inputs[i] = join_rows(inputs[i], part, 0 if i == stage else 1)
            at += size

    outgoing = [grad[None] for grad in grads]

    def exchange(stage, levels):
        keeps, sends = [], []
        for i in levels:
            half = outgoing[i].shape[2] // 2
            low, high = outgoing[i][:, :, :half], outgoing[i][:, :, half:]
            keeps.append(jnp.where(bits[stage], high, low))
            sends.append(jnp.where(bits[stage], low, high))
        got = partner(
            jnp.concatenate([part.reshape(-1, 128) for part in sends], axis=0), "sub", 1 << stage
        )
        at = 0
        for i, keep in zip(levels, keeps):
            size = keep.size // 128
            part = got[at : at + size].reshape(keep.shape)
            outgoing[i] = join_rows(keep, part, 0 if i == stage else 1)
            at += size

    for stage in reversed(range(1, depth)):
        exchange(stage, list(range(stage, depth)))
    if depth > 1:
        exchange(0, list(range(1, depth)))
    exchange(0, [0])

    def by_rep(values):
        return values.reshape(values.shape[0], 2, 2, width // 4)

    def sides(level, pair):
        if level == depth:
            return pair
        return [jnp.where(bits[level], pair[1 - i], pair[i]) for i in range(2)]

    def rep_sum(levels):
        near_parts, far_parts = [], []
        for level in levels:
            if level == depth:
                x_pair, g_pair = [root, root], [grad_value, grad_gate]
            else:
                x_pair = [inputs[level][i] for i in range(2)]
                g_pair = [outgoing[level][i] for i in range(2)]
            x_pair, g_pair = sides(level, x_pair), sides(level, g_pair)
            kept, given = [], []
            for x_side, g_side in zip(x_pair, g_pair):
                x_side = by_rep(x_side)
                low, high = x_side[:, :, 0], x_side[:, :, 1]
                keep = jnp.where(core == 1, high, low).reshape(rows, -1)
                give = jnp.where(core == 1, low, high).reshape(rows, -1)
                kept.append(inner_t(keep, g_side))
                given.append(bf16(inner_t(give, g_side)))
            near_parts.append(jnp.stack(kept))
            far_parts.append(jnp.stack(given))
        kept = jnp.concatenate(near_parts, axis=2)
        total = kept + f32(partner(jnp.concatenate(far_parts, axis=2), "rep", 1))
        quarter = width // 4
        low, high = total[:, :quarter], total[:, quarter:]
        keep = jnp.where(far == 1, high, low)
        give = jnp.where(far == 1, low, high)
        return bf16(keep + f32(partner(bf16(give), "rep", 2)))

    upper = rep_sum(list(range(1, depth + 1)))
    upper = jnp.concatenate([rep_sum([0]), upper], axis=2)
    upper = jnp.transpose(upper, (1, 0, 2))
    return leaf_grad[None], mid_grad[None, None], upper[None]


def solution(mesh):
    placed = (
        P("rep", "sub", None),
        P("sub"),
        P(("sub", "rep"), None, None, None),
        P("sub", "rep", None, None),
        P("sub", None, None, None),
        P("rep", "sub"),
    )
    return jax.shard_map(
        on_device,
        mesh=mesh,
        in_specs=placed,
        out_specs=(
            P(("sub", "rep"), None, None, None),
            P("sub", "rep", None, None),
            P("sub", "rep", None, None),
        ),
        check_vma=False,
    )
```

```python
import functools

import jax
import jax.numpy as jnp
from jax import lax
from jax.experimental import pallas as pl
from jax.experimental.pallas import tpu as pltpu
from jax.sharding import PartitionSpec as P

EPSILON = 1e-06
CHILDREN = 4
MIB = 1024 * 1024


def partner(value, axis, offset):
    return lax.ppermute(value, axis, [(i, i ^ offset) for i in range(lax.axis_size(axis))])


def rms_factor(values):
    return lax.rsqrt(jnp.mean(values * values, axis=-1, keepdims=True) + EPSILON)


def norm_back(gradient, normed, factor):
    return factor * (gradient - normed * jnp.mean(gradient * normed, axis=-1, keepdims=True))


def matmul(left_arr, right_arr):
    return jnp.dot(left_arr, right_arr, preferred_element_type=jnp.float32)


def matmul_t(left_arr, right_arr):
    return lax.dot_general(
        left_arr, right_arr, (((1,), (1,)), ((), ())), preferred_element_type=jnp.float32
    )


def inner_t(left_arr, right_arr):
    return lax.dot_general(
        left_arr, right_arr, (((0,), (0,)), ((), ())), preferred_element_type=jnp.float32
    )


def bf16(value):
    return value.astype(jnp.bfloat16)


def f32(value):
    return value.astype(jnp.float32)


def whole_block():
    return pl.BlockSpec(memory_space=pltpu.VMEM)


def place_kernel(slots, ids_ref, map_ref, regions_ref, *rest):
    outs, wide = rest[:CHILDREN], rest[CHILDREN]
    rows = regions_ref.shape[0] // slots
    parts = wide.shape[0]
    for part in range(parts):
        wide[part] = regions_ref[:, part * 128 : (part + 1) * 128].astype(jnp.float32)
    row = lax.broadcasted_iota(jnp.int32, (rows, rows), 0)
    col = lax.broadcasted_iota(jnp.int32, (rows, rows), 1)
    select = (jnp.bitwise_xor(row, ids_ref[1]) == col).astype(jnp.bfloat16)
    for offset in range(CHILDREN):
        node = jnp.bitwise_xor(ids_ref[0], offset)
        for child in range(CHILDREN):
            region = map_ref[node * CHILDREN + child]
            for part in range(parts):
                values = wide[part, pl.ds(region, rows, stride=slots), :].astype(jnp.bfloat16)
                outs[offset][child, :, part * 128 : (part + 1) * 128] = matmul(
                    select, values
                ).astype(jnp.bfloat16)


def place(regions, leaf_map, ids):
    rows, slots, feats = regions.shape
    flat = regions.reshape(rows * slots, feats)
    smem = pl.BlockSpec(memory_space=pltpu.SMEM)
    return pl.pallas_call(
        functools.partial(place_kernel, slots),
        out_shape=[jax.ShapeDtypeStruct((CHILDREN, rows, feats), jnp.bfloat16)] * CHILDREN,
        in_specs=[smem, smem, whole_block()],
        out_specs=[whole_block()] * CHILDREN,
        scratch_shapes=[pltpu.VMEM((feats // 128, rows * slots, 128), jnp.float32)],
        compiler_params=pltpu.CompilerParams(vmem_limit_bytes=16 * MIB),
        name="place",
    )(ids, leaf_map, flat)


def leaf_forward_kernel(count, *refs):
    placed, leaf_w, mid_w = refs[:count], refs[count], refs[count + 1]
    msgs, terms = refs[count + 2 : 2 * count + 2], refs[2 * count + 2 :]
    rows = placed[0].shape[1]
    product = None
    for child in range(CHILDREN):
        values = jnp.concatenate([ref[child] for ref in placed], axis=0)
        factor = 1.0 + matmul(values, leaf_w[child])
        product = factor if product is None else product * factor
    message = bf16(product * rms_factor(product))
    out = bf16(matmul(message, mid_w[...]))
    for i in range(count):
        msgs[i][...] = message[i * rows : (i + 1) * rows]
        terms[i][...] = out[i * rows : (i + 1) * rows]


def leaf_forward(placed, leaf_w, mid_w):
    count = len(placed)
    rows = placed[0].shape[1]
    width = mid_w.shape[0]
    return pl.pallas_call(
        functools.partial(leaf_forward_kernel, count),
        out_shape=[jax.ShapeDtypeStruct((rows, width), jnp.bfloat16)] * (2 * count),
        in_specs=[whole_block()] * (count + 2),
        out_specs=[whole_block()] * (2 * count),
        compiler_params=pltpu.CompilerParams(vmem_limit_bytes=24 * MIB),
        name="leaf_forward",
    )(*placed, leaf_w, mid_w)


def leaf_backward_kernel(*refs):
    placed, msgs, grads = refs[0:4], refs[4:8], refs[8:12]
    leaf_w, mid_w, leaf_out, mid_out, cot = refs[12:17]
    rows = placed[0].shape[1]
    for pair in range(2):
        chunk = [2 * pair, 2 * pair + 1]
        factors = [
            1.0 + matmul(jnp.concatenate([placed[c][child] for c in chunk], axis=0), leaf_w[child])
            for child in range(CHILDREN)
        ]
        low = factors[0] * factors[1]
        high = factors[2] * factors[3]
        product = low * high
        scale = rms_factor(product)
        back = matmul_t(jnp.concatenate([grads[c][...] for c in chunk], axis=0), mid_w[...])
        node = norm_back(back, product * scale, scale)
        node_high = node * high
        node_low = node * low
        where = slice(pair * 2 * rows, (pair + 1) * 2 * rows)
        cot[0, where] = bf16(node_high * factors[1])
        cot[1, where] = bf16(node_high * factors[0])
        cot[2, where] = bf16(node_low * factors[3])
        cot[3, where] = bf16(node_low * factors[2])
    all_grads = jnp.concatenate([ref[...] for ref in grads], axis=0)
    all_msgs = jnp.concatenate([ref[...] for ref in msgs], axis=0)
    mid_out[...] = bf16(inner_t(all_msgs, all_grads))
    for child in range(CHILDREN):
        values = jnp.concatenate([ref[child] for ref in placed], axis=0)
        leaf_out[child] = bf16(inner_t(values, cot[child]))


def leaf_backward(placed, msgs, grads, leaf_w, mid_w):
    rows = placed[0].shape[1]
    return pl.pallas_call(
        leaf_backward_kernel,
        out_shape=[
            jax.ShapeDtypeStruct(leaf_w.shape, jnp.bfloat16),
            jax.ShapeDtypeStruct(mid_w.shape, jnp.bfloat16),
        ],
        in_specs=[whole_block()] * 14,
        out_specs=[whole_block()] * 2,
        scratch_shapes=[pltpu.VMEM((CHILDREN, 4 * rows, mid_w.shape[0]), jnp.bfloat16)],
        compiler_params=pltpu.CompilerParams(vmem_limit_bytes=48 * MIB),
        name="leaf_backward",
    )(*placed, *msgs, *grads, leaf_w, mid_w)


def fused(body, name, *args):
    if any(arg.shape[-2] % 16 for arg in args):
        return body(*args)
    shapes = jax.eval_shape(body, *args)

    def kernel(*refs):
        results = body(*[ref[...] for ref in refs[: len(args)]])
        for ref, result in zip(refs[len(args) :], results):
            ref[...] = result

    return pl.pallas_call(
        kernel,
        out_shape=shapes,
        in_specs=[whole_block()] * len(args),
        out_specs=[whole_block()] * len(shapes),
        compiler_params=pltpu.CompilerParams(vmem_limit_bytes=24 * MIB),
        name=name,
    )(*args)


def ids_of(*values):
    return jnp.stack(values).astype(jnp.int32)


def smem_block():
    return pl.BlockSpec(memory_space=pltpu.SMEM)


def reverse_bits(value, count):
    out = 0
    for i in range(count):
        out = out * 2 + (value >> i) % 2
    return out


def join(pieces):
    if pieces[0].shape[0] % 16 == 0:
        return jnp.concatenate(pieces, axis=0)
    wide = lax.optimization_barrier(tuple(f32(piece) for piece in pieces))
    return bf16(lax.optimization_barrier(jnp.concatenate(wide, axis=0)))


def cut_kernel(depth, ids_ref, maps_ref, *outs):
    width = maps_ref.shape[1]
    half = width // 2
    rows = pl.ds(pl.multiple_of(ids_ref[0] * half, half), half)
    for level in range(depth):
        span = width >> (level + 1)
        cols = pl.ds(width - 2 * span, span)
        side = ids_ref[1 + level]
        outs[3 * level][...] = maps_ref[side, :, cols]
        outs[3 * level + 1][...] = maps_ref[side, rows, cols]
        outs[3 * level + 2][...] = maps_ref[1 - side, rows, cols]
    span = width >> depth
    for side in range(2):
        outs[3 * depth + side][...] = maps_ref[side, :, pl.ds(width - span, span)]


def cut_maps(maps, core, sides):
    depth = len(sides)
    width = maps.shape[1]
    half = width // 2
    spans = [width >> (level + 1) for level in range(depth)]
    if spans[-1] % 128 == 0:
        shapes = []
        for span in spans:
            shapes += [(width, span), (half, span), (half, span)]
        shapes += [(width, spans[-1])] * 2
        outs = pl.pallas_call(
            functools.partial(cut_kernel, depth),
            out_shape=[jax.ShapeDtypeStruct(shape, maps.dtype) for shape in shapes],
            in_specs=[smem_block(), whole_block()],
            out_specs=[whole_block()] * len(shapes),
            compiler_params=pltpu.CompilerParams(vmem_limit_bytes=24 * MIB),
            name="cut_maps",
        )(ids_of(core, *sides), maps)
    else:
        outs = []
        for span, side in zip(spans, sides):
            first = width - 2 * span
            outs.append(lax.dynamic_slice(maps, (side, 0, first), (1, width, span))[0])
            for which in (side, 1 - side):
                outs.append(lax.dynamic_slice(maps, (which, core * half, first), (1, half, span))[0])
        outs += [maps[0, :, width - spans[-1] :], maps[1, :, width - spans[-1] :]]
    return [outs[3 * i : 3 * i + 3] for i in range(depth)], outs[3 * depth :]


def assemble_kernel(count, ids_ref, own_ref, *refs):
    mine, other, out_ref = refs[:count], refs[count : 2 * count], refs[2 * count]
    half, span = mine[0].shape
    for offset in range(count + 1):
        block = jnp.bitwise_xor(ids_ref[1], offset)
        cols = pl.ds(pl.multiple_of(block * span, span), span)
        if offset == 0:
            out_ref[:, cols] = own_ref[...]
            continue
        for ref, core in ((mine[offset - 1], ids_ref[0]), (other[offset - 1], 1 - ids_ref[0])):
            out_ref[pl.ds(pl.multiple_of(core * half, half), half), cols] = ref[...]


def assemble(own, mine, other, core, block):
    width, span = own.shape
    count = len(mine)
    if span % 128 == 0:
        return pl.pallas_call(
            functools.partial(assemble_kernel, count),
            out_shape=jax.ShapeDtypeStruct((width, span * (count + 1)), own.dtype),
            in_specs=[smem_block()] + [whole_block()] * (2 * count + 1),
            out_specs=whole_block(),
            compiler_params=pltpu.CompilerParams(vmem_limit_bytes=16 * MIB),
            name="assemble",
        )(ids_of(core, block), own, *mine, *other)
    out = jnp.zeros((width, span * (count + 1)), own.dtype)
    out = lax.dynamic_update_slice(out, own, (0, block * span))
    for i in range(count):
        col = (block ^ (i + 1)) * span
        out = lax.dynamic_update_slice(out, mine[i], (core * (width // 2), col))
        out = lax.dynamic_update_slice(out, other[i], ((1 - core) * (width // 2), col))
    return out


def cut_grads_kernel(count, ids_ref, low_ref, high_ref, *outs):
    rows, width = low_ref.shape
    span = width // count
    for offset in range(count):
        block = jnp.bitwise_xor(ids_ref[0], offset)
        cols = pl.ds(pl.multiple_of(block * span, span), span)
        outs[offset][:rows] = low_ref[:, cols]
        outs[offset][rows:] = high_ref[:, cols]


def cut_grads(low, high, block, count):
    rows, width = low.shape
    span = width // count
    if span % 128 == 0 and rows % 16 == 0:
        return pl.pallas_call(
            functools.partial(cut_grads_kernel, count),
            out_shape=[jax.ShapeDtypeStruct((2 * rows, span), low.dtype)] * count,
            in_specs=[smem_block(), whole_block(), whole_block()],
            out_specs=[whole_block()] * count,
            name="cut_grads",
        )(ids_of(block), low, high)
    full = join([low, high])
    return [
        lax.dynamic_slice_in_dim(full, (block ^ offset) * span, span, 1) for offset in range(count)
    ]


def upper_grads_kernel(counts, ids_ref, *refs):
    keep_ref, give_ref = refs[-2:]
    quarter = keep_ref.shape[1] // 2
    at, col = 0, 0
    for index, count in enumerate(counts):
        inputs, grads = refs[at : at + count], refs[at + count : at + 2 * count]
        at += 2 * count
        span = grads[0].shape[1]
        half = count // 2
        for turn in range(2):
            pick = range(turn * half, (turn + 1) * half)
            grad = jnp.concatenate([grads[i][...] for i in pick], axis=0)
            side = jnp.bitwise_xor(ids_ref[1 + index], turn)
            for far in range(2):
                for which, out in ((ids_ref[0], keep_ref), (1 - ids_ref[0], give_ref)):
                    lanes = pl.ds(pl.multiple_of((2 * far + which) * quarter, quarter), quarter)
                    rows = jnp.concatenate([inputs[i][:, lanes] for i in pick], axis=0)
                    out[side, far * quarter : (far + 1) * quarter, col : col + span] = inner_t(
                        rows, grad
                    ).astype(out.dtype)
        col += span


def upper_grads(entries, core):
    width = entries[0][1][0].shape[1]
    spans = [entry[2][0].shape[1] for entry in entries]
    shape = (2, width // 2, sum(spans))
    pieces = []
    for _, inputs, grads in entries:
        pieces += list(inputs) + list(grads)
    if all(piece.shape[0] % 16 == 0 and piece.shape[1] % 128 == 0 for piece in pieces):
        return pl.pallas_call(
            functools.partial(upper_grads_kernel, [len(entry[1]) for entry in entries]),
            out_shape=[
                jax.ShapeDtypeStruct(shape, jnp.float32),
                jax.ShapeDtypeStruct(shape, jnp.bfloat16),
            ],
            in_specs=[smem_block()] + [whole_block()] * len(pieces),
            out_specs=[whole_block()] * 2,
            compiler_params=pltpu.CompilerParams(vmem_limit_bytes=24 * MIB),
            name="upper_grads",
        )(ids_of(core, *[entry[0] for entry in entries]), *pieces)
    kept, given = [], []
    for first, inputs, grads in entries:
        half = len(inputs) // 2
        both = []
        for turn in range(2):
            pick = slice(turn * half, (turn + 1) * half)
            both.append(inner_t(join(inputs[pick]), join(grads[pick])))
        pair = jnp.stack([jnp.where(first == 1, both[1 - i], both[i]) for i in range(2)])
        pair = pair.reshape(2, 2, 2, width // 4, -1)
        keep = jnp.where(core == 1, pair[:, :, 1], pair[:, :, 0])
        give = jnp.where(core == 1, pair[:, :, 0], pair[:, :, 1])
        kept.append(keep.reshape(2, width // 2, -1))
        given.append(bf16(give.reshape(2, width // 2, -1)))
    return jnp.concatenate(kept, axis=2), jnp.concatenate(given, axis=2)


def mid_forward(term, near, far, weight):
    product = (1.0 + f32(term)) * (1.0 + f32(near)) * f32(far)
    return up_product(bf16(product * rms_factor(product)), weight)


def up_product(message, weight):
    up = matmul(message, weight)
    keep = up.shape[0] // 2
    return message, up[:keep], bf16(up[keep:])


def up_forward(own_up, other_up, weight):
    joined = (1.0 + own_up) * (1.0 + f32(other_up))
    return up_product(bf16(joined * rms_factor(joined)), weight)


def top_forward(own_up, other_up):
    joined = (1.0 + own_up) * (1.0 + f32(other_up))
    return (bf16(joined * rms_factor(joined)),)


def head_body(count, cotangent, left, right, *pieces):
    root = jnp.concatenate(pieces, axis=0) if len(pieces) > 1 else pieces[0]
    value = matmul(root, left)
    gating = jax.nn.sigmoid(matmul(root, right))
    grad_value = bf16(cotangent * gating)
    grad_gate = bf16(cotangent * value * gating * (1.0 - gating))
    back = matmul_t(grad_value, left) + matmul_t(grad_gate, right)
    rows = root.shape[0] // count
    outs = [back[:rows]] + [bf16(back[i * rows : (i + 1) * rows]) for i in range(1, count)]
    return [root, grad_value, grad_gate] + outs


def level_back(grad_msg, own_up, other_up):
    own_up, other_up = 1.0 + own_up, 1.0 + f32(other_up)
    joined = own_up * other_up
    scaling = rms_factor(joined)
    grad = norm_back(grad_msg, joined * scaling, scaling)
    return bf16(grad * other_up), bf16(grad * own_up)


def top_back(own_up, other_up, own_part, *parts):
    total = own_part
    for part in parts:
        total = total + f32(part)
    return level_back(total, own_up, other_up)


def down_back(own_up, other_up, weight, low, high):
    return level_back(matmul_t(join([low, high]), weight), own_up, other_up)


def mid_back(term, near, far, weight, low, high):
    own, near, far = 1.0 + f32(term), 1.0 + f32(near), f32(far)
    pair = own * near
    product = pair * far
    scale = rms_factor(product)
    grad_msg = matmul_t(join([low, high]), weight)
    grad = norm_back(grad_msg, product * scale, scale)
    grad_pair = grad * far
    return bf16(grad_pair * near), bf16(grad_pair * own), bf16(grad * pair)


def far_back(grad_pair, term, near):
    grad_pair = f32(grad_pair)
    return bf16(grad_pair * (1.0 + f32(near))), bf16(grad_pair * (1.0 + f32(term)))


def pair_product(term, near):
    return (bf16((1.0 + f32(term)) * (1.0 + f32(near))),)


def swap_blocks(array, size, axis):
    count = array.shape[axis] // size
    parts = [lax.slice_in_dim(array, i * size, (i + 1) * size, axis=axis) for i in range(count)]
    return jnp.concatenate([parts[i ^ 1] for i in range(count)], axis=axis)


def on_device(regions, leaf_map, leaf_bond_weight, mid_weight, upper_weight, head_cotangent):
    rows = regions.shape[0]
    width = upper_weight.shape[1]
    sub_count = lax.axis_size("sub")
    depth = sub_count.bit_length() - 1
    sub_index = lax.axis_index("sub")
    rep_index = lax.axis_index("rep")
    core = rep_index % 2
    far = rep_index // 2
    bits = [(sub_index >> level) % 2 for level in range(depth)]
    flip = sum(bits[level] * (rows >> (level + 1)) for level in range(depth))
    leaf_w = leaf_bond_weight[0]
    mid_w = mid_weight[0, 0]

    sent = place(regions, leaf_map, ids_of(rep_index, flip))
    far_both = partner(sent[3], "rep", 3)
    far_one = partner(sent[2], "rep", 2)
    near = partner(sent[1], "rep", 1)
    placed = [sent[0], near, far_one, far_both]

    maps = lax.optimization_barrier(jnp.transpose(upper_weight[0], (1, 0, 2)))
    blocks, (head_left, head_right) = cut_maps(maps, core, bits)
    mine = [
        [
            partner(blocks[level][1 if offset < 1 << level else 2], "sub", offset)
            for offset in range(1, 2 << level)
        ]
        for level in range(depth)
    ]
    other = [[partner(piece, "rep", 1) for piece in pieces] for pieces in mine]
    weights = [
        assemble(blocks[level][0], mine[level], other[level], core, sub_index % (2 << level))
        for level in range(depth)
    ]
    cotangent = head_cotangent
    for level in range(depth):
        swapped = swap_blocks(cotangent, rows >> (level + 1), 0)
        cotangent = jnp.where(bits[level] == 1, swapped, cotangent)

    msg0, msg1, term0, term1 = leaf_forward(placed[:2], leaf_w, mid_w)
    near0 = partner(term1, "rep", 1)
    msg2, msg3, term2, term3 = leaf_forward(placed[2:], leaf_w, mid_w)
    near2 = partner(term3, "rep", 1)
    far_pair = partner(fused(pair_product, "pair_product", term2, near2)[0], "rep", 2)

    messages, own_ups, other_ups = [], [], []
    for level in range(depth):
        if level == 0:
            step = fused(mid_forward, "mid_forward", term0, near0, far_pair, weights[0])
        else:
            step = fused(up_forward, "up_forward", own_ups[-1], other_ups[-1], weights[level])
        messages.append(step[0])
        own_ups.append(step[1])
        other_ups.append(partner(step[2], "sub", 1 << level))
    (root,) = fused(top_forward, "top_forward", own_ups[-1], other_ups[-1])

    order = [reverse_bits(i, depth) for i in range(sub_count)]
    roots = [root] + [partner(root, "sub", offset) for offset in range(1, sub_count)]
    pieces = [roots[offset] for offset in order]
    if root.shape[0] % 16:
        pieces = [join(pieces)]
    root, grad_value, grad_gate, *parts = fused(
        functools.partial(head_body, sub_count),
        "head",
        cotangent,
        head_left,
        head_right,
        *pieces,
    )
    parts = [parts[0]] + [
        partner(parts[block], "sub", order[block]) for block in range(1, sub_count)
    ]

    lows, highs = [None] * depth, [None] * depth
    for level in reversed(range(depth)):
        if level == depth - 1:
            low, high = fused(top_back, "top_back", own_ups[level], other_ups[level], *parts)
        else:
            low, high = fused(
                down_back,
                "down_back",
                own_ups[level],
                other_ups[level],
                weights[level + 1],
                lows[level + 1],
                highs[level + 1],
            )
        lows[level] = low
        highs[level] = partner(high, "sub", 1 << level)

    back0, back1, pair_back = fused(
        mid_back, "mid_back", term0, near0, far_pair, weights[0], lows[0], highs[0]
    )
    pair_back = partner(pair_back, "rep", 2)
    back1 = partner(back1, "rep", 1)
    back2, back3 = fused(far_back, "far_back", pair_back, term2, near2)
    back3 = partner(back3, "rep", 1)
    leaf_grad, mid_grad = leaf_backward(
        placed, [msg0, msg1, msg2, msg3], [back0, back1, back2, back3], leaf_w, mid_w
    )

    entries = []
    for level in range(depth):
        count = 2 << level
        inputs = [messages[level]] + [
            partner(messages[level], "sub", offset) for offset in range(1, count)
        ]
        cut = cut_grads(lows[level], highs[level], sub_index % count, count)
        grads = [cut[0]] + [partner(cut[offset], "sub", offset) for offset in range(1, count)]
        entries.append((bits[level], inputs, grads))
    entries.append((0, [root, root], [grad_value, grad_gate]))

    def rep_sum(entries):
        keep, give = upper_grads(entries, core)
        got = partner(give, "rep", 1)
        quarter = width // 4

        def part(index):
            return lax.dynamic_slice_in_dim(keep, index * quarter, quarter, 1) + f32(
                lax.dynamic_slice_in_dim(got, index * quarter, quarter, 1)
            )

        return bf16(part(far) + f32(partner(bf16(part(1 - far)), "rep", 2)))

    upper = rep_sum(entries[1:])
    upper = jnp.concatenate([rep_sum(entries[:1]), upper], axis=2)
    upper = jnp.transpose(upper, (1, 0, 2))
    return leaf_grad[None], mid_grad[None, None], upper[None]


def solution(mesh):
    placed = (
        P("rep", "sub", None),
        P("sub"),
        P(("sub", "rep"), None, None, None),
        P("sub", "rep", None, None),
        P("sub", None, None, None),
        P("rep", "sub"),
    )
    return jax.shard_map(
        on_device,
        mesh=mesh,
        in_specs=placed,
        out_specs=(
            P(("sub", "rep"), None, None, None),
            P("sub", "rep", None, None),
            P("sub", "rep", None, None),
        ),
        check_vma=False,
    )
```

```python
import functools

import jax
import jax.numpy as jnp
from jax import lax
from jax.experimental import pallas as pl
from jax.experimental.pallas import tpu as pltpu
from jax.sharding import PartitionSpec as P

EPSILON = 1e-06
CHILDREN = 4
MIB = 1024 * 1024


def partner(value, axis, offset):
    return lax.ppermute(value, axis, [(i, i ^ offset) for i in range(lax.axis_size(axis))])


def rms_factor(values):
    return lax.rsqrt(jnp.mean(values * values, axis=-1, keepdims=True) + EPSILON)


def norm_back(gradient, normed, factor):
    return factor * (gradient - normed * jnp.mean(gradient * normed, axis=-1, keepdims=True))


def matmul(left_arr, right_arr):
    return jnp.dot(left_arr, right_arr, preferred_element_type=jnp.float32)


def matmul_t(left_arr, right_arr):
    return lax.dot_general(
        left_arr, right_arr, (((1,), (1,)), ((), ())), preferred_element_type=jnp.float32
    )


def inner_t(left_arr, right_arr):
    return lax.dot_general(
        left_arr, right_arr, (((0,), (0,)), ((), ())), preferred_element_type=jnp.float32
    )


def bf16(value):
    return value.astype(jnp.bfloat16)


def f32(value):
    return value.astype(jnp.float32)


def whole_block():
    return pl.BlockSpec(memory_space=pltpu.VMEM)


def place_kernel(slots, ids_ref, map_ref, regions_ref, *rest):
    outs, wide = rest[:CHILDREN], rest[CHILDREN]
    rows = regions_ref.shape[0] // slots
    parts = wide.shape[0]
    for part in range(parts):
        wide[part] = regions_ref[:, part * 128 : (part + 1) * 128].astype(jnp.float32)
    row = lax.broadcasted_iota(jnp.int32, (rows, rows), 0)
    col = lax.broadcasted_iota(jnp.int32, (rows, rows), 1)
    select = (jnp.bitwise_xor(row, ids_ref[1]) == col).astype(jnp.bfloat16)
    for offset in range(CHILDREN):
        node = jnp.bitwise_xor(ids_ref[0], offset)
        for child in range(CHILDREN):
            region = map_ref[node * CHILDREN + child]
            for part in range(parts):
                values = wide[part, pl.ds(region, rows, stride=slots), :].astype(jnp.bfloat16)
                outs[offset][child, :, part * 128 : (part + 1) * 128] = matmul(
                    select, values
                ).astype(jnp.bfloat16)


def place(regions, leaf_map, ids):
    rows, slots, feats = regions.shape
    flat = regions.reshape(rows * slots, feats)
    smem = pl.BlockSpec(memory_space=pltpu.SMEM)
    return pl.pallas_call(
        functools.partial(place_kernel, slots),
        out_shape=[jax.ShapeDtypeStruct((CHILDREN, rows, feats), jnp.bfloat16)] * CHILDREN,
        in_specs=[smem, smem, whole_block()],
        out_specs=[whole_block()] * CHILDREN,
        scratch_shapes=[pltpu.VMEM((feats // 128, rows * slots, 128), jnp.float32)],
        compiler_params=pltpu.CompilerParams(vmem_limit_bytes=6 * MIB),
        name="place",
    )(ids, leaf_map, flat)


def leaf_forward_kernel(count, *refs):
    placed, leaf_w, mid_w = refs[:count], refs[count], refs[count + 1]
    msgs, terms = refs[count + 2 : 2 * count + 2], refs[2 * count + 2 :]
    rows = placed[0].shape[1]
    product = None
    for child in range(CHILDREN):
        values = jnp.concatenate([ref[child] for ref in placed], axis=0)
        factor = 1.0 + matmul(values, leaf_w[child])
        product = factor if product is None else product * factor
    message = bf16(product * rms_factor(product))
    out = bf16(matmul(message, mid_w[...]))
    for i in range(count):
        msgs[i][...] = message[i * rows : (i + 1) * rows]
        terms[i][...] = out[i * rows : (i + 1) * rows]


def leaf_forward(placed, leaf_w, mid_w):
    count = len(placed)
    rows = placed[0].shape[1]
    width = mid_w.shape[0]
    return pl.pallas_call(
        functools.partial(leaf_forward_kernel, count),
        out_shape=[jax.ShapeDtypeStruct((rows, width), jnp.bfloat16)] * (2 * count),
        in_specs=[whole_block()] * (count + 2),
        out_specs=[whole_block()] * (2 * count),
        compiler_params=pltpu.CompilerParams(vmem_limit_bytes=14 * MIB),
        name="leaf_forward",
    )(*placed, leaf_w, mid_w)


def leaf_cotangents(placed, grads, leaf_w, mid_w):
    factors = [
        1.0 + matmul(jnp.concatenate([ref[child] for ref in placed], axis=0), leaf_w[child])
        for child in range(CHILDREN)
    ]
    low = factors[0] * factors[1]
    high = factors[2] * factors[3]
    product = low * high
    scale = rms_factor(product)
    back = matmul_t(jnp.concatenate([ref[...] for ref in grads], axis=0), mid_w[...])
    node = norm_back(back, product * scale, scale)
    high, low = node * high, node * low
    return [
        bf16(high * factors[1]),
        bf16(high * factors[0]),
        bf16(low * factors[3]),
        bf16(low * factors[2]),
    ]


def leaf_first_kernel(*refs):
    placed, grads, leaf_w, mid_w, out = refs[0:2], refs[2:4], refs[4], refs[5], refs[6]
    for child, value in enumerate(leaf_cotangents(placed, grads, leaf_w, mid_w)):
        out[child] = value


def leaf_first(placed, grads, leaf_w, mid_w):
    rows = placed[0].shape[1]
    return pl.pallas_call(
        leaf_first_kernel,
        out_shape=jax.ShapeDtypeStruct((CHILDREN, 2 * rows, mid_w.shape[0]), jnp.bfloat16),
        in_specs=[whole_block()] * 6,
        out_specs=whole_block(),
        compiler_params=pltpu.CompilerParams(vmem_limit_bytes=18 * MIB),
        name="leaf_first",
    )(*placed, *grads, leaf_w, mid_w)


def leaf_backward_kernel(*refs):
    placed, msgs, grads = refs[0:4], refs[4:8], refs[8:12]
    leaf_w, mid_w, first, leaf_out, mid_out = refs[12:17]
    all_grads = jnp.concatenate([ref[...] for ref in grads], axis=0)
    all_msgs = jnp.concatenate([ref[...] for ref in msgs], axis=0)
    mid_out[...] = bf16(inner_t(all_msgs, all_grads))
    second = leaf_cotangents(placed[2:], grads[2:], leaf_w, mid_w)
    for child in range(CHILDREN):
        values = jnp.concatenate([ref[child] for ref in placed], axis=0)
        cot = jnp.concatenate([first[child], second[child]], axis=0)
        leaf_out[child] = bf16(inner_t(values, cot))


def leaf_backward(placed, msgs, grads, leaf_w, mid_w, first):
    return pl.pallas_call(
        leaf_backward_kernel,
        out_shape=[
            jax.ShapeDtypeStruct(leaf_w.shape, jnp.bfloat16),
            jax.ShapeDtypeStruct(mid_w.shape, jnp.bfloat16),
        ],
        in_specs=[whole_block()] * 15,
        out_specs=[whole_block()] * 2,
        compiler_params=pltpu.CompilerParams(vmem_limit_bytes=30 * MIB),
        name="leaf_backward",
    )(*placed, *msgs, *grads, leaf_w, mid_w, first)


def fused(body, name, *args, limit=8):
    if any(arg.shape[-2] % 16 or arg.shape[-1] % 128 for arg in args):
        return body(*args)
    shapes = jax.eval_shape(body, *args)

    def kernel(*refs):
        results = body(*[ref[...] for ref in refs[: len(args)]])
        for ref, result in zip(refs[len(args) :], results):
            ref[...] = result

    return pl.pallas_call(
        kernel,
        out_shape=shapes,
        in_specs=[whole_block()] * len(args),
        out_specs=[whole_block()] * len(shapes),
        compiler_params=pltpu.CompilerParams(vmem_limit_bytes=limit * MIB),
        name=name,
    )(*args)


def ids_of(*values):
    return jnp.stack(values).astype(jnp.int32)


def smem_block():
    return pl.BlockSpec(memory_space=pltpu.SMEM)


def reverse_bits(value, count):
    out = 0
    for i in range(count):
        out = out * 2 + (value >> i) % 2
    return out


def join(pieces):
    if pieces[0].shape[0] % 16 == 0:
        return jnp.concatenate(pieces, axis=0)
    wide = lax.optimization_barrier(tuple(f32(piece) for piece in pieces))
    return bf16(lax.optimization_barrier(jnp.concatenate(wide, axis=0)))


def pack(pieces):
    arrays = []
    for array, _, _ in pieces:
        if not any(array is known for known in arrays):
            arrays.append(array)
    spots = [next(i for i, known in enumerate(arrays) if known is piece[0]) for piece in pieces]

    def body(*values):
        parts = [values[i][:, at : at + span] for i, (_, at, span) in zip(spots, pieces)]
        return (jnp.concatenate(parts, axis=1),)

    if any(piece[2] % 128 for piece in pieces):
        return body(*arrays)[0]
    return fused(body, "pack", *arrays, limit=6)[0]


def cut_kernel(depth, ids_ref, maps_ref, *refs):
    outs, split = refs[:-1], refs[-1]
    split[...] = jnp.swapaxes(maps_ref[...], 0, 1)
    width = maps_ref.shape[0]
    half = width // 2
    rows = pl.ds(pl.multiple_of(ids_ref[0] * half, half), half)
    for level in range(depth):
        span = width >> (level + 1)
        cols = pl.ds(width - 2 * span, span)
        side = ids_ref[1 + level]
        outs[3 * level][...] = split[side, :, cols]
        outs[3 * level + 1][...] = split[side, rows, cols]
        outs[3 * level + 2][...] = split[1 - side, rows, cols]
    span = width >> depth
    for side in range(2):
        outs[3 * depth + side][...] = split[side, :, width - span :]


def cut_maps(maps, core, sides):
    depth = len(sides)
    width = maps.shape[0]
    half = width // 2
    spans = [width >> (level + 1) for level in range(depth)]
    if spans[-1] % 128 == 0:
        shapes = []
        for span in spans:
            shapes += [(width, span), (half, span), (half, span)]
        shapes += [(width, spans[-1])] * 2
        outs = pl.pallas_call(
            functools.partial(cut_kernel, depth),
            out_shape=[jax.ShapeDtypeStruct(shape, maps.dtype) for shape in shapes],
            in_specs=[smem_block(), whole_block()],
            out_specs=[whole_block()] * len(shapes),
            scratch_shapes=[pltpu.VMEM((2, width, width), maps.dtype)],
            compiler_params=pltpu.CompilerParams(vmem_limit_bytes=18 * MIB),
            name="cut_maps",
        )(ids_of(core, *sides), maps)
    else:
        maps = jnp.transpose(maps, (1, 0, 2))
        outs = []
        for span, side in zip(spans, sides):
            first = width - 2 * span
            outs.append(lax.dynamic_slice(maps, (side, 0, first), (1, width, span))[0])
            for which in (side, 1 - side):
                outs.append(lax.dynamic_slice(maps, (which, core * half, first), (1, half, span))[0])
        outs += [maps[0, :, width - spans[-1] :], maps[1, :, width - spans[-1] :]]
    return [outs[3 * i : 3 * i + 3] for i in range(depth)], outs[3 * depth :]


def assemble_kernel(spots, count, ids_ref, own_ref, *refs):
    out_ref = refs[-1]
    width, span = own_ref.shape
    half = width // 2
    block = ids_ref[1]
    out_ref[:, pl.ds(pl.multiple_of(block * span, span), span)] = own_ref[...]
    for offset, index, at in spots:
        col = jnp.bitwise_xor(block, offset) * span
        for ref, core in ((refs[index], ids_ref[0]), (refs[count + index], 1 - ids_ref[0])):
            out_ref[
                pl.ds(pl.multiple_of(core * half, half), half),
                pl.ds(pl.multiple_of(col, span), span),
            ] = ref[:, at : at + span]


def assemble(own, pieces, core, block):
    width, span = own.shape
    count = len(pieces) + 1
    if span % 128 == 0:
        mine, other, spots = [], [], []
        for offset, (near_half, far_half, at) in pieces.items():
            known = [i for i, array in enumerate(mine) if array is near_half]
            if not known:
                mine.append(near_half)
                other.append(far_half)
                known = [len(mine) - 1]
            spots.append((offset, known[0], at))
        return pl.pallas_call(
            functools.partial(assemble_kernel, spots, len(mine)),
            out_shape=jax.ShapeDtypeStruct((width, span * count), own.dtype),
            in_specs=[smem_block()] + [whole_block()] * (2 * len(mine) + 1),
            out_specs=whole_block(),
            compiler_params=pltpu.CompilerParams(vmem_limit_bytes=8 * MIB),
            name="assemble",
        )(ids_of(core, block), own, *mine, *other)
    out = jnp.zeros((width, span * count), own.dtype)
    out = lax.dynamic_update_slice(out, own, (0, block * span))
    for offset, (near_half, far_half, at) in pieces.items():
        col = (block ^ offset) * span
        for array, which in ((near_half, core), (far_half, 1 - core)):
            part = array[:, at : at + span]
            out = lax.dynamic_update_slice(out, part, (which * (width // 2), col))
    return out


def after(value, *others):
    return lax.optimization_barrier((value, *others))[0]


class MapGather:
    def __init__(self, blocks, core, sub_index):
        self.blocks, self.core, self.sub_index = blocks, core, sub_index
        self.depth = len(blocks)
        self.spans = [block[0].shape[1] for block in blocks]
        self.held = [{0: (block[1], 0)} for block in blocks]
        self.first = partner(blocks[0][2], "sub", 1)
        self.early = [self.send([(level, 0) for level in range(1, self.depth)], 0)]

    def send(self, picks, stage, extra=None, gate=None):
        pieces = [(*self.held[level][offset], self.spans[level]) for level, offset in picks]
        picks = list(picks)
        if extra is not None:
            pieces.append((self.blocks[extra][2], 0, self.spans[extra]))
            picks.append((extra, 0))
        if gate is not None:
            pieces[-1] = (after(pieces[-1][0], gate), *pieces[-1][1:])
        value = pieces[0][0] if len(pieces) == 1 else pack(pieces)
        got = partner(value, "sub", 1 << stage)
        at = 0
        for level, offset in picks:
            self.held[level][offset ^ (1 << stage)] = (got, at)
            at += self.spans[level]
        return got

    def stage(self, stage, gate=None):
        picks = [
            (level, offset)
            for level in range(stage + 1, self.depth)
            for offset in self.held[level]
            if offset % (2 << stage) == 0
        ]
        self.early.append(self.send(picks, stage, stage, gate))

    def last(self, gate):
        picks = [
            (level, offset)
            for level in range(1, self.depth)
            for offset in self.held[level]
            if offset % 2 == 0 and offset > 0
        ]
        self.late = self.send(picks, 0, None, gate)

    def weight(self, level, exchanged):
        pieces = {}
        if level == 0:
            pieces[1] = (self.first, exchanged[0], 0)
        else:
            for offset, (array, at) in self.held[level].items():
                if offset == 0:
                    continue
                if array is self.late:
                    pieces[offset] = (array, exchanged[2], at)
                    continue
                pieces[offset] = (self.packed_early, exchanged[1], at + self.early_at(array))
        return assemble(
            self.blocks[level][0], pieces, self.core, self.sub_index % (2 << level)
        )

    def early_at(self, array):
        at = 0
        for known in self.early:
            if known is array:
                return at
            at += known.shape[1]

    def pack_early(self):
        self.packed_early = pack([(array, 0, array.shape[1]) for array in self.early])
        return self.packed_early


class View:
    def __init__(self, array, rows=None, cols=None):
        self.array = array
        self.rows = (0, array.shape[0]) if rows is None else rows
        self.cols = (0, array.shape[1]) if cols is None else cols
        self.shape = (self.rows[1] - self.rows[0], self.cols[1] - self.cols[0])

    def value(self):
        return self.array[slice(*self.rows), slice(*self.cols)]

    def part(self, first, last):
        return View(self.array, (self.rows[0] + first, self.rows[0] + last), self.cols)

    def aligned(self):
        edges = (*self.rows, *self.cols)
        return all(edge % unit == 0 for edge, unit in zip(edges, (16, 16, 128, 128)))


def spots_of(views):
    arrays, spots = [], []
    for view in views:
        known = [i for i, array in enumerate(arrays) if array is view.array]
        if not known:
            arrays.append(view.array)
            known = [len(arrays) - 1]
        spots.append((known[0], view.rows, view.cols))
    return arrays, spots


def stack_rows(views):
    if len(views) == 1 and views[0].shape == views[0].array.shape:
        return views[0].array
    if not all(view.aligned() for view in views):
        return join_all([view.value() for view in views])
    arrays, spots = spots_of(views)

    def body(*values):
        parts = [values[i][slice(*rows), slice(*cols)] for i, rows, cols in spots]
        return (jnp.concatenate(parts, axis=0),)

    return fused(body, "stack_rows", *arrays, limit=6)[0]


def join_all(pieces):
    if all(piece.shape[0] % 16 == 0 for piece in pieces):
        return jnp.concatenate(pieces, axis=0)
    wide = lax.optimization_barrier(tuple(f32(piece) for piece in pieces))
    return bf16(lax.optimization_barrier(jnp.concatenate(wide, axis=0)))


def halve_kernel(groups, count, ids_ref, *refs):
    outs = refs[count:]
    send_ref = outs[-1]
    col = 0
    for spots, keep_ref in zip(groups, outs):
        half = keep_ref.shape[1]
        at = 0
        for index, (first, last), (left, _) in spots:
            where = slice(at, at + last - first)
            for bit, out, here in ((ids_ref[0], keep_ref, 0), (1 - ids_ref[0], send_ref, col)):
                lanes = pl.ds(pl.multiple_of(left + bit * half, 128), half)
                out[where, here : here + half] = refs[index][first:last, lanes]
            at += last - first
        col += half


def halve(groups, bit):
    views = [view for group in groups for view in group]
    if all(view.aligned() and view.shape[1] % 256 == 0 for view in views):
        arrays, spots = spots_of(views)
        by_group, out_shapes = [], []
        for group in groups:
            by_group.append([spots.pop(0) for _ in group])
            out_shapes.append((sum(view.shape[0] for view in group), group[0].shape[1] // 2))
        out_shapes.append((out_shapes[0][0], sum(shape[1] for shape in out_shapes)))
        outs = pl.pallas_call(
            functools.partial(halve_kernel, by_group, len(arrays)),
            out_shape=[jax.ShapeDtypeStruct(shape, jnp.bfloat16) for shape in out_shapes],
            in_specs=[smem_block()] + [whole_block()] * len(arrays),
            out_specs=[whole_block()] * len(out_shapes),
            compiler_params=pltpu.CompilerParams(vmem_limit_bytes=6 * MIB),
            name="halve",
        )(ids_of(bit), *arrays)
        return outs[:-1], outs[-1]
    keeps, sends = [], []
    for group in groups:
        full = join_all([view.value() for view in group])
        half = full.shape[1] // 2
        keeps.append(lax.dynamic_slice_in_dim(full, bit * half, half, 1))
        sends.append(lax.dynamic_slice_in_dim(full, (1 - bit) * half, half, 1))
    return keeps, jnp.concatenate(sends, axis=1)


def upper_grads_kernel(entries, count, ids_ref, *refs):
    own_ref, far_ref, give_ref = refs[count:]
    quarter = own_ref.shape[1]
    col = 0
    for index, turns in enumerate(entries):
        for turn, (inputs, grads) in enumerate(turns):
            grad = jnp.concatenate(
                [refs[i][slice(*rows), slice(*cols)] for i, rows, cols in grads], axis=0
            )
            span = grad.shape[1]
            side = jnp.bitwise_xor(ids_ref[2 + index], turn)
            for far in range(2):
                for core in range(2):
                    which = jnp.bitwise_xor(ids_ref[1], far) * 2 + jnp.bitwise_xor(ids_ref[0], core)
                    lanes = pl.ds(pl.multiple_of(which * quarter, quarter), quarter)
                    rows = jnp.concatenate(
                        [refs[i][slice(*edges), lanes] for i, edges, _ in inputs], axis=0
                    )
                    value = inner_t(rows, grad)
                    if core == 1:
                        give_ref[side, far, :, col : col + span] = bf16(value)
                    elif far == 1:
                        far_ref[side, :, col : col + span] = value
                    else:
                        own_ref[side, :, col : col + span] = value
        col += span


def upper_grads(entries, core, far):
    width = entries[0][1][0][0].shape[1]
    spans = [entry[1][1][0].shape[1] for entry in entries]
    quarter = width // 4
    views = []
    for _, *turns in entries:
        for inputs, grads in turns:
            views += inputs + grads
    if all(view.aligned() for view in views):
        total = sum(spans)
        arrays, spots = spots_of(views)
        by_entry = []
        for _, *turns in entries:
            by_entry.append(
                [
                    ([spots.pop(0) for _ in inputs], [spots.pop(0) for _ in grads])
                    for inputs, grads in turns
                ]
            )
        return pl.pallas_call(
            functools.partial(upper_grads_kernel, by_entry, len(arrays)),
            out_shape=[
                jax.ShapeDtypeStruct((2, quarter, total), jnp.float32),
                jax.ShapeDtypeStruct((2, quarter, total), jnp.float32),
                jax.ShapeDtypeStruct((2, 2, quarter, total), jnp.bfloat16),
            ],
            in_specs=[smem_block()] + [whole_block()] * len(arrays),
            out_specs=[whole_block()] * 3,
            compiler_params=pltpu.CompilerParams(vmem_limit_bytes=12 * MIB),
            name="upper_grads",
        )(ids_of(core, far, *[entry[0] for entry in entries]), *arrays)
    owns, fars, gives = [], [], []
    for first, *turns in entries:
        both = [
            inner_t(join_all([v.value() for v in inputs]), join_all([v.value() for v in grads]))
            for inputs, grads in turns
        ]
        pair = jnp.stack([jnp.where(first == 1, both[1 - i], both[i]) for i in range(2)])
        pair = pair.reshape(2, 2, 2, quarter, -1)
        pair = jnp.where(far == 1, pair[:, ::-1], pair)
        pair = jnp.where(core == 1, pair[:, :, ::-1], pair)
        owns.append(pair[:, 0, 0])
        fars.append(pair[:, 1, 0])
        gives.append(bf16(pair[:, :, 1]))
    return [jnp.concatenate(parts, axis=-1) for parts in (owns, fars, gives)]


def far_sum(far_part, got):
    return (bf16(far_part + f32(got[:, 1])),)


def last_sum(*args):
    parts = []
    for own, got, last in (args[:3], args[3:]):
        parts.append(bf16(own + f32(got[:, 0]) + f32(last)))
    return (jnp.swapaxes(jnp.concatenate(parts, axis=2), 0, 1),)


def mid_forward(term, near, far, weight):
    product = (1.0 + f32(term)) * (1.0 + f32(near)) * f32(far)
    return up_product(bf16(product * rms_factor(product)), weight)


def up_product(message, weight):
    up = matmul(message, weight)
    keep = up.shape[0] // 2
    return message, up[:keep], bf16(up[keep:])


def up_forward(own_up, other_up, weight):
    joined = (1.0 + own_up) * (1.0 + f32(other_up))
    return up_product(bf16(joined * rms_factor(joined)), weight)


def top_forward(own_up, other_up):
    joined = (1.0 + own_up) * (1.0 + f32(other_up))
    return (bf16(joined * rms_factor(joined)),)


def head_body(cotangent, left, right, low, high):
    root = join([low, high])
    value = matmul(root, left)
    gating = jax.nn.sigmoid(matmul(root, right))
    grad_value = bf16(cotangent * gating)
    grad_gate = bf16(cotangent * value * gating * (1.0 - gating))
    back = matmul_t(grad_value, left) + matmul_t(grad_gate, right)
    half = root.shape[0] // 2
    return root, grad_value, grad_gate, back[:half], bf16(back[half:])


def joined(low, high):
    return (join([low, high]),)


def partial_sum(own, got):
    total = own + f32(got)
    half = total.shape[0] // 2
    return total[:half], bf16(total[half:])


def level_back(grad_msg, own_up, other_up):
    own_up, other_up = 1.0 + own_up, 1.0 + f32(other_up)
    joined = own_up * other_up
    scaling = rms_factor(joined)
    grad = norm_back(grad_msg, joined * scaling, scaling)
    return bf16(grad * other_up), bf16(grad * own_up)


def top_back(own_up, other_up, own_part, got):
    return level_back(own_part + f32(got), own_up, other_up)


def down_back(own_up, other_up, weight, low, high):
    return level_back(matmul_t(join([low, high]), weight), own_up, other_up)


def mid_back(term, near, far, weight, low, high):
    own, near, far = 1.0 + f32(term), 1.0 + f32(near), f32(far)
    pair = own * near
    product = pair * far
    scale = rms_factor(product)
    grad_msg = matmul_t(join([low, high]), weight)
    grad = norm_back(grad_msg, product * scale, scale)
    grad_pair = grad * far
    return bf16(grad_pair * near), bf16(grad_pair * own), bf16(grad * pair)


def far_back(grad_pair, term, near):
    grad_pair = f32(grad_pair)
    return bf16(grad_pair * (1.0 + f32(near))), bf16(grad_pair * (1.0 + f32(term)))


def pair_product(term, near):
    return (bf16((1.0 + f32(term)) * (1.0 + f32(near))),)


def swap_blocks(array, size, axis):
    count = array.shape[axis] // size
    parts = [lax.slice_in_dim(array, i * size, (i + 1) * size, axis=axis) for i in range(count)]
    return jnp.concatenate([parts[i ^ 1] for i in range(count)], axis=axis)


def on_device(regions, leaf_map, leaf_bond_weight, mid_weight, upper_weight, head_cotangent):
    rows = regions.shape[0]
    width = upper_weight.shape[1]
    sub_count = lax.axis_size("sub")
    depth = sub_count.bit_length() - 1
    sub_index = lax.axis_index("sub")
    rep_index = lax.axis_index("rep")
    core = rep_index % 2
    far = rep_index // 2
    bits = [(sub_index >> level) % 2 for level in range(depth)]
    flip = sum(bits[level] * (rows >> (level + 1)) for level in range(depth))
    leaf_w = leaf_bond_weight[0]
    mid_w = mid_weight[0, 0]

    blocks, (head_left, head_right) = cut_maps(upper_weight[0], core, bits)
    gather = MapGather(blocks, core, sub_index)
    gather.stage(depth - 1)

    sent = place(after(regions, head_right), leaf_map, ids_of(rep_index, flip))
    near = partner(sent[1], "rep", 1)
    far_both = partner(sent[3], "rep", 3)
    far_one = partner(sent[2], "rep", 2)
    placed = [sent[0], near, far_one, far_both]
    msg0, msg1, term0, term1 = leaf_forward(placed[:2], leaf_w, mid_w)
    near0 = partner(term1, "rep", 1)
    for stage in reversed(range(1, depth - 1)):
        gather.stage(stage, sent[3])
    far_placed = [after(placed[2], term1), placed[3]]
    msg2, msg3, term2, term3 = leaf_forward(far_placed, leaf_w, mid_w)
    near2 = partner(term3, "rep", 1)
    (pair,) = fused(pair_product, "pair_product", term2, near2)
    far_pair = partner(pair, "rep", 2)
    cotangent = after(head_cotangent, pair)
    for level in range(depth):
        swapped = swap_blocks(cotangent, rows >> (level + 1), 0)
        cotangent = jnp.where(bits[level] == 1, swapped, cotangent)
    gather.last(pair)
    exchanged = [partner(after(gather.first, pair), "rep", 1)]
    exchanged.append(partner(after(gather.pack_early(), pair), "rep", 1))
    exchanged.append(partner(gather.late, "rep", 1))
    weights = [gather.weight(level, exchanged) for level in range(depth)]

    messages, own_ups, other_ups = [], [], []
    for level in range(depth):
        if level == 0:
            step = fused(mid_forward, "mid_forward", term0, near0, far_pair, weights[0])
        else:
            step = fused(up_forward, "up_forward", own_ups[-1], other_ups[-1], weights[level])
        messages.append(step[0])
        own_ups.append(step[1])
        other_ups.append(partner(step[2], "sub", 1 << level))
    (root,) = fused(top_forward, "top_forward", own_ups[-1], other_ups[-1])

    for level in reversed(range(1, depth)):
        (root,) = fused(joined, "joined", root, partner(root, "sub", 1 << level))
    root_high = partner(root, "sub", 1)
    root, grad_value, grad_gate, grad_msg, give = fused(
        head_body, "head", cotangent, head_left, head_right, root, root_high
    )
    gates = [give]
    for level in range(depth - 1):
        got = partner(give, "sub", 1 << level)
        grad_msg, give = fused(partial_sum, "partial_sum", grad_msg, got)
        gates.append(give)
    last_part = partner(give, "sub", 1 << (depth - 1))

    turns = [[[View(message)], []] for message in messages]
    for stage in reversed(range(depth)):
        levels = range(stage, depth)
        views = []
        for level in levels:
            views += turns[level][0] + (turns[level][1] if level > stage else [])
        views[0] = View(
            after(views[0].array, gates[depth - 1 - stage]), views[0].rows, views[0].cols
        )
        got = partner(stack_rows(views), "sub", 1 << stage)
        at = 0
        for level in levels:
            count = sum(view.shape[0] for view in turns[level][0])
            turns[level][0 if level > stage else 1].append(View(got, (at, at + count)))
            at += count
            if level > stage:
                turns[level][1].append(View(got, (at, at + count)))
                at += count

    lows, highs = [None] * depth, [None] * depth
    columns = [None] * depth

    def spread(stage, levels, gate):
        groups = []
        for level in levels:
            if columns[level] is None:
                groups.append([View(lows[level]), View(highs[level])])
            else:
                groups.append(list(columns[level]))
        first = groups[0][0]
        groups[0][0] = View(after(first.array, gate), first.rows, first.cols)
        keeps, send = halve(groups, bits[stage])
        got = partner(send, "sub", 1 << stage)
        at = 0
        for level, keep in zip(levels, keeps):
            span = keep.shape[1]
            columns[level] = [View(keep), View(got, None, (at, at + span))]
            at += span

    def columns_of(level, turn):
        if level == 0:
            return [columns[0][turn]]
        count = rows >> level
        return [
            view.part(i * count, (i + 1) * count)
            for view in columns[level]
            for i in range(turn, view.shape[0] // count, 2)
        ]

    for level in reversed(range(depth)):
        if level == depth - 1:
            low, high = fused(
                top_back, "top_back", own_ups[level], other_ups[level], grad_msg, last_part
            )
        else:
            low, high = fused(
                down_back,
                "down_back",
                own_ups[level],
                other_ups[level],
                weights[level + 1],
                lows[level + 1],
                highs[level + 1],
            )
        lows[level] = low
        highs[level] = partner(high, "sub", 1 << level)
        if level < depth - 1:
            spread(level + 1, list(range(level + 1, depth)), low)

    back0, back1, pair_back = fused(
        mid_back, "mid_back", term0, near0, far_pair, weights[0], lows[0], highs[0]
    )
    pair_back = partner(pair_back, "rep", 2)
    back1 = partner(back1, "rep", 1)
    first = leaf_first(placed[:2], [back0, back1], leaf_w, mid_w)
    back2, back3 = fused(far_back, "far_back", after(pair_back, first), term2, near2)
    back3 = partner(back3, "rep", 1)
    spread(0, list(range(1, depth)), back0)
    spread(0, [0], back0)

    def entry(level):
        return (bits[level], *[(turns[level][i], columns_of(level, i)) for i in range(2)])

    groups = [
        [entry(0)],
        [entry(level) for level in range(1, depth)]
        + [(0, ([View(root)], [View(grad_value)]), ([View(root)], [View(grad_gate)]))],
    ]
    sums = [None, None]
    for index, gate in ((1, back1), (0, back2)):
        views = groups[index][0][1][1]
        views[0] = View(after(views[0].array, gate), views[0].rows, views[0].cols)
        own, far_part, give = upper_grads(groups[index], core, far)
        got = partner(give, "rep", 1)
        (far_part,) = fused(far_sum, "far_sum", far_part, got)
        sums[index] = [own, got, partner(far_part, "rep", 2)]
    leaf_grad, mid_grad = leaf_backward(
        placed,
        [msg0, msg1, msg2, msg3],
        [back0, back1, after(back2, far_part), back3],
        leaf_w,
        mid_w,
        first,
    )
    (upper,) = fused(last_sum, "last_sum", *sums[0], *sums[1], limit=16)
    return leaf_grad[None], mid_grad[None, None], upper[None]


def solution(mesh):
    placed = (
        P("rep", "sub", None),
        P("sub"),
        P(("sub", "rep"), None, None, None),
        P("sub", "rep", None, None),
        P("sub", None, None, None),
        P("rep", "sub"),
    )
    return jax.shard_map(
        on_device,
        mesh=mesh,
        in_specs=placed,
        out_specs=(
            P(("sub", "rep"), None, None, None),
            P("sub", "rep", None, None),
            P("sub", "rep", None, None),
        ),
        check_vma=False,
    )
```

```python
import functools

import jax
import jax.numpy as jnp
from jax import lax
from jax.experimental import pallas as pl
from jax.experimental.pallas import tpu as pltpu
from jax.sharding import PartitionSpec as P

EPSILON = 1e-06
CHILDREN = 4
MIB = 1024 * 1024


def partner(value, axis, offset):
    return lax.ppermute(value, axis, [(i, i ^ offset) for i in range(lax.axis_size(axis))])


def rms_factor(values):
    return lax.rsqrt(jnp.mean(values * values, axis=-1, keepdims=True) + EPSILON)


def norm_back(gradient, normed, factor):
    return factor * (gradient - normed * jnp.mean(gradient * normed, axis=-1, keepdims=True))


def matmul(left_arr, right_arr):
    return jnp.dot(left_arr, right_arr, preferred_element_type=jnp.float32)


def matmul_t(left_arr, right_arr):
    return lax.dot_general(
        left_arr, right_arr, (((1,), (1,)), ((), ())), preferred_element_type=jnp.float32
    )


def inner_t(left_arr, right_arr):
    return lax.dot_general(
        left_arr, right_arr, (((0,), (0,)), ((), ())), preferred_element_type=jnp.float32
    )


def bf16(value):
    return value.astype(jnp.bfloat16)


def f32(value):
    return value.astype(jnp.float32)


def whole_block():
    return pl.BlockSpec(memory_space=pltpu.VMEM)


def smem_block():
    return pl.BlockSpec(memory_space=pltpu.SMEM)


def bit_of(value, level):
    return jnp.bitwise_and(jnp.right_shift(value, level), 1)


def place_kernel(slots, depth, ids_ref, map_ref, regions_ref, cotangent_ref, *rest):
    outs, cotangent_out, wide = rest[:CHILDREN], rest[CHILDREN], rest[CHILDREN + 1]
    rows = regions_ref.shape[0] // slots
    parts = wide.shape[0]
    for part in range(parts):
        wide[part] = regions_ref[:, part * 128 : (part + 1) * 128].astype(jnp.float32)
    flip = 0
    for level in range(depth):
        flip = flip + bit_of(ids_ref[0], level) * (rows >> (level + 1))
    row = lax.broadcasted_iota(jnp.int32, (rows, rows), 0)
    col = lax.broadcasted_iota(jnp.int32, (rows, rows), 1)
    select = bf16(jnp.bitwise_xor(row, flip) == col)
    left = cotangent_ref[...]
    picked = 0.0
    for _ in range(3):
        top = bf16(left)
        left = left - f32(top)
        picked = picked + matmul(select, top)
    cotangent_out[...] = picked
    for offset in range(CHILDREN):
        node = jnp.bitwise_xor(ids_ref[1], offset)
        for child in range(CHILDREN):
            region = map_ref[node * CHILDREN + child]
            for part in range(parts):
                values = bf16(wide[part, pl.ds(region, rows, stride=slots), :])
                outs[offset][child, :, part * 128 : (part + 1) * 128] = bf16(
                    matmul(select, values)
                )


def place(regions, leaf_map, cotangent, ids, depth):
    rows, slots, feats = regions.shape
    flat = regions.reshape(rows * slots, feats)
    return pl.pallas_call(
        functools.partial(place_kernel, slots, depth),
        out_shape=[jax.ShapeDtypeStruct((CHILDREN, rows, feats), jnp.bfloat16)] * CHILDREN
        + [jax.ShapeDtypeStruct(cotangent.shape, cotangent.dtype)],
        in_specs=[smem_block(), smem_block(), whole_block(), whole_block()],
        out_specs=[whole_block()] * (CHILDREN + 1),
        scratch_shapes=[pltpu.VMEM((feats // 128, rows * slots, 128), jnp.float32)],
        compiler_params=pltpu.CompilerParams(vmem_limit_bytes=7 * MIB),
        name="place",
    )(ids, leaf_map, flat, cotangent)


def leaf_forward_kernel(count, *refs):
    placed, leaf_w, mid_w = refs[:count], refs[count], refs[count + 1]
    msgs, terms = refs[count + 2 : 2 * count + 2], refs[2 * count + 2 :]
    rows = placed[0].shape[1]
    product = None
    for child in range(CHILDREN):
        values = jnp.concatenate([ref[child] for ref in placed], axis=0)
        factor = 1.0 + matmul(values, leaf_w[child])
        product = factor if product is None else product * factor
    message = bf16(product * rms_factor(product))
    out = bf16(matmul(message, mid_w[...]))
    for i in range(count):
        msgs[i][...] = message[i * rows : (i + 1) * rows]
        terms[i][...] = out[i * rows : (i + 1) * rows]


def leaf_forward(placed, leaf_w, mid_w):
    count = len(placed)
    rows = placed[0].shape[1]
    width = mid_w.shape[0]
    return pl.pallas_call(
        functools.partial(leaf_forward_kernel, count),
        out_shape=[jax.ShapeDtypeStruct((rows, width), jnp.bfloat16)] * (2 * count),
        in_specs=[whole_block()] * (count + 2),
        out_specs=[whole_block()] * (2 * count),
        compiler_params=pltpu.CompilerParams(vmem_limit_bytes=14 * MIB),
        name="leaf_forward",
    )(*placed, leaf_w, mid_w)


def leaf_cotangents(placed, grads, leaf_w, mid_w):
    factors = [
        1.0 + matmul(jnp.concatenate([ref[child] for ref in placed], axis=0), leaf_w[child])
        for child in range(CHILDREN)
    ]
    low = factors[0] * factors[1]
    high = factors[2] * factors[3]
    product = low * high
    scale = rms_factor(product)
    back = matmul_t(jnp.concatenate([ref[...] for ref in grads], axis=0), mid_w[...])
    node = norm_back(back, product * scale, scale)
    high, low = node * high, node * low
    return [
        bf16(high * factors[1]),
        bf16(high * factors[0]),
        bf16(low * factors[3]),
        bf16(low * factors[2]),
    ]


def leaf_first_kernel(*refs):
    placed, grads, leaf_w, mid_w, out = refs[0:2], refs[2:4], refs[4], refs[5], refs[6]
    for child, value in enumerate(leaf_cotangents(placed, grads, leaf_w, mid_w)):
        out[child] = value


def leaf_first(placed, grads, leaf_w, mid_w):
    rows = placed[0].shape[1]
    return pl.pallas_call(
        leaf_first_kernel,
        out_shape=jax.ShapeDtypeStruct((CHILDREN, 2 * rows, mid_w.shape[0]), jnp.bfloat16),
        in_specs=[whole_block()] * 6,
        out_specs=whole_block(),
        compiler_params=pltpu.CompilerParams(vmem_limit_bytes=18 * MIB),
        name="leaf_first",
    )(*placed, *grads, leaf_w, mid_w)


def leaf_backward_kernel(*refs):
    placed, msgs, grads = refs[0:4], refs[4:8], refs[8:12]
    leaf_w, mid_w, first, leaf_out, mid_out = refs[12:17]
    all_grads = jnp.concatenate([ref[...] for ref in grads], axis=0)
    all_msgs = jnp.concatenate([ref[...] for ref in msgs], axis=0)
    mid_out[...] = bf16(inner_t(all_msgs, all_grads))
    second = leaf_cotangents(placed[2:], grads[2:], leaf_w, mid_w)
    for child in range(CHILDREN):
        values = jnp.concatenate([ref[child] for ref in placed], axis=0)
        cot = jnp.concatenate([first[child], second[child]], axis=0)
        leaf_out[child] = bf16(inner_t(values, cot))


def leaf_backward(placed, msgs, grads, leaf_w, mid_w, first):
    return pl.pallas_call(
        leaf_backward_kernel,
        out_shape=[
            jax.ShapeDtypeStruct(leaf_w.shape, jnp.bfloat16),
            jax.ShapeDtypeStruct(mid_w.shape, jnp.bfloat16),
        ],
        in_specs=[whole_block()] * 15,
        out_specs=[whole_block()] * 2,
        compiler_params=pltpu.CompilerParams(vmem_limit_bytes=30 * MIB),
        name="leaf_backward",
    )(*placed, *msgs, *grads, leaf_w, mid_w, first)


def fused(body, name, *args, limit=8, ids=None, plain=False):
    if plain or any(arg.shape[-2] % 16 or arg.shape[-1] % 128 for arg in args):
        return body(*args) if ids is None else body(ids, *args)
    count = len(args)
    if ids is None:
        shapes = jax.eval_shape(body, *args)
    else:
        shapes = jax.eval_shape(body, ids, *args)
        args = (ids, *args)

    def kernel(*refs):
        outs = refs[len(args) :]
        values = [ref[...] for ref in refs[len(args) - count : len(args)]]
        results = body(*values) if ids is None else body(refs[0], *values)
        for ref, result in zip(outs, results):
            ref[...] = result

    return pl.pallas_call(
        kernel,
        out_shape=shapes,
        in_specs=[smem_block()] * (len(args) - count) + [whole_block()] * count,
        out_specs=[whole_block()] * len(shapes),
        compiler_params=pltpu.CompilerParams(vmem_limit_bytes=limit * MIB),
        name=name,
    )(*args)


def join(pieces):
    if pieces[0].shape[0] % 16 == 0:
        return jnp.concatenate(pieces, axis=0)
    wide = lax.optimization_barrier(tuple(f32(piece) for piece in pieces))
    return bf16(lax.optimization_barrier(jnp.concatenate(wide, axis=0)))


def pack(pieces):
    arrays = []
    for array, _, _ in pieces:
        if not any(array is known for known in arrays):
            arrays.append(array)
    spots = [next(i for i, known in enumerate(arrays) if known is piece[0]) for piece in pieces]

    def body(*values):
        parts = [values[i][:, at : at + span] for i, (_, at, span) in zip(spots, pieces)]
        return (jnp.concatenate(parts, axis=1),)

    if any(piece[2] % 128 for piece in pieces):
        return body(*arrays)[0]
    return fused(body, "pack", *arrays, limit=6)[0]


def cut_kernel(depth, ids_ref, maps_ref, *refs):
    outs, split = refs[:-1], refs[-1]
    split[...] = jnp.swapaxes(maps_ref[...], 0, 1)
    width = maps_ref.shape[0]
    half = width // 2
    rows = pl.ds(pl.multiple_of(bit_of(ids_ref[1], 0) * half, half), half)
    for level in range(depth):
        span = width >> (level + 1)
        cols = pl.ds(width - 2 * span, span)
        side = bit_of(ids_ref[0], level)
        outs[3 * level][...] = split[side, :, cols]
        outs[3 * level + 1][...] = split[side, rows, cols]
        outs[3 * level + 2][...] = split[1 - side, rows, cols]
    span = width >> depth
    for side in range(2):
        outs[3 * depth + side][...] = split[side, :, width - span :]


def cut_maps(maps, ids, depth):
    width = maps.shape[0]
    half = width // 2
    spans = [width >> (level + 1) for level in range(depth)]
    if spans[-1] % 128 == 0:
        shapes = []
        for span in spans:
            shapes += [(width, span), (half, span), (half, span)]
        shapes += [(width, spans[-1])] * 2
        outs = pl.pallas_call(
            functools.partial(cut_kernel, depth),
            out_shape=[jax.ShapeDtypeStruct(shape, maps.dtype) for shape in shapes],
            in_specs=[smem_block(), whole_block()],
            out_specs=[whole_block()] * len(shapes),
            scratch_shapes=[pltpu.VMEM((2, width, width), maps.dtype)],
            compiler_params=pltpu.CompilerParams(vmem_limit_bytes=18 * MIB),
            name="cut_maps",
        )(ids, maps)
    else:
        maps = jnp.transpose(maps, (1, 0, 2))
        outs = []
        core = bit_of(ids[1], 0)
        for level, span in enumerate(spans):
            side = bit_of(ids[0], level)
            first = width - 2 * span
            outs.append(lax.dynamic_slice(maps, (side, 0, first), (1, width, span))[0])
            for which in (side, 1 - side):
                outs.append(lax.dynamic_slice(maps, (which, core * half, first), (1, half, span))[0])
        outs += [maps[0, :, width - spans[-1] :], maps[1, :, width - spans[-1] :]]
    return [outs[3 * i : 3 * i + 3] for i in range(depth)], outs[3 * depth :]


def assemble_kernel(spots, count, ids_ref, own_ref, *refs):
    out_ref = refs[-1]
    width, span = own_ref.shape
    half = width // 2
    block = jnp.bitwise_and(ids_ref[0], out_ref.shape[1] // span - 1)
    own_core = bit_of(ids_ref[1], 0)
    out_ref[:, pl.ds(pl.multiple_of(block * span, span), span)] = own_ref[...]
    for offset, index, at in spots:
        col = jnp.bitwise_xor(block, offset) * span
        for ref, core in ((refs[index], own_core), (refs[count + index], 1 - own_core)):
            out_ref[
                pl.ds(pl.multiple_of(core * half, half), half),
                pl.ds(pl.multiple_of(col, span), span),
            ] = ref[:, at : at + span]


def assemble(own, pieces, ids):
    width, span = own.shape
    count = len(pieces) + 1
    if span % 128 == 0:
        mine, other, spots = [], [], []
        for offset, (near_half, far_half, at) in pieces.items():
            known = [i for i, array in enumerate(mine) if array is near_half]
            if not known:
                mine.append(near_half)
                other.append(far_half)
                known = [len(mine) - 1]
            spots.append((offset, known[0], at))
        return pl.pallas_call(
            functools.partial(assemble_kernel, spots, len(mine)),
            out_shape=jax.ShapeDtypeStruct((width, span * count), own.dtype),
            in_specs=[smem_block()] + [whole_block()] * (2 * len(mine) + 1),
            out_specs=whole_block(),
            compiler_params=pltpu.CompilerParams(vmem_limit_bytes=8 * MIB),
            name="assemble",
        )(ids, own, *mine, *other)
    block = jnp.bitwise_and(ids[0], count - 1)
    core = bit_of(ids[1], 0)
    out = jnp.zeros((width, span * count), own.dtype)
    out = lax.dynamic_update_slice(out, own, (0, block * span))
    for offset, (near_half, far_half, at) in pieces.items():
        col = (block ^ offset) * span
        for array, which in ((near_half, core), (far_half, 1 - core)):
            part = array[:, at : at + span]
            out = lax.dynamic_update_slice(out, part, (which * (width // 2), col))
    return out


def after(value, *others):
    return lax.optimization_barrier((value, *others))[0]


class MapGather:
    def __init__(self, blocks, ids):
        self.blocks, self.ids = blocks, ids
        self.depth = len(blocks)
        self.spans = [block[0].shape[1] for block in blocks]
        self.held = [{0: (block[1], 0)} for block in blocks]
        self.first = partner(blocks[0][2], "sub", 1)
        self.early = [self.send([(level, 0) for level in range(1, self.depth)], 0)]

    def send(self, picks, stage, extra=None, gate=None):
        pieces = [(*self.held[level][offset], self.spans[level]) for level, offset in picks]
        picks = list(picks)
        if extra is not None:
            pieces.append((self.blocks[extra][2], 0, self.spans[extra]))
            picks.append((extra, 0))
        if gate is not None:
            pieces[-1] = (after(pieces[-1][0], gate), *pieces[-1][1:])
        value = pieces[0][0] if len(pieces) == 1 else pack(pieces)
        self.packed = value
        got = partner(value, "sub", 1 << stage)
        at = 0
        for level, offset in picks:
            self.held[level][offset ^ (1 << stage)] = (got, at)
            at += self.spans[level]
        return got

    def stage(self, stage, gate=None):
        picks = [
            (level, offset)
            for level in range(stage + 1, self.depth)
            for offset in self.held[level]
            if offset % (2 << stage) == 0
        ]
        self.early.append(self.send(picks, stage, stage, gate))

    def last(self, gate):
        picks = [
            (level, offset)
            for level in range(1, self.depth)
            for offset in self.held[level]
            if offset % 2 == 0 and offset > 0
        ]
        self.late = self.send(picks, 0, None, gate)

    def weight(self, level, exchanged):
        pieces = {}
        if level == 0:
            pieces[1] = (self.first, exchanged[0], 0)
        else:
            for offset, (array, at) in self.held[level].items():
                if offset == 0:
                    continue
                if array is self.late:
                    pieces[offset] = (array, exchanged[2], at)
                    continue
                pieces[offset] = (self.packed_early, exchanged[1], at + self.early_at(array))
        return assemble(self.blocks[level][0], pieces, self.ids)

    def early_at(self, array):
        at = 0
        for known in self.early:
            if known is array:
                return at
            at += known.shape[1]

    def pack_early(self, gate):
        pieces = [(array, 0, array.shape[1]) for array in self.early]
        pieces[0] = (after(self.early[0], gate), *pieces[0][1:])
        self.packed_early = pack(pieces)
        return self.packed_early


class View:
    def __init__(self, array, rows=None, cols=None):
        self.array = array
        self.rows = (0, array.shape[0]) if rows is None else rows
        self.cols = (0, array.shape[1]) if cols is None else cols
        self.shape = (self.rows[1] - self.rows[0], self.cols[1] - self.cols[0])

    def value(self):
        return self.array[slice(*self.rows), slice(*self.cols)]

    def part(self, first, last):
        return View(self.array, (self.rows[0] + first, self.rows[0] + last), self.cols)

    def gated(self, *gates):
        return View(after(self.array, *gates), self.rows, self.cols)

    def aligned(self):
        edges = (*self.rows, *self.cols)
        return all(edge % unit == 0 for edge, unit in zip(edges, (16, 16, 128, 128)))


def spots_of(views):
    arrays, spots = [], []
    for view in views:
        known = [i for i, array in enumerate(arrays) if array is view.array]
        if not known:
            arrays.append(view.array)
            known = [len(arrays) - 1]
        spots.append((known[0], view.rows, view.cols))
    return arrays, spots


def join_all(pieces):
    if all(piece.shape[0] % 16 == 0 for piece in pieces):
        return jnp.concatenate(pieces, axis=0)
    wide = lax.optimization_barrier(tuple(f32(piece) for piece in pieces))
    return bf16(lax.optimization_barrier(jnp.concatenate(wide, axis=0)))


def step(body, name, args, stacks=(), halves=(), level=0, far=None, ids=None, limit=8):
    groups = [list(stacks)] + [list(group) for group in halves] + [list(far or ())]
    views = [view for group in groups for view in group]
    arrays = list(args)
    for view in views:
        if not any(array is view.array for array in arrays):
            arrays.append(view.array)

    def cut(values, group):
        parts = []
        for view in group:
            index = next(i for i, array in enumerate(arrays) if array is view.array)
            parts.append(values[index][slice(*view.rows), slice(*view.cols)])
        return join_all(parts)

    def whole(ids, *values):
        results = list(body(*values[: len(args)]))
        if stacks:
            results.append(cut(values, groups[0]))
        if halves:
            own = bit_of(ids[0], level) == 1
            sends = []
            for group in groups[1:-1]:
                full = cut(values, group)
                half = full.shape[1] // 2
                low, high = full[:, :half], full[:, half:]
                results.append(jnp.where(own, high, low))
                sends.append(jnp.where(own, low, high))
            results.append(jnp.concatenate(sends, axis=1))
        if far:
            full = cut(values, groups[-1])
            half = full.shape[1] // 2
            results.append(jnp.where(bit_of(ids[1], 1) == 1, full[:, :half], full[:, half:]))
        return results

    plain = not all(view.aligned() for view in views)
    return fused(whole, name, *arrays, limit=limit, ids=ids, plain=plain)


def near_inputs_kernel(spots, ids_ref, far_ref, *refs):
    out_ref = refs[-1]
    quarter = out_ref.shape[1]
    other = 1 - bit_of(ids_ref[1], 0)
    lanes = pl.ds(pl.multiple_of((bit_of(ids_ref[1], 1) * 2 + other) * quarter, quarter), quarter)
    at = 0
    for index, (first, last), _ in spots:
        out_ref[at : at + last - first] = refs[index][first:last, lanes]
        at += last - first
    out_ref[at:] = far_ref[:, pl.ds(pl.multiple_of(other * quarter, quarter), quarter)]


def near_inputs(views, got, ids):
    quarter = views[0].shape[1] // 4
    if not all(view.aligned() for view in views):
        full = join_all([view.value() for view in views])
        other = 1 - bit_of(ids[1], 0)
        where = (bit_of(ids[1], 1) * 2 + other) * quarter
        own = lax.dynamic_slice_in_dim(full, where, quarter, 1)
        return jnp.concatenate(
            [own, lax.dynamic_slice_in_dim(got, other * quarter, quarter, 1)], axis=0
        )
    arrays, spots = spots_of(views)
    return pl.pallas_call(
        functools.partial(near_inputs_kernel, spots),
        out_shape=jax.ShapeDtypeStruct((2 * got.shape[0], quarter), jnp.bfloat16),
        in_specs=[smem_block()] + [whole_block()] * (len(arrays) + 1),
        out_specs=whole_block(),
        compiler_params=pltpu.CompilerParams(vmem_limit_bytes=8 * MIB),
        name="near_inputs",
    )(ids, got, *arrays)


def side_by_side_kernel(groups, *refs):
    out_ref = refs[-1]
    col = 0
    for spots in groups:
        at = 0
        for index, rows, cols in spots:
            span = cols[1] - cols[0]
            count = rows[1] - rows[0]
            out_ref[at : at + count, col : col + span] = refs[index][slice(*rows), slice(*cols)]
            at += count
        col += span


def side_by_side(groups):
    views = [view for group in groups for view in group]
    if not all(view.aligned() for view in views):
        return jnp.concatenate(
            [join_all([view.value() for view in group]) for group in groups], axis=1
        )
    arrays, spots = spots_of(views)
    by_group = [[spots.pop(0) for _ in group] for group in groups]
    shape = (
        sum(view.shape[0] for view in groups[0]),
        sum(group[0].shape[1] for group in groups),
    )
    return pl.pallas_call(
        functools.partial(side_by_side_kernel, by_group),
        out_shape=jax.ShapeDtypeStruct(shape, jnp.bfloat16),
        in_specs=[whole_block()] * len(arrays),
        out_specs=whole_block(),
        compiler_params=pltpu.CompilerParams(vmem_limit_bytes=6 * MIB),
        name="side_by_side",
    )(*arrays)


def upper_grads_kernel(spots, spans, rows, ids_ref, far_ref, near_ref, *refs):
    grads, inputs, out_ref, both = refs[:4], refs[4:-2], refs[-2], refs[-1]
    quarter = out_ref.shape[0]
    core, far = bit_of(ids_ref[1], 0), bit_of(ids_ref[1], 1)
    lanes = pl.ds(pl.multiple_of((far * 2 + core) * quarter, quarter), quarter)
    far_lanes = pl.ds(pl.multiple_of(core * quarter, quarter), quarter)
    total = far_ref.shape[0]
    col = 0
    for level, span in enumerate(spans):
        for turn in range(2):
            here, at = spots[level][turn]
            pieces = [inputs[i][slice(*edges), lanes] for i, edges, _ in here]
            pieces.append(far_ref[at : at + rows, far_lanes])
            pieces.append(near_ref[at : at + rows])
            pieces.append(near_ref[total + at : total + at + rows])
            grad = jnp.concatenate(
                [ref[turn * rows : (turn + 1) * rows, col : col + span] for ref in grads], axis=0
            )
            value = bf16(inner_t(jnp.concatenate(pieces, axis=0), grad))
            side = turn
            if level < len(spans) - 1:
                side = jnp.bitwise_xor(bit_of(ids_ref[0], level), turn)
            both[side, :, col : col + span] = value
        col += span
    out_ref[...] = jnp.swapaxes(both[...], 0, 1)


def upper_grads(entries, far_got, near_got, grads, ids):
    depth = len(entries) - 1
    width = entries[0][0][0].shape[1]
    rows = sum(view.shape[0] for view in entries[0][0])
    spans = [width >> (level + 1) for level in range(depth)] + [width >> depth]
    views = [view for entry in entries for turn in entry for view in turn]
    starts, at = [], 0
    for level in range(depth + 1):
        starts.append([at, at + rows if level < depth else at])
        at += 2 * rows
    if all(view.aligned() for view in views) and spans[-1] % 128 == 0:
        arrays, flat = spots_of(views)
        spots = [
            [([flat.pop(0) for _ in entry[turn]], starts[level][turn]) for turn in range(2)]
            for level, entry in enumerate(entries)
        ]
        return pl.pallas_call(
            functools.partial(upper_grads_kernel, spots, spans, rows),
            out_shape=jax.ShapeDtypeStruct((width // 4, 2, width), jnp.bfloat16),
            in_specs=[smem_block()] + [whole_block()] * (len(arrays) + 6),
            out_specs=whole_block(),
            scratch_shapes=[pltpu.VMEM((2, width // 4, width), jnp.bfloat16)],
            compiler_params=pltpu.CompilerParams(vmem_limit_bytes=16 * MIB),
            name="upper_grads",
        )(ids, far_got, near_got, *grads, *arrays)
    quarter = width // 4
    core, far = bit_of(ids[1], 0), bit_of(ids[1], 1)
    total = far_got.shape[0]
    parts, col = [], 0
    for level, span in enumerate(spans):
        both = []
        for turn in range(2):
            at = starts[level][turn]
            own = join_all([view.value() for view in entries[level][turn]])
            pieces = [
                lax.dynamic_slice_in_dim(own, (far * 2 + core) * quarter, quarter, 1),
                lax.dynamic_slice_in_dim(far_got[at : at + rows], core * quarter, quarter, 1),
                near_got[at : at + rows],
                near_got[total + at : total + at + rows],
            ]
            grad = [part[turn * rows : (turn + 1) * rows, col : col + span] for part in grads]
            both.append(bf16(inner_t(jnp.concatenate(pieces), jnp.concatenate(grad))))
        if level < depth:
            swap = bit_of(ids[0], level) == 1
            both = [jnp.where(swap, both[1 - i], both[i]) for i in range(2)]
        parts.append(jnp.stack(both, axis=1))
        col += span
    return jnp.concatenate(parts, axis=2)


def mid_forward(term, near, far, weight):
    product = (1.0 + f32(term)) * (1.0 + f32(near)) * f32(far)
    return up_product(bf16(product * rms_factor(product)), weight)


def up_product(message, weight):
    up = matmul(message, weight)
    keep = up.shape[0] // 2
    return message, up[:keep], bf16(up[keep:])


def up_forward(own_up, other_up, weight):
    joined = (1.0 + own_up) * (1.0 + f32(other_up))
    return up_product(bf16(joined * rms_factor(joined)), weight)


def top_forward(own_up, other_up):
    joined = (1.0 + own_up) * (1.0 + f32(other_up))
    return (bf16(joined * rms_factor(joined)),)


def head_body(cotangent, left, right, low, high):
    root = join([low, high])
    value = matmul(root, left)
    gating = jax.nn.sigmoid(matmul(root, right))
    grad_value = bf16(cotangent * gating)
    grad_gate = bf16(cotangent * value * gating * (1.0 - gating))
    back = matmul_t(grad_value, left) + matmul_t(grad_gate, right)
    half = root.shape[0] // 2
    return root, grad_value, grad_gate, back[:half], bf16(back[half:])


def joined(low, high):
    return (join([low, high]),)


def partial_sum(own, got):
    total = own + f32(got)
    half = total.shape[0] // 2
    return total[:half], bf16(total[half:])


def level_back(grad_msg, own_up, other_up):
    own_up, other_up = 1.0 + own_up, 1.0 + f32(other_up)
    joined = own_up * other_up
    scaling = rms_factor(joined)
    grad = norm_back(grad_msg, joined * scaling, scaling)
    return bf16(grad * other_up), bf16(grad * own_up)


def top_back(own_up, other_up, own_part, got):
    return level_back(own_part + f32(got), own_up, other_up)


def down_back(own_up, other_up, weight, low, high):
    return level_back(matmul_t(join([low, high]), weight), own_up, other_up)


def mid_back(term, near, far, weight, low, high):
    own, near, far = 1.0 + f32(term), 1.0 + f32(near), f32(far)
    pair = own * near
    product = pair * far
    scale = rms_factor(product)
    grad_msg = matmul_t(join([low, high]), weight)
    grad = norm_back(grad_msg, product * scale, scale)
    grad_pair = grad * far
    return bf16(grad_pair * near), bf16(grad_pair * own), bf16(grad * pair)


def far_back(grad_pair, term, near):
    grad_pair = f32(grad_pair)
    return bf16(grad_pair * (1.0 + f32(near))), bf16(grad_pair * (1.0 + f32(term)))


def pair_product(term, near):
    return (bf16((1.0 + f32(term)) * (1.0 + f32(near))),)


def on_device(regions, leaf_map, leaf_bond_weight, mid_weight, upper_weight, head_cotangent):
    rows = regions.shape[0]
    sub_count = lax.axis_size("sub")
    depth = sub_count.bit_length() - 1
    ids = jnp.stack([lax.axis_index("sub"), lax.axis_index("rep")]).astype(jnp.int32)
    leaf_w = leaf_bond_weight[0]
    mid_w = mid_weight[0, 0]

    blocks, (head_left, head_right) = cut_maps(upper_weight[0], ids, depth)
    gather = MapGather(blocks, ids)

    *sent, cotangent = place(after(regions, gather.packed), leaf_map, head_cotangent, ids, depth)
    near = partner(sent[1], "rep", 1)
    far_both = partner(sent[3], "rep", 3)
    far_one = partner(sent[2], "rep", 2)
    placed = [sent[0], near, far_one, far_both]
    for stage in reversed(range(1, depth)):
        gather.stage(stage, sent[3] if stage < depth - 1 else None)

    near_placed = [sent[0], after(near, gather.packed)]
    msg0, msg1, term0, term1 = leaf_forward(near_placed, leaf_w, mid_w)
    near0 = partner(term1, "rep", 1)
    far_placed = [after(far_one, term1), far_both]
    msg2, msg3, term2, term3 = leaf_forward(far_placed, leaf_w, mid_w)
    near2 = partner(term3, "rep", 1)
    (pair,) = fused(pair_product, "pair_product", term2, near2)
    far_pair = partner(pair, "rep", 2)
    exchanged = [partner(after(gather.first, term1), "rep", 1)]
    gather.last(pair)

    weights, messages, own_ups, other_ups = [], [], [], []
    for level in range(depth):
        if level == 1:
            exchanged.append(partner(gather.pack_early(other_ups[0]), "rep", 1))
            exchanged.append(partner(after(gather.late, other_ups[0]), "rep", 1))
        weights.append(gather.weight(level, exchanged))
        if level == 0:
            outs = fused(mid_forward, "mid_forward", term0, near0, far_pair, weights[0])
        else:
            outs = fused(up_forward, "up_forward", own_ups[-1], other_ups[-1], weights[level])
        messages.append(outs[0])
        own_ups.append(outs[1])
        other_ups.append(partner(outs[2], "sub", 1 << level))
    (root,) = fused(top_forward, "top_forward", own_ups[-1], other_ups[-1])

    turns = [[[View(message)], []] for message in messages]

    def gather_turns(stage, value):
        got = partner(value, "sub", 1 << stage)
        at = 0
        for level in range(stage, depth):
            count = sum(view.shape[0] for view in turns[level][0])
            turns[level][0 if level > stage else 1].append(View(got, (at, at + count)))
            at += count
            if level > stage:
                turns[level][1].append(View(got, (at, at + count)))
                at += count

    gather_turns(depth - 1, messages[-1])
    for stage in reversed(range(1, depth)):
        views = []
        for level in range(stage - 1, depth):
            views += turns[level][0] + (turns[level][1] if level > stage - 1 else [])
        got = partner(root, "sub", 1 << stage)
        root, stack = step(joined, "joined", [root, got], stacks=views, ids=ids)
        gather_turns(stage - 1, stack)
    root_high = partner(root, "sub", 1)
    root, grad_value, grad_gate, grad_msg, give = fused(
        head_body, "head", cotangent, head_left, head_right, root, root_high
    )
    for level in range(depth - 1):
        got = partner(give, "sub", 1 << level)
        grad_msg, give = fused(partial_sum, "partial_sum", grad_msg, got)
    last_part = partner(give, "sub", 1 << (depth - 1))
    turns.append([[View(root)], [View(root)]])
    inputs = [view for entry in turns[:depth] for turn in entry for view in turn] + turns[depth][0]

    lows, highs = [None] * depth, [None] * depth
    columns = [None] * depth

    def groups_of(stage):
        return [
            [View(lows[level]), View(highs[level])] if columns[level] is None else columns[level]
            for level in range(stage, depth)
        ]

    def spread(stage, keeps, send):
        got = partner(send, "sub", 1 << stage)
        at = 0
        for level, keep in zip(range(stage, depth), keeps):
            span = keep.shape[1]
            columns[level] = [View(keep), View(got, None, (at, at + span))]
            at += span

    def columns_of(level, turn):
        if level == depth:
            return [View(grad_gate if turn else grad_value)]
        if level == 0:
            return [columns[0][turn]]
        count = rows >> level
        return [
            view.part(i * count, (i + 1) * count)
            for view in columns[level]
            for i in range(turn, view.shape[0] // count, 2)
        ]

    far_got = None
    for level in reversed(range(depth)):
        if level == depth - 1:
            low, high = fused(
                top_back, "top_back", own_ups[level], other_ups[level], grad_msg, last_part
            )
        else:
            above = level + 1
            low, high, *rest = step(
                down_back,
                "down_back",
                [own_ups[level], other_ups[level], weights[above], lows[above], highs[above]],
                halves=groups_of(above),
                level=above,
                far=inputs if above == depth - 1 else None,
                ids=ids,
                limit=12,
            )
            if above == depth - 1:
                far_got = partner(rest.pop(), "rep", 2)
            spread(above, rest[:-1], rest[-1])
        lows[level] = low
        highs[level] = partner(high, "sub", 1 << level)

    back0, back1, pair_back, *rest = step(
        mid_back,
        "mid_back",
        [term0, near0, far_pair, weights[0], lows[0], highs[0]],
        halves=groups_of(0),
        level=0,
        ids=ids,
        limit=12,
    )
    back1 = partner(back1, "rep", 1)
    pair_back = partner(pair_back, "rep", 2)
    spread(0, rest[:-1], rest[-1])
    first = leaf_first(placed[:2], [back0, back1], leaf_w, mid_w)
    groups = [
        [view for turn in range(2) for view in columns_of(level, turn)]
        for level in range(depth + 1)
    ]
    groups[0][0] = groups[0][0].gated(first)
    own_grads = side_by_side(groups)
    far_grads = partner(own_grads, "rep", 2)
    near_grads = partner(own_grads, "rep", 1)
    back2, back3 = fused(far_back, "far_back", after(pair_back, own_grads), term2, near2)
    back3 = partner(back3, "rep", 1)
    near_got = partner(near_inputs([inputs[0].gated(back2)] + inputs[1:], far_got, ids), "rep", 1)
    leaf_grad, mid_grad = leaf_backward(
        placed, [msg0, msg1, msg2, msg3], [back0, back1, back2, back3], leaf_w, mid_w, first
    )
    grads = [own_grads, far_grads, near_grads]
    grads.append(partner(after(far_grads, leaf_grad), "rep", 1))
    upper = upper_grads(turns, far_got, near_got, grads, ids)
    return leaf_grad[None], mid_grad[None, None], upper[None]


def solution(mesh):
    placed = (
        P("rep", "sub", None),
        P("sub"),
        P(("sub", "rep"), None, None, None),
        P("sub", "rep", None, None),
        P("sub", None, None, None),
        P("rep", "sub"),
    )
    return jax.shard_map(
        on_device,
        mesh=mesh,
        in_specs=placed,
        out_specs=(
            P(("sub", "rep"), None, None, None),
            P("sub", "rep", None, None),
            P("sub", "rep", None, None),
        ),
        check_vma=False,
    )
```

```python
import functools

import jax
import jax.numpy as jnp
from jax import lax
from jax.experimental import pallas as pl
from jax.experimental.pallas import tpu as pltpu
from jax.sharding import PartitionSpec as P

EPSILON = 1e-06
CHILDREN = 4
MIB = 1024 * 1024


def partner(value, axis, offset):
    return lax.ppermute(value, axis, [(i, i ^ offset) for i in range(lax.axis_size(axis))])


def rms_factor(values):
    return lax.rsqrt(jnp.mean(values * values, axis=-1, keepdims=True) + EPSILON)


def norm_back(gradient, normed, factor):
    return factor * (gradient - normed * jnp.mean(gradient * normed, axis=-1, keepdims=True))


def matmul(left_arr, right_arr):
    return jnp.dot(left_arr, right_arr, preferred_element_type=jnp.float32)


def matmul_t(left_arr, right_arr):
    return lax.dot_general(
        left_arr, right_arr, (((1,), (1,)), ((), ())), preferred_element_type=jnp.float32
    )


def inner_t(left_arr, right_arr):
    return lax.dot_general(
        left_arr, right_arr, (((0,), (0,)), ((), ())), preferred_element_type=jnp.float32
    )


def bf16(value):
    return value.astype(jnp.bfloat16)


def f32(value):
    return value.astype(jnp.float32)


def whole_block():
    return pl.BlockSpec(memory_space=pltpu.VMEM)


def smem_block():
    return pl.BlockSpec(memory_space=pltpu.SMEM)


def bit_of(value, level):
    return jnp.bitwise_and(jnp.right_shift(value, level), 1)


def place_kernel(slots, depth, ids_ref, map_ref, regions_ref, cotangent_ref, *rest):
    outs, cotangent_out, wide = rest[:CHILDREN], rest[CHILDREN], rest[CHILDREN + 1]
    rows = regions_ref.shape[0] // slots
    parts = wide.shape[0]
    for part in range(parts):
        wide[part] = regions_ref[:, part * 128 : (part + 1) * 128].astype(jnp.float32)
    flip = 0
    for level in range(depth):
        flip = flip + bit_of(ids_ref[0], level) * (rows >> (level + 1))
    row = lax.broadcasted_iota(jnp.int32, (rows, rows), 0)
    col = lax.broadcasted_iota(jnp.int32, (rows, rows), 1)
    select = bf16(jnp.bitwise_xor(row, flip) == col)
    left = cotangent_ref[...]
    picked = 0.0
    for _ in range(3):
        top = bf16(left)
        left = left - f32(top)
        picked = picked + matmul(select, top)
    cotangent_out[...] = picked
    for offset in range(CHILDREN):
        node = jnp.bitwise_xor(ids_ref[1], offset)
        for child in range(CHILDREN):
            region = map_ref[node * CHILDREN + child]
            for part in range(parts):
                values = bf16(wide[part, pl.ds(region, rows, stride=slots), :])
                outs[offset][child, :, part * 128 : (part + 1) * 128] = bf16(
                    matmul(select, values)
                )


def place(regions, leaf_map, cotangent, ids, depth):
    rows, slots, feats = regions.shape
    flat = regions.reshape(rows * slots, feats)
    return pl.pallas_call(
        functools.partial(place_kernel, slots, depth),
        out_shape=[jax.ShapeDtypeStruct((CHILDREN, rows, feats), jnp.bfloat16)] * CHILDREN
        + [jax.ShapeDtypeStruct(cotangent.shape, cotangent.dtype)],
        in_specs=[smem_block(), smem_block(), whole_block(), whole_block()],
        out_specs=[whole_block()] * (CHILDREN + 1),
        scratch_shapes=[pltpu.VMEM((feats // 128, rows * slots, 128), jnp.float32)],
        compiler_params=pltpu.CompilerParams(vmem_limit_bytes=7 * MIB),
        name="place",
    )(ids, leaf_map, flat, cotangent)


def leaf_forward_kernel(count, *refs):
    placed, leaf_w, mid_w = refs[:count], refs[count], refs[count + 1]
    msgs, terms = refs[count + 2 : 2 * count + 2], refs[2 * count + 2 :]
    rows = placed[0].shape[1]
    product = None
    for child in range(CHILDREN):
        values = jnp.concatenate([ref[child] for ref in placed], axis=0)
        factor = 1.0 + matmul(values, leaf_w[child])
        product = factor if product is None else product * factor
    message = bf16(product * rms_factor(product))
    out = bf16(matmul(message, mid_w[...]))
    for i in range(count):
        msgs[i][...] = message[i * rows : (i + 1) * rows]
        terms[i][...] = out[i * rows : (i + 1) * rows]


def leaf_forward(placed, leaf_w, mid_w):
    count = len(placed)
    rows = placed[0].shape[1]
    width = mid_w.shape[0]
    return pl.pallas_call(
        functools.partial(leaf_forward_kernel, count),
        out_shape=[jax.ShapeDtypeStruct((rows, width), jnp.bfloat16)] * (2 * count),
        in_specs=[whole_block()] * (count + 2),
        out_specs=[whole_block()] * (2 * count),
        compiler_params=pltpu.CompilerParams(vmem_limit_bytes=14 * MIB),
        name="leaf_forward",
    )(*placed, leaf_w, mid_w)


def leaf_cotangents(placed, grads, leaf_w, mid_w):
    factors = [
        1.0 + matmul(jnp.concatenate([ref[child] for ref in placed], axis=0), leaf_w[child])
        for child in range(CHILDREN)
    ]
    low = factors[0] * factors[1]
    high = factors[2] * factors[3]
    product = low * high
    scale = rms_factor(product)
    back = matmul_t(jnp.concatenate([ref[...] for ref in grads], axis=0), mid_w[...])
    node = norm_back(back, product * scale, scale)
    high, low = node * high, node * low
    return [
        bf16(high * factors[1]),
        bf16(high * factors[0]),
        bf16(low * factors[3]),
        bf16(low * factors[2]),
    ]


def leaf_first_kernel(*refs):
    placed, grads, leaf_w, mid_w, out = refs[0:2], refs[2:4], refs[4], refs[5], refs[6]
    for child, value in enumerate(leaf_cotangents(placed, grads, leaf_w, mid_w)):
        out[child] = value


def leaf_first(placed, grads, leaf_w, mid_w):
    rows = placed[0].shape[1]
    return pl.pallas_call(
        leaf_first_kernel,
        out_shape=jax.ShapeDtypeStruct((CHILDREN, 2 * rows, mid_w.shape[0]), jnp.bfloat16),
        in_specs=[whole_block()] * 6,
        out_specs=whole_block(),
        compiler_params=pltpu.CompilerParams(vmem_limit_bytes=18 * MIB),
        name="leaf_first",
    )(*placed, *grads, leaf_w, mid_w)


def leaf_backward_kernel(*refs):
    placed, msgs, grads = refs[0:4], refs[4:8], refs[8:12]
    leaf_w, mid_w, first, leaf_out, mid_out = refs[12:17]
    all_grads = jnp.concatenate([ref[...] for ref in grads], axis=0)
    all_msgs = jnp.concatenate([ref[...] for ref in msgs], axis=0)
    mid_out[...] = bf16(inner_t(all_msgs, all_grads))
    second = leaf_cotangents(placed[2:], grads[2:], leaf_w, mid_w)
    for child in range(CHILDREN):
        values = jnp.concatenate([ref[child] for ref in placed], axis=0)
        cot = jnp.concatenate([first[child], second[child]], axis=0)
        leaf_out[child] = bf16(inner_t(values, cot))


def leaf_backward(placed, msgs, grads, leaf_w, mid_w, first):
    return pl.pallas_call(
        leaf_backward_kernel,
        out_shape=[
            jax.ShapeDtypeStruct(leaf_w.shape, jnp.bfloat16),
            jax.ShapeDtypeStruct(mid_w.shape, jnp.bfloat16),
        ],
        in_specs=[whole_block()] * 15,
        out_specs=[whole_block()] * 2,
        compiler_params=pltpu.CompilerParams(vmem_limit_bytes=30 * MIB),
        name="leaf_backward",
    )(*placed, *msgs, *grads, leaf_w, mid_w, first)


def fused(body, name, *args, limit=8, ids=None, plain=False):
    if plain or any(arg.shape[-2] % 16 or arg.shape[-1] % 128 for arg in args):
        return body(*args) if ids is None else body(ids, *args)
    count = len(args)
    if ids is None:
        shapes = jax.eval_shape(body, *args)
    else:
        shapes = jax.eval_shape(body, ids, *args)
        args = (ids, *args)

    def kernel(*refs):
        outs = refs[len(args) :]
        values = [ref[...] for ref in refs[len(args) - count : len(args)]]
        results = body(*values) if ids is None else body(refs[0], *values)
        for ref, result in zip(outs, results):
            ref[...] = result

    return pl.pallas_call(
        kernel,
        out_shape=shapes,
        in_specs=[smem_block()] * (len(args) - count) + [whole_block()] * count,
        out_specs=[whole_block()] * len(shapes),
        compiler_params=pltpu.CompilerParams(vmem_limit_bytes=limit * MIB),
        name=name,
    )(*args)


def join(pieces):
    if pieces[0].shape[0] % 16 == 0:
        return jnp.concatenate(pieces, axis=0)
    wide = lax.optimization_barrier(tuple(f32(piece) for piece in pieces))
    return bf16(lax.optimization_barrier(jnp.concatenate(wide, axis=0)))


def pack(pieces):
    arrays = []
    for array, _, _ in pieces:
        if not any(array is known for known in arrays):
            arrays.append(array)
    spots = [next(i for i, known in enumerate(arrays) if known is piece[0]) for piece in pieces]

    def body(*values):
        parts = [values[i][:, at : at + span] for i, (_, at, span) in zip(spots, pieces)]
        return (jnp.concatenate(parts, axis=1),)

    if any(piece[2] % 128 for piece in pieces):
        return body(*arrays)[0]
    return fused(body, "pack", *arrays, limit=6)[0]


def cut_kernel(depth, ids_ref, maps_ref, *refs):
    outs, split = refs[:-1], refs[-1]
    split[...] = jnp.swapaxes(maps_ref[...], 0, 1)
    width = maps_ref.shape[0]
    half = width // 2
    rows = pl.ds(pl.multiple_of(bit_of(ids_ref[1], 0) * half, half), half)
    for level in range(depth):
        span = width >> (level + 1)
        cols = pl.ds(width - 2 * span, span)
        side = bit_of(ids_ref[0], level)
        outs[3 * level][...] = split[side, :, cols]
        outs[3 * level + 1][...] = split[side, rows, cols]
        outs[3 * level + 2][...] = split[1 - side, rows, cols]
    span = width >> depth
    for side in range(2):
        outs[3 * depth + side][...] = split[side, :, width - span :]


def cut_maps(maps, ids, depth):
    width = maps.shape[0]
    half = width // 2
    spans = [width >> (level + 1) for level in range(depth)]
    if spans[-1] % 128 == 0:
        shapes = []
        for span in spans:
            shapes += [(width, span), (half, span), (half, span)]
        shapes += [(width, spans[-1])] * 2
        outs = pl.pallas_call(
            functools.partial(cut_kernel, depth),
            out_shape=[jax.ShapeDtypeStruct(shape, maps.dtype) for shape in shapes],
            in_specs=[smem_block(), whole_block()],
            out_specs=[whole_block()] * len(shapes),
            scratch_shapes=[pltpu.VMEM((2, width, width), maps.dtype)],
            compiler_params=pltpu.CompilerParams(vmem_limit_bytes=18 * MIB),
            name="cut_maps",
        )(ids, maps)
    else:
        maps = jnp.transpose(maps, (1, 0, 2))
        outs = []
        core = bit_of(ids[1], 0)
        for level, span in enumerate(spans):
            side = bit_of(ids[0], level)
            first = width - 2 * span
            outs.append(lax.dynamic_slice(maps, (side, 0, first), (1, width, span))[0])
            for which in (side, 1 - side):
                outs.append(lax.dynamic_slice(maps, (which, core * half, first), (1, half, span))[0])
        outs += [maps[0, :, width - spans[-1] :], maps[1, :, width - spans[-1] :]]
    return [outs[3 * i : 3 * i + 3] for i in range(depth)], outs[3 * depth :]


def assemble_kernel(spots, count, ids_ref, own_ref, *refs):
    out_ref = refs[-1]
    width, span = own_ref.shape
    half = width // 2
    block = jnp.bitwise_and(ids_ref[0], out_ref.shape[1] // span - 1)
    own_core = bit_of(ids_ref[1], 0)
    out_ref[:, pl.ds(pl.multiple_of(block * span, span), span)] = own_ref[...]
    for offset, index, at in spots:
        col = jnp.bitwise_xor(block, offset) * span
        for ref, core in ((refs[index], own_core), (refs[count + index], 1 - own_core)):
            out_ref[
                pl.ds(pl.multiple_of(core * half, half), half),
                pl.ds(pl.multiple_of(col, span), span),
            ] = ref[:, at : at + span]


def assemble(own, pieces, ids):
    width, span = own.shape
    count = len(pieces) + 1
    if span % 128 == 0:
        mine, other, spots = [], [], []
        for offset, (near_half, far_half, at) in pieces.items():
            known = [i for i, array in enumerate(mine) if array is near_half]
            if not known:
                mine.append(near_half)
                other.append(far_half)
                known = [len(mine) - 1]
            spots.append((offset, known[0], at))
        return pl.pallas_call(
            functools.partial(assemble_kernel, spots, len(mine)),
            out_shape=jax.ShapeDtypeStruct((width, span * count), own.dtype),
            in_specs=[smem_block()] + [whole_block()] * (2 * len(mine) + 1),
            out_specs=whole_block(),
            compiler_params=pltpu.CompilerParams(vmem_limit_bytes=8 * MIB),
            name="assemble",
        )(ids, own, *mine, *other)
    block = jnp.bitwise_and(ids[0], count - 1)
    core = bit_of(ids[1], 0)
    out = jnp.zeros((width, span * count), own.dtype)
    out = lax.dynamic_update_slice(out, own, (0, block * span))
    for offset, (near_half, far_half, at) in pieces.items():
        col = (block ^ offset) * span
        for array, which in ((near_half, core), (far_half, 1 - core)):
            part = array[:, at : at + span]
            out = lax.dynamic_update_slice(out, part, (which * (width // 2), col))
    return out


def after(value, *others):
    return lax.optimization_barrier((value, *others))[0]


class MapGather:
    def __init__(self, blocks, ids):
        self.blocks, self.ids = blocks, ids
        self.depth = len(blocks)
        self.spans = [block[0].shape[1] for block in blocks]
        self.held = [{0: (block[1], 0)} for block in blocks]
        self.other = {}
        pieces = [(blocks[0][2], 0, self.spans[0])]
        pieces += [(blocks[i][1], 0, self.spans[i]) for i in range(1, self.depth)]
        self.first = pack(pieces)
        got = partner(self.first, "sub", 1)
        self.received = got
        at = 0
        for level in range(self.depth):
            self.held[level][1] = (got, at)
            at += self.spans[level]

    def relay(self, level, stage, gate=None):
        if stage == level:
            offsets, value = [0], self.blocks[level][2]
            if gate is not None:
                value = after(value, gate)
        else:
            offsets = [i for i in self.held[level] if i % (2 << stage) == 0]
            if stage == 0:
                offsets = [i for i in offsets if i > 0]
            pieces = [(*self.held[level][i], self.spans[level]) for i in offsets]
            if gate is not None:
                pieces[-1] = (after(pieces[-1][0], gate), *pieces[-1][1:])
            if len(pieces) == 1 and pieces[0][0].shape[1] == pieces[0][2]:
                value = pieces[0][0]
            else:
                value = pack(pieces)
            for place, offset in enumerate(offsets):
                if offset > 0:
                    self.held[level][offset] = (value, place * self.spans[level])
        got = partner(value, "sub", 1 << stage)
        for place, offset in enumerate(offsets):
            self.held[level][offset ^ (1 << stage)] = (got, place * self.spans[level])
        return value

    def exchange(self, level, gate):
        for offset, (array, _) in self.held[level].items():
            if offset > 0 and id(array) not in self.other:
                self.other[id(array)] = (array, partner(after(array, gate), "rep", 1))

    def weight(self, level):
        pieces = {}
        for offset, (array, at) in self.held[level].items():
            if offset > 0:
                pieces[offset] = (array, self.other[id(array)][1], at)
        return assemble(self.blocks[level][0], pieces, self.ids)


class View:
    def __init__(self, array, rows=None, cols=None):
        self.array = array
        self.rows = (0, array.shape[0]) if rows is None else rows
        self.cols = (0, array.shape[1]) if cols is None else cols
        self.shape = (self.rows[1] - self.rows[0], self.cols[1] - self.cols[0])

    def value(self):
        return self.array[slice(*self.rows), slice(*self.cols)]

    def part(self, first, last):
        return View(self.array, (self.rows[0] + first, self.rows[0] + last), self.cols)

    def gated(self, *gates):
        return View(after(self.array, *gates), self.rows, self.cols)

    def aligned(self):
        edges = (*self.rows, *self.cols)
        return all(edge % unit == 0 for edge, unit in zip(edges, (16, 16, 128, 128)))


def spots_of(views):
    arrays, spots = [], []
    for view in views:
        known = [i for i, array in enumerate(arrays) if array is view.array]
        if not known:
            arrays.append(view.array)
            known = [len(arrays) - 1]
        spots.append((known[0], view.rows, view.cols))
    return arrays, spots


def join_all(pieces):
    if all(piece.shape[0] % 16 == 0 for piece in pieces):
        return jnp.concatenate(pieces, axis=0)
    wide = lax.optimization_barrier(tuple(f32(piece) for piece in pieces))
    return bf16(lax.optimization_barrier(jnp.concatenate(wide, axis=0)))


def step(body, name, args, stacks=(), halves=(), level=0, far=None, ids=None, limit=8):
    groups = [list(stacks)] + [list(group) for group in halves] + [list(far or ())]
    views = [view for group in groups for view in group]
    arrays = list(args)
    for view in views:
        if not any(array is view.array for array in arrays):
            arrays.append(view.array)

    def cut(values, group):
        parts = []
        for view in group:
            index = next(i for i, array in enumerate(arrays) if array is view.array)
            parts.append(values[index][slice(*view.rows), slice(*view.cols)])
        return join_all(parts)

    def whole(ids, *values):
        results = list(body(*values[: len(args)]))
        if stacks:
            results.append(cut(values, groups[0]))
        if halves:
            own = bit_of(ids[0], level) == 1
            sends = []
            for group in groups[1:-1]:
                full = cut(values, group)
                half = full.shape[1] // 2
                low, high = full[:, :half], full[:, half:]
                results.append(jnp.where(own, high, low))
                sends.append(jnp.where(own, low, high))
            results.append(jnp.concatenate(sends, axis=1))
        if far:
            full = cut(values, groups[-1])
            half = full.shape[1] // 2
            results.append(jnp.where(bit_of(ids[1], 1) == 1, full[:, :half], full[:, half:]))
        return results

    plain = not all(view.aligned() for view in views)
    return fused(whole, name, *arrays, limit=limit, ids=ids, plain=plain)


def near_inputs_kernel(spots, ids_ref, far_ref, *refs):
    out_ref = refs[-1]
    quarter = out_ref.shape[1]
    other = 1 - bit_of(ids_ref[1], 0)
    lanes = pl.ds(pl.multiple_of((bit_of(ids_ref[1], 1) * 2 + other) * quarter, quarter), quarter)
    at = 0
    for index, (first, last), _ in spots:
        out_ref[at : at + last - first] = refs[index][first:last, lanes]
        at += last - first
    out_ref[at:] = far_ref[:, pl.ds(pl.multiple_of(other * quarter, quarter), quarter)]


def near_inputs(views, got, ids):
    quarter = views[0].shape[1] // 4
    if not all(view.aligned() for view in views):
        full = join_all([view.value() for view in views])
        other = 1 - bit_of(ids[1], 0)
        where = (bit_of(ids[1], 1) * 2 + other) * quarter
        own = lax.dynamic_slice_in_dim(full, where, quarter, 1)
        return jnp.concatenate(
            [own, lax.dynamic_slice_in_dim(got, other * quarter, quarter, 1)], axis=0
        )
    arrays, spots = spots_of(views)
    return pl.pallas_call(
        functools.partial(near_inputs_kernel, spots),
        out_shape=jax.ShapeDtypeStruct((2 * got.shape[0], quarter), jnp.bfloat16),
        in_specs=[smem_block()] + [whole_block()] * (len(arrays) + 1),
        out_specs=whole_block(),
        compiler_params=pltpu.CompilerParams(vmem_limit_bytes=8 * MIB),
        name="near_inputs",
    )(ids, got, *arrays)


def side_by_side_kernel(groups, *refs):
    out_ref = refs[-1]
    col = 0
    for spots in groups:
        at = 0
        for index, rows, cols in spots:
            span = cols[1] - cols[0]
            count = rows[1] - rows[0]
            out_ref[at : at + count, col : col + span] = refs[index][slice(*rows), slice(*cols)]
            at += count
        col += span


def side_by_side(groups):
    views = [view for group in groups for view in group]
    if not all(view.aligned() for view in views):
        return jnp.concatenate(
            [join_all([view.value() for view in group]) for group in groups], axis=1
        )
    arrays, spots = spots_of(views)
    by_group = [[spots.pop(0) for _ in group] for group in groups]
    shape = (
        sum(view.shape[0] for view in groups[0]),
        sum(group[0].shape[1] for group in groups),
    )
    return pl.pallas_call(
        functools.partial(side_by_side_kernel, by_group),
        out_shape=jax.ShapeDtypeStruct(shape, jnp.bfloat16),
        in_specs=[whole_block()] * len(arrays),
        out_specs=whole_block(),
        compiler_params=pltpu.CompilerParams(vmem_limit_bytes=6 * MIB),
        name="side_by_side",
    )(*arrays)


def upper_grads_kernel(spots, spans, rows, ids_ref, far_ref, near_ref, *refs):
    grads, inputs, out_ref, both = refs[:4], refs[4:-2], refs[-2], refs[-1]
    quarter = out_ref.shape[0]
    core, far = bit_of(ids_ref[1], 0), bit_of(ids_ref[1], 1)
    lanes = pl.ds(pl.multiple_of((far * 2 + core) * quarter, quarter), quarter)
    far_lanes = pl.ds(pl.multiple_of(core * quarter, quarter), quarter)
    total = far_ref.shape[0]
    col = 0
    for level, span in enumerate(spans):
        for turn in range(2):
            here, at = spots[level][turn]
            pieces = [inputs[i][slice(*edges), lanes] for i, edges, _ in here]
            pieces.append(far_ref[at : at + rows, far_lanes])
            pieces.append(near_ref[at : at + rows])
            pieces.append(near_ref[total + at : total + at + rows])
            grad = jnp.concatenate(
                [ref[turn * rows : (turn + 1) * rows, col : col + span] for ref in grads], axis=0
            )
            value = bf16(inner_t(jnp.concatenate(pieces, axis=0), grad))
            side = turn
            if level < len(spans) - 1:
                side = jnp.bitwise_xor(bit_of(ids_ref[0], level), turn)
            both[side, :, col : col + span] = value
        col += span
    out_ref[...] = jnp.swapaxes(both[...], 0, 1)


def upper_grads(entries, far_got, near_got, grads, ids):
    depth = len(entries) - 1
    width = entries[0][0][0].shape[1]
    rows = sum(view.shape[0] for view in entries[0][0])
    spans = [width >> (level + 1) for level in range(depth)] + [width >> depth]
    views = [view for entry in entries for turn in entry for view in turn]
    starts, at = [], 0
    for level in range(depth + 1):
        starts.append([at, at + rows if level < depth else at])
        at += 2 * rows
    if all(view.aligned() for view in views) and spans[-1] % 128 == 0:
        arrays, flat = spots_of(views)
        spots = [
            [([flat.pop(0) for _ in entry[turn]], starts[level][turn]) for turn in range(2)]
            for level, entry in enumerate(entries)
        ]
        return pl.pallas_call(
            functools.partial(upper_grads_kernel, spots, spans, rows),
            out_shape=jax.ShapeDtypeStruct((width // 4, 2, width), jnp.bfloat16),
            in_specs=[smem_block()] + [whole_block()] * (len(arrays) + 6),
            out_specs=whole_block(),
            scratch_shapes=[pltpu.VMEM((2, width // 4, width), jnp.bfloat16)],
            compiler_params=pltpu.CompilerParams(vmem_limit_bytes=16 * MIB),
            name="upper_grads",
        )(ids, far_got, near_got, *grads, *arrays)
    quarter = width // 4
    core, far = bit_of(ids[1], 0), bit_of(ids[1], 1)
    total = far_got.shape[0]
    parts, col = [], 0
    for level, span in enumerate(spans):
        both = []
        for turn in range(2):
            at = starts[level][turn]
            own = join_all([view.value() for view in entries[level][turn]])
            pieces = [
                lax.dynamic_slice_in_dim(own, (far * 2 + core) * quarter, quarter, 1),
                lax.dynamic_slice_in_dim(far_got[at : at + rows], core * quarter, quarter, 1),
                near_got[at : at + rows],
                near_got[total + at : total + at + rows],
            ]
            grad = [part[turn * rows : (turn + 1) * rows, col : col + span] for part in grads]
            both.append(bf16(inner_t(jnp.concatenate(pieces), jnp.concatenate(grad))))
        if level < depth:
            swap = bit_of(ids[0], level) == 1
            both = [jnp.where(swap, both[1 - i], both[i]) for i in range(2)]
        parts.append(jnp.stack(both, axis=1))
        col += span
    return jnp.concatenate(parts, axis=2)


def mid_forward(term, near, far, weight):
    product = (1.0 + f32(term)) * (1.0 + f32(near)) * f32(far)
    return up_product(bf16(product * rms_factor(product)), weight)


def up_product(message, weight):
    up = matmul(message, weight)
    keep = up.shape[0] // 2
    return message, up[:keep], bf16(up[keep:])


def up_forward(own_up, other_up, weight):
    joined = (1.0 + own_up) * (1.0 + f32(other_up))
    return up_product(bf16(joined * rms_factor(joined)), weight)


def top_forward(own_up, other_up):
    joined = (1.0 + own_up) * (1.0 + f32(other_up))
    return (bf16(joined * rms_factor(joined)),)


def head_body(cotangent, left, right, low, high):
    root = join([low, high])
    value = matmul(root, left)
    gating = jax.nn.sigmoid(matmul(root, right))
    grad_value = bf16(cotangent * gating)
    grad_gate = bf16(cotangent * value * gating * (1.0 - gating))
    back = matmul_t(grad_value, left) + matmul_t(grad_gate, right)
    half = root.shape[0] // 2
    return root, grad_value, grad_gate, back[:half], bf16(back[half:])


def joined(low, high):
    return (join([low, high]),)


def partial_sum(own, got):
    total = own + f32(got)
    half = total.shape[0] // 2
    return total[:half], bf16(total[half:])


def level_back(grad_msg, own_up, other_up):
    own_up, other_up = 1.0 + own_up, 1.0 + f32(other_up)
    joined = own_up * other_up
    scaling = rms_factor(joined)
    grad = norm_back(grad_msg, joined * scaling, scaling)
    return bf16(grad * other_up), bf16(grad * own_up)


def top_back(own_up, other_up, own_part, got):
    return level_back(own_part + f32(got), own_up, other_up)


def down_back(own_up, other_up, weight, low, high):
    return level_back(matmul_t(join([low, high]), weight), own_up, other_up)


def mid_back(term, near, far, weight, low, high):
    own, near, far = 1.0 + f32(term), 1.0 + f32(near), f32(far)
    pair = own * near
    product = pair * far
    scale = rms_factor(product)
    grad_msg = matmul_t(join([low, high]), weight)
    grad = norm_back(grad_msg, product * scale, scale)
    grad_pair = grad * far
    return bf16(grad_pair * near), bf16(grad_pair * own), bf16(grad * pair)


def far_back(grad_pair, term, near):
    grad_pair = f32(grad_pair)
    return bf16(grad_pair * (1.0 + f32(near))), bf16(grad_pair * (1.0 + f32(term)))


def pair_product(term, near):
    return (bf16((1.0 + f32(term)) * (1.0 + f32(near))),)


def on_device(regions, leaf_map, leaf_bond_weight, mid_weight, upper_weight, head_cotangent):
    rows = regions.shape[0]
    sub_count = lax.axis_size("sub")
    depth = sub_count.bit_length() - 1
    ids = jnp.stack([lax.axis_index("sub"), lax.axis_index("rep")]).astype(jnp.int32)
    leaf_w = leaf_bond_weight[0]
    mid_w = mid_weight[0, 0]

    blocks, (head_left, head_right) = cut_maps(upper_weight[0], ids, depth)
    gather = MapGather(blocks, ids)

    *sent, cotangent = place(after(regions, gather.first), leaf_map, head_cotangent, ids, depth)
    near = partner(sent[1], "rep", 1)
    far_both = partner(sent[3], "rep", 3)
    far_one = partner(sent[2], "rep", 2)
    placed = [sent[0], near, far_one, far_both]
    for level in reversed(range(1, depth)):
        value = gather.relay(level, level, sent[3] if level < depth - 1 else None)
    gather.got = gather.held[1][2][0]
    for level in range(2, depth):
        for stage in reversed(range(1, level)):
            value = gather.relay(level, stage, sent[3])

    msg0, msg1, term0, term1 = leaf_forward(placed[:2], leaf_w, mid_w)
    near0 = partner(term1, "rep", 1)
    far_placed = [after(far_one, term1, value, gather.got), far_both]
    msg2, msg3, term2, term3 = leaf_forward(far_placed, leaf_w, mid_w)
    near2 = partner(term3, "rep", 1)
    for level in range(1, depth):
        gather.relay(level, 0, term3)
    gather.exchange(0, term3)
    (pair,) = fused(pair_product, "pair_product", term2, near2)
    far_pair = partner(pair, "rep", 2)
    for level in range(1, depth):
        gather.exchange(level, pair)

    weights, messages, own_ups, other_ups = [], [], [], []
    for level in range(depth):
        weights.append(gather.weight(level))
        if level == 0:
            outs = fused(mid_forward, "mid_forward", term0, near0, far_pair, weights[0])
        else:
            outs = fused(up_forward, "up_forward", own_ups[-1], other_ups[-1], weights[level])
        messages.append(outs[0])
        own_ups.append(outs[1])
        other_ups.append(partner(outs[2], "sub", 1 << level))
    (root,) = fused(top_forward, "top_forward", own_ups[-1], other_ups[-1])

    turns = [[[View(message)], []] for message in messages]

    def gather_turns(stage, value, levels):
        got = partner(value, "sub", 1 << stage)
        at = 0
        for level in levels:
            count = sum(view.shape[0] for view in turns[level][0])
            turns[level][0 if level > stage else 1].append(View(got, (at, at + count)))
            at += count
            if level > stage:
                turns[level][1].append(View(got, (at, at + count)))
                at += count

    gather_turns(0, after(messages[0], other_ups[0]), [0])
    gather_turns(depth - 1, messages[-1], [depth - 1])
    for stage in reversed(range(1, depth)):
        views = []
        for level in range(max(stage - 1, 1), depth):
            views += turns[level][0] + (turns[level][1] if level > stage - 1 else [])
        got = partner(root, "sub", 1 << stage)
        if stage == depth - 1:
            root = after(root, turns[0][1][0].array)
        root, stack = step(joined, "joined", [root, got], stacks=views, ids=ids)
        if stage > 1:
            gather_turns(stage - 1, stack, range(stage - 1, depth))
    root_high = partner(root, "sub", 1)
    root, grad_value, grad_gate, grad_msg, give = fused(
        head_body, "head", cotangent, head_left, head_right, root, root_high
    )
    for level in range(depth - 1):
        got = partner(give, "sub", 1 << level)
        grad_msg, give = fused(partial_sum, "partial_sum", grad_msg, got)
        if level == 0:
            gather_turns(0, after(stack, give), range(1, depth))
    last_part = partner(give, "sub", 1 << (depth - 1))
    turns.append([[View(root)], [View(root)]])
    inputs = [view for entry in turns[:depth] for turn in entry for view in turn] + turns[depth][0]

    lows, highs = [None] * depth, [None] * depth
    columns = [None] * depth

    def groups_of(stage):
        return [
            [View(lows[level]), View(highs[level])] if columns[level] is None else columns[level]
            for level in range(stage, depth)
        ]

    def spread(stage, keeps, send):
        got = partner(send, "sub", 1 << stage)
        at = 0
        for level, keep in zip(range(stage, depth), keeps):
            span = keep.shape[1]
            columns[level] = [View(keep), View(got, None, (at, at + span))]
            at += span

    def columns_of(level, turn):
        if level == depth:
            return [View(grad_gate if turn else grad_value)]
        if level == 0:
            return [columns[0][turn]]
        count = rows >> level
        return [
            view.part(i * count, (i + 1) * count)
            for view in columns[level]
            for i in range(turn, view.shape[0] // count, 2)
        ]

    far_got = None
    for level in reversed(range(depth)):
        if level == depth - 1:
            low, high = fused(
                top_back, "top_back", own_ups[level], other_ups[level], grad_msg, last_part
            )
        else:
            above = level + 1
            low, high, *rest = step(
                down_back,
                "down_back",
                [own_ups[level], other_ups[level], weights[above], lows[above], highs[above]],
                halves=groups_of(above),
                level=above,
                far=inputs if above == depth - 1 else None,
                ids=ids,
                limit=12,
            )
            if above == depth - 1:
                far_got = partner(rest.pop(), "rep", 2)
            spread(above, rest[:-1], rest[-1])
        lows[level] = low
        highs[level] = partner(high, "sub", 1 << level)

    back0, back1, pair_back, *rest = step(
        mid_back,
        "mid_back",
        [term0, near0, far_pair, weights[0], lows[0], highs[0]],
        halves=groups_of(0),
        level=0,
        ids=ids,
        limit=12,
    )
    back1 = partner(back1, "rep", 1)
    pair_back = partner(pair_back, "rep", 2)
    spread(0, rest[:-1], rest[-1])
    first = leaf_first(placed[:2], [back0, back1], leaf_w, mid_w)
    groups = [
        [view for turn in range(2) for view in columns_of(level, turn)]
        for level in range(depth + 1)
    ]
    groups[0][0] = groups[0][0].gated(first)
    own_grads = side_by_side(groups)
    far_grads = partner(own_grads, "rep", 2)
    near_grads = partner(own_grads, "rep", 1)
    back2, back3 = fused(far_back, "far_back", after(pair_back, own_grads), term2, near2)
    back3 = partner(back3, "rep", 1)
    near_got = partner(near_inputs([inputs[0].gated(back2)] + inputs[1:], far_got, ids), "rep", 1)
    leaf_grad, mid_grad = leaf_backward(
        placed, [msg0, msg1, msg2, msg3], [back0, back1, back2, back3], leaf_w, mid_w, first
    )
    grads = [own_grads, far_grads, near_grads]
    grads.append(partner(after(far_grads, leaf_grad), "rep", 1))
    upper = upper_grads(turns, far_got, near_got, grads, ids)
    return leaf_grad[None], mid_grad[None, None], upper[None]


def solution(mesh):
    placed = (
        P("rep", "sub", None),
        P("sub"),
        P(("sub", "rep"), None, None, None),
        P("sub", "rep", None, None),
        P("sub", None, None, None),
        P("rep", "sub"),
    )
    return jax.shard_map(
        on_device,
        mesh=mesh,
        in_specs=placed,
        out_specs=(
            P(("sub", "rep"), None, None, None),
            P("sub", "rep", None, None),
            P("sub", "rep", None, None),
        ),
        check_vma=False,
    )
```

```python
import functools

import jax
import jax.numpy as jnp
from jax import lax
from jax.experimental import pallas as pl
from jax.experimental.pallas import tpu as pltpu
from jax.sharding import PartitionSpec as P

EPSILON = 1e-06
CHILDREN = 4
MIB = 1024 * 1024


def partner(value, axis, offset):
    return lax.ppermute(value, axis, [(i, i ^ offset) for i in range(lax.axis_size(axis))])


def rms_factor(values):
    return lax.rsqrt(jnp.mean(values * values, axis=-1, keepdims=True) + EPSILON)


def norm_back(gradient, normed, factor):
    return factor * (gradient - normed * jnp.mean(gradient * normed, axis=-1, keepdims=True))


def matmul(left_arr, right_arr):
    return jnp.dot(left_arr, right_arr, preferred_element_type=jnp.float32)


def matmul_t(left_arr, right_arr):
    return lax.dot_general(
        left_arr, right_arr, (((1,), (1,)), ((), ())), preferred_element_type=jnp.float32
    )


def inner_t(left_arr, right_arr):
    return lax.dot_general(
        left_arr, right_arr, (((0,), (0,)), ((), ())), preferred_element_type=jnp.float32
    )


def bf16(value):
    return value.astype(jnp.bfloat16)


def f32(value):
    return value.astype(jnp.float32)


def whole_block():
    return pl.BlockSpec(memory_space=pltpu.VMEM)


def smem_block():
    return pl.BlockSpec(memory_space=pltpu.SMEM)


def bit_of(value, level):
    return jnp.bitwise_and(jnp.right_shift(value, level), 1)


def place_kernel(slots, depth, ids_ref, map_ref, regions_ref, cotangent_ref, *rest):
    outs, keep_ref, send_ref, wide = rest[:CHILDREN], *rest[CHILDREN:]
    rows = regions_ref.shape[0] // slots
    parts = wide.shape[0]
    for part in range(parts):
        wide[part] = regions_ref[:, part * 128 : (part + 1) * 128].astype(jnp.float32)
    flip = 0
    for level in range(depth):
        flip = flip + bit_of(ids_ref[0], level) * (rows >> (level + 1))
    row = lax.broadcasted_iota(jnp.int32, (rows, rows), 0)
    col = lax.broadcasted_iota(jnp.int32, (rows, rows), 1)
    select = bf16(jnp.bitwise_xor(row, flip) == col)
    block = rows >> depth
    wanted = jnp.bitwise_and(row, block - 1)
    for level in range(depth):
        wanted = wanted + bit_of(row // block, level) * (block << (depth - 1 - level))
    pick = bf16(jnp.bitwise_xor(wanted, flip) == col)
    left = cotangent_ref[...]
    picked = 0.0
    for _ in range(3):
        top = bf16(left)
        left = left - f32(top)
        picked = picked + matmul(pick, top)
    keep_ref[...] = picked[: rows // 2]
    send_ref[...] = picked[rows // 2 :]
    for offset in range(CHILDREN):
        node = jnp.bitwise_xor(ids_ref[1], offset)
        for child in range(CHILDREN):
            region = map_ref[node * CHILDREN + child]
            for part in range(parts):
                values = bf16(wide[part, pl.ds(region, rows, stride=slots), :])
                outs[offset][child, :, part * 128 : (part + 1) * 128] = bf16(
                    matmul(select, values)
                )


def place(regions, leaf_map, cotangent, ids, depth):
    rows, slots, feats = regions.shape
    flat = regions.reshape(rows * slots, feats)
    return pl.pallas_call(
        functools.partial(place_kernel, slots, depth),
        out_shape=[jax.ShapeDtypeStruct((CHILDREN, rows, feats), jnp.bfloat16)] * CHILDREN
        + [jax.ShapeDtypeStruct((rows // 2, cotangent.shape[1]), cotangent.dtype)] * 2,
        in_specs=[smem_block(), smem_block(), whole_block(), whole_block()],
        out_specs=[whole_block()] * (CHILDREN + 2),
        scratch_shapes=[pltpu.VMEM((feats // 128, rows * slots, 128), jnp.float32)],
        compiler_params=pltpu.CompilerParams(vmem_limit_bytes=7 * MIB),
        name="place",
    )(ids, leaf_map, flat, cotangent)


def leaf_forward_kernel(count, *refs):
    placed, leaf_w, mid_w = refs[:count], refs[count], refs[count + 1]
    msgs, terms = refs[count + 2 : 2 * count + 2], refs[2 * count + 2 :]
    rows = placed[0].shape[1]
    product = None
    for child in range(CHILDREN):
        values = jnp.concatenate([ref[child] for ref in placed], axis=0)
        factor = 1.0 + matmul(values, leaf_w[child])
        product = factor if product is None else product * factor
    message = bf16(product * rms_factor(product))
    out = bf16(matmul(message, mid_w[...]))
    for i in range(count):
        msgs[i][...] = message[i * rows : (i + 1) * rows]
        terms[i][...] = out[i * rows : (i + 1) * rows]


def leaf_forward(placed, leaf_w, mid_w):
    count = len(placed)
    rows = placed[0].shape[1]
    width = mid_w.shape[0]
    return pl.pallas_call(
        functools.partial(leaf_forward_kernel, count),
        out_shape=[jax.ShapeDtypeStruct((rows, width), jnp.bfloat16)] * (2 * count),
        in_specs=[whole_block()] * (count + 2),
        out_specs=[whole_block()] * (2 * count),
        compiler_params=pltpu.CompilerParams(vmem_limit_bytes=14 * MIB),
        name="leaf_forward",
    )(*placed, leaf_w, mid_w)


def leaf_cotangents(placed, grads, leaf_w, mid_w):
    factors = [
        1.0 + matmul(jnp.concatenate([ref[child] for ref in placed], axis=0), leaf_w[child])
        for child in range(CHILDREN)
    ]
    low = factors[0] * factors[1]
    high = factors[2] * factors[3]
    product = low * high
    scale = rms_factor(product)
    back = matmul_t(jnp.concatenate([ref[...] for ref in grads], axis=0), mid_w[...])
    node = norm_back(back, product * scale, scale)
    high, low = node * high, node * low
    return [
        bf16(high * factors[1]),
        bf16(high * factors[0]),
        bf16(low * factors[3]),
        bf16(low * factors[2]),
    ]


def leaf_first_kernel(*refs):
    placed, grads, leaf_w, mid_w, out = refs[0:2], refs[2:4], refs[4], refs[5], refs[6]
    for child, value in enumerate(leaf_cotangents(placed, grads, leaf_w, mid_w)):
        out[child] = value


def leaf_first(placed, grads, leaf_w, mid_w):
    rows = placed[0].shape[1]
    return pl.pallas_call(
        leaf_first_kernel,
        out_shape=jax.ShapeDtypeStruct((CHILDREN, 2 * rows, mid_w.shape[0]), jnp.bfloat16),
        in_specs=[whole_block()] * 6,
        out_specs=whole_block(),
        compiler_params=pltpu.CompilerParams(vmem_limit_bytes=18 * MIB),
        name="leaf_first",
    )(*placed, *grads, leaf_w, mid_w)


def leaf_backward_kernel(*refs):
    placed, msgs, grads = refs[0:4], refs[4:8], refs[8:12]
    leaf_w, mid_w, first, leaf_out, mid_out = refs[12:17]
    all_grads = jnp.concatenate([ref[...] for ref in grads], axis=0)
    all_msgs = jnp.concatenate([ref[...] for ref in msgs], axis=0)
    mid_out[...] = bf16(inner_t(all_msgs, all_grads))
    second = leaf_cotangents(placed[2:], grads[2:], leaf_w, mid_w)
    for child in range(CHILDREN):
        values = jnp.concatenate([ref[child] for ref in placed], axis=0)
        cot = jnp.concatenate([first[child], second[child]], axis=0)
        leaf_out[child] = bf16(inner_t(values, cot))


def leaf_backward(placed, msgs, grads, leaf_w, mid_w, first):
    return pl.pallas_call(
        leaf_backward_kernel,
        out_shape=[
            jax.ShapeDtypeStruct(leaf_w.shape, jnp.bfloat16),
            jax.ShapeDtypeStruct(mid_w.shape, jnp.bfloat16),
        ],
        in_specs=[whole_block()] * 15,
        out_specs=[whole_block()] * 2,
        compiler_params=pltpu.CompilerParams(vmem_limit_bytes=30 * MIB),
        name="leaf_backward",
    )(*placed, *msgs, *grads, leaf_w, mid_w, first)


def fused(body, name, *args, limit=8, ids=None, plain=False):
    if plain or any(arg.shape[-2] % 16 or arg.shape[-1] % 128 for arg in args):
        return body(*args) if ids is None else body(ids, *args)
    count = len(args)
    if ids is None:
        shapes = jax.eval_shape(body, *args)
    else:
        shapes = jax.eval_shape(body, ids, *args)
        args = (ids, *args)

    def kernel(*refs):
        outs = refs[len(args) :]
        values = [ref[...] for ref in refs[len(args) - count : len(args)]]
        results = body(*values) if ids is None else body(refs[0], *values)
        for ref, result in zip(outs, results):
            ref[...] = result

    return pl.pallas_call(
        kernel,
        out_shape=shapes,
        in_specs=[smem_block()] * (len(args) - count) + [whole_block()] * count,
        out_specs=[whole_block()] * len(shapes),
        compiler_params=pltpu.CompilerParams(vmem_limit_bytes=limit * MIB),
        name=name,
    )(*args)


def join(pieces):
    if pieces[0].shape[0] % 16 == 0:
        return jnp.concatenate(pieces, axis=0)
    wide = lax.optimization_barrier(tuple(f32(piece) for piece in pieces))
    return bf16(lax.optimization_barrier(jnp.concatenate(wide, axis=0)))


def pack(pieces):
    arrays = []
    for array, _, _ in pieces:
        if not any(array is known for known in arrays):
            arrays.append(array)
    spots = [next(i for i, known in enumerate(arrays) if known is piece[0]) for piece in pieces]

    def body(*values):
        parts = [values[i][:, at : at + span] for i, (_, at, span) in zip(spots, pieces)]
        return (jnp.concatenate(parts, axis=1),)

    if any(piece[2] % 128 for piece in pieces):
        return body(*arrays)[0]
    return fused(body, "pack", *arrays, limit=6)[0]


def cut_kernel(depth, ids_ref, maps_ref, *refs):
    outs, split = refs[:-1], refs[-1]
    split[...] = jnp.swapaxes(maps_ref[...], 0, 1)
    width = maps_ref.shape[0]
    half = width // 2
    rows = pl.ds(pl.multiple_of(bit_of(ids_ref[1], 0) * half, half), half)
    for level in range(depth):
        span = width >> (level + 1)
        cols = pl.ds(width - 2 * span, span)
        side = bit_of(ids_ref[0], level)
        outs[3 * level][...] = split[side, :, cols]
        outs[3 * level + 1][...] = split[side, rows, cols]
        outs[3 * level + 2][...] = split[1 - side, rows, cols]
    span = width >> depth
    for side in range(2):
        outs[3 * depth + side][...] = split[side, :, width - span :]
        outs[3 * depth + 2][:, side * span : (side + 1) * span] = split[side, rows, width - span :]


def cut_maps(maps, ids, depth):
    width = maps.shape[0]
    half = width // 2
    spans = [width >> (level + 1) for level in range(depth)]
    if spans[-1] % 128 == 0:
        shapes = []
        for span in spans:
            shapes += [(width, span), (half, span), (half, span)]
        shapes += [(width, spans[-1])] * 2 + [(half, 2 * spans[-1])]
        outs = pl.pallas_call(
            functools.partial(cut_kernel, depth),
            out_shape=[jax.ShapeDtypeStruct(shape, maps.dtype) for shape in shapes],
            in_specs=[smem_block(), whole_block()],
            out_specs=[whole_block()] * len(shapes),
            scratch_shapes=[pltpu.VMEM((2, width, width), maps.dtype)],
            compiler_params=pltpu.CompilerParams(vmem_limit_bytes=18 * MIB),
            name="cut_maps",
        )(ids, maps)
    else:
        maps = jnp.transpose(maps, (1, 0, 2))
        outs = []
        core = bit_of(ids[1], 0)
        for level, span in enumerate(spans):
            side = bit_of(ids[0], level)
            first = width - 2 * span
            outs.append(lax.dynamic_slice(maps, (side, 0, first), (1, width, span))[0])
            for which in (side, 1 - side):
                outs.append(lax.dynamic_slice(maps, (which, core * half, first), (1, half, span))[0])
        outs += [maps[0, :, width - spans[-1] :], maps[1, :, width - spans[-1] :]]
        both = jnp.concatenate(outs[-2:], axis=1)
        outs.append(lax.dynamic_slice_in_dim(both, core * half, half, 0))
    return [outs[3 * i : 3 * i + 3] for i in range(depth)], outs[3 * depth :]


def assemble_kernel(spots, count, ids_ref, own_ref, *refs):
    out_ref = refs[-1]
    width, span = own_ref.shape
    half = width // 2
    block = jnp.bitwise_and(ids_ref[0], out_ref.shape[1] // span - 1)
    own_core = bit_of(ids_ref[1], 0)
    out_ref[:, pl.ds(pl.multiple_of(block * span, span), span)] = own_ref[...]
    for offset, index, at in spots:
        col = jnp.bitwise_xor(block, offset) * span
        for ref, core in ((refs[index], own_core), (refs[count + index], 1 - own_core)):
            out_ref[
                pl.ds(pl.multiple_of(core * half, half), half),
                pl.ds(pl.multiple_of(col, span), span),
            ] = ref[:, at : at + span]


def assemble(own, pieces, ids):
    width, span = own.shape
    count = len(pieces) + 1
    if span % 128 == 0:
        mine, other, spots = [], [], []
        for offset, (near_half, far_half, at) in pieces.items():
            known = [i for i, array in enumerate(mine) if array is near_half]
            if not known:
                mine.append(near_half)
                other.append(far_half)
                known = [len(mine) - 1]
            spots.append((offset, known[0], at))
        return pl.pallas_call(
            functools.partial(assemble_kernel, spots, len(mine)),
            out_shape=jax.ShapeDtypeStruct((width, span * count), own.dtype),
            in_specs=[smem_block()] + [whole_block()] * (2 * len(mine) + 1),
            out_specs=whole_block(),
            compiler_params=pltpu.CompilerParams(vmem_limit_bytes=8 * MIB),
            name="assemble",
        )(ids, own, *mine, *other)
    block = jnp.bitwise_and(ids[0], count - 1)
    core = bit_of(ids[1], 0)
    out = jnp.zeros((width, span * count), own.dtype)
    out = lax.dynamic_update_slice(out, own, (0, block * span))
    for offset, (near_half, far_half, at) in pieces.items():
        col = (block ^ offset) * span
        for array, which in ((near_half, core), (far_half, 1 - core)):
            part = array[:, at : at + span]
            out = lax.dynamic_update_slice(out, part, (which * (width // 2), col))
    return out


def assemble_head_kernel(spots, count, ids_ref, left_ref, right_ref, *refs):
    out_ref = refs[-1]
    width, span = left_ref.shape
    half, total = width // 2, out_ref.shape[1] // 2
    out_ref[:, :span] = left_ref[...]
    out_ref[:, total : total + span] = right_ref[...]
    own_core = bit_of(ids_ref[1], 0)
    for offset, index, at in spots:
        for ref, core in ((refs[index], own_core), (refs[count + index], 1 - own_core)):
            rows = pl.ds(pl.multiple_of(core * half, half), half)
            for side in range(2):
                col = side * total + (offset // 2) * span
                out_ref[rows, col : col + span] = ref[:, at + side * span : at + (side + 1) * span]


def assemble_head(left, right, pieces, ids):
    width, span = left.shape
    total = span * (len(pieces) + 1)
    mine, other, spots = [], [], []
    for offset, (near_half, far_half, at) in pieces.items():
        known = [i for i, array in enumerate(mine) if array is near_half]
        if not known:
            mine.append(near_half)
            other.append(far_half)
            known = [len(mine) - 1]
        spots.append((offset, known[0], at))
    if span % 128 == 0:
        return pl.pallas_call(
            functools.partial(assemble_head_kernel, spots, len(mine)),
            out_shape=jax.ShapeDtypeStruct((width, 2 * total), left.dtype),
            in_specs=[smem_block()] + [whole_block()] * (2 * len(mine) + 2),
            out_specs=whole_block(),
            compiler_params=pltpu.CompilerParams(vmem_limit_bytes=8 * MIB),
            name="assemble_head",
        )(ids, left, right, *mine, *other)
    core = bit_of(ids[1], 0)
    out = jnp.zeros((width, 2 * total), left.dtype)
    out = lax.dynamic_update_slice(out, left, (0, 0))
    out = lax.dynamic_update_slice(out, right, (0, total))
    for offset, index, at in spots:
        for array, which in ((mine[index], core), (other[index], 1 - core)):
            for side in range(2):
                part = array[:, at + side * span : at + (side + 1) * span]
                col = side * total + (offset // 2) * span
                out = lax.dynamic_update_slice(out, part, (which * (width // 2), col))
    return out


def after(value, *others):
    return lax.optimization_barrier((value, *others))[0]


class MapGather:
    def __init__(self, blocks, head_half, ids):
        self.blocks, self.ids = blocks + [(None, head_half, None)], ids
        self.depth = len(blocks)
        blocks = self.blocks
        self.spans = [block[1].shape[1] for block in blocks]
        self.held = [{0: (block[1], 0)} for block in blocks]
        self.other = {}
        pieces = [(blocks[0][2], 0, self.spans[0])]
        pieces += [(blocks[i][1], 0, self.spans[i]) for i in range(1, self.depth)]
        self.first = pack(pieces)
        got = partner(self.first, "sub", 1)
        self.received = got
        at = 0
        for level in range(self.depth):
            self.held[level][1] = (got, at)
            at += self.spans[level]

    def relay(self, level, stage, gate=None):
        if stage == level:
            offsets, value = [0], self.blocks[level][2]
            if gate is not None:
                value = after(value, gate)
        else:
            offsets = [i for i in self.held[level] if i % (2 << stage) == 0]
            if stage == 0:
                offsets = [i for i in offsets if i > 0]
            pieces = [(*self.held[level][i], self.spans[level]) for i in offsets]
            if gate is not None:
                pieces[-1] = (after(pieces[-1][0], gate), *pieces[-1][1:])
            if len(pieces) == 1 and pieces[0][0].shape[1] == pieces[0][2]:
                value = pieces[0][0]
            else:
                value = pack(pieces)
            if 0 not in offsets:
                for place, offset in enumerate(offsets):
                    self.held[level][offset] = (value, place * self.spans[level])
        got = partner(value, "sub", 1 << stage)
        for place, offset in enumerate(offsets):
            self.held[level][offset ^ (1 << stage)] = (got, place * self.spans[level])
        return value

    def exchange(self, level, gate):
        for offset, (array, _) in self.held[level].items():
            if offset > 0 and id(array) not in self.other:
                self.other[id(array)] = (array, partner(after(array, gate), "rep", 1))

    def head(self, left, right):
        return assemble_head(left, right, self.pieces(self.depth), self.ids)

    def weight(self, level):
        return assemble(self.blocks[level][0], self.pieces(level), self.ids)

    def pieces(self, level):
        pieces = {}
        for offset, (array, at) in self.held[level].items():
            if offset > 0:
                pieces[offset] = (array, self.other[id(array)][1], at)
        return pieces


class View:
    def __init__(self, array, rows=None, cols=None):
        self.array = array
        self.rows = (0, array.shape[0]) if rows is None else rows
        self.cols = (0, array.shape[1]) if cols is None else cols
        self.shape = (self.rows[1] - self.rows[0], self.cols[1] - self.cols[0])

    def value(self):
        return self.array[slice(*self.rows), slice(*self.cols)]

    def part(self, first, last):
        return View(self.array, (self.rows[0] + first, self.rows[0] + last), self.cols)

    def gated(self, *gates):
        return View(after(self.array, *gates), self.rows, self.cols)

    def aligned(self):
        edges = (*self.rows, *self.cols)
        return all(edge % unit == 0 for edge, unit in zip(edges, (16, 16, 128, 128)))


def spots_of(views):
    arrays, spots = [], []
    for view in views:
        known = [i for i, array in enumerate(arrays) if array is view.array]
        if not known:
            arrays.append(view.array)
            known = [len(arrays) - 1]
        spots.append((known[0], view.rows, view.cols))
    return arrays, spots


def join_all(pieces):
    if len(pieces) == 1:
        return pieces[0]
    if pieces[0].dtype == jnp.float32 or all(piece.shape[0] % 16 == 0 for piece in pieces):
        return jnp.concatenate(pieces, axis=0)
    wide = lax.optimization_barrier(tuple(f32(piece) for piece in pieces))
    return bf16(lax.optimization_barrier(jnp.concatenate(wide, axis=0)))


def step(body, name, args, parts=(), stacks=(), halves=(), fixed=(), level=0, far=None, **options):
    groups = [[view] for view in parts] + [list(group) for group in stacks]
    halved = [list(group) for group in (*halves, *fixed)]
    views = [view for group in (*groups, *halved, far or ()) for view in group]
    arrays = list(args)
    for view in views:
        if not any(array is view.array for array in arrays):
            arrays.append(view.array)

    def cut(values, group):
        pieces = []
        for view in group:
            index = next(i for i, array in enumerate(arrays) if array is view.array)
            pieces.append(values[index][slice(*view.rows), slice(*view.cols)])
        return join_all(pieces)

    def whole(ids, *values):
        given = [cut(values, group) for group in groups[: len(parts)]]
        results = list(body(*values[: len(args)], *given))
        results += [cut(values, group) for group in groups[len(parts) :]]
        sends = []
        for index, group in enumerate(halved):
            full = cut(values, group)
            half = full.shape[1] // 2
            low, high = full[:, :half], full[:, half:]
            if index < len(halves):
                own = bit_of(ids[0], level) == 1
                low, high = jnp.where(own, high, low), jnp.where(own, low, high)
            results.append(low)
            sends.append(high)
        if sends:
            results.append(jnp.concatenate(sends, axis=1))
        if far:
            full = cut(values, far)
            half = full.shape[1] // 2
            results.append(jnp.where(bit_of(ids[1], 1) == 1, full[:, :half], full[:, half:]))
        return results

    plain = not all(view.aligned() for view in views)
    return fused(whole, name, *arrays, plain=plain, **options)


def near_inputs_kernel(spots, ids_ref, first_ref, second_ref, *refs):
    out_ref = refs[-1]
    quarter = out_ref.shape[1]
    other = 1 - bit_of(ids_ref[1], 0)
    lanes = pl.ds(pl.multiple_of((bit_of(ids_ref[1], 1) * 2 + other) * quarter, quarter), quarter)
    at = 0
    for index, (first, last), _ in spots:
        out_ref[at : at + last - first] = refs[index][first:last, lanes]
        at += last - first
    for ref in (first_ref, second_ref):
        count = ref.shape[0]
        lanes = pl.ds(pl.multiple_of(other * quarter, quarter), quarter)
        out_ref[at : at + count] = ref[:, lanes]
        at += count


def near_inputs(views, got, ids):
    quarter = views[0].shape[1] // 4
    if not all(view.aligned() for view in views):
        full = join_all([view.value() for view in views])
        other = 1 - bit_of(ids[1], 0)
        where = (bit_of(ids[1], 1) * 2 + other) * quarter
        own = lax.dynamic_slice_in_dim(full, where, quarter, 1)
        far = jnp.concatenate(got, axis=0)
        return jnp.concatenate(
            [own, lax.dynamic_slice_in_dim(far, other * quarter, quarter, 1)], axis=0
        )
    arrays, spots = spots_of(views)
    return pl.pallas_call(
        functools.partial(near_inputs_kernel, spots),
        out_shape=jax.ShapeDtypeStruct(
            (2 * sum(array.shape[0] for array in got), quarter), jnp.bfloat16
        ),
        in_specs=[smem_block()] + [whole_block()] * (len(arrays) + 2),
        out_specs=whole_block(),
        compiler_params=pltpu.CompilerParams(vmem_limit_bytes=8 * MIB),
        name="near_inputs",
    )(ids, *got, *arrays)


def side_by_side_kernel(groups, *refs):
    out_ref = refs[-1]
    col = 0
    for spots in groups:
        at = 0
        for index, rows, cols in spots:
            span = cols[1] - cols[0]
            count = rows[1] - rows[0]
            out_ref[at : at + count, col : col + span] = refs[index][slice(*rows), slice(*cols)]
            at += count
        col += span


def side_by_side(groups):
    views = [view for group in groups for view in group]
    if not all(view.aligned() for view in views):
        return jnp.concatenate(
            [join_all([view.value() for view in group]) for group in groups], axis=1
        )
    arrays, spots = spots_of(views)
    by_group = [[spots.pop(0) for _ in group] for group in groups]
    shape = (
        sum(view.shape[0] for view in groups[0]),
        sum(group[0].shape[1] for group in groups),
    )
    return pl.pallas_call(
        functools.partial(side_by_side_kernel, by_group),
        out_shape=jax.ShapeDtypeStruct(shape, jnp.bfloat16),
        in_specs=[whole_block()] * len(arrays),
        out_specs=whole_block(),
        compiler_params=pltpu.CompilerParams(vmem_limit_bytes=6 * MIB),
        name="side_by_side",
    )(*arrays)


def upper_grads_kernel(spots, spans, rows, ids_ref, first_ref, second_ref, near_ref, *refs):
    grads, inputs, out_ref, both = refs[:4], refs[4:-2], refs[-2], refs[-1]
    quarter = out_ref.shape[0]
    core, far = bit_of(ids_ref[1], 0), bit_of(ids_ref[1], 1)
    lanes = pl.ds(pl.multiple_of((far * 2 + core) * quarter, quarter), quarter)
    far_lanes = pl.ds(pl.multiple_of(core * quarter, quarter), quarter)
    total = first_ref.shape[0] + second_ref.shape[0]
    col = 0
    for level, span in enumerate(spans):
        for turn in range(2):
            here, at = spots[level][turn]
            pieces = [inputs[i][slice(*edges), lanes] for i, edges, _ in here]
            if at < first_ref.shape[0]:
                pieces.append(first_ref[at : at + rows, far_lanes])
            else:
                there = at - first_ref.shape[0]
                pieces.append(second_ref[there : there + rows, far_lanes])
            pieces.append(near_ref[at : at + rows])
            pieces.append(near_ref[total + at : total + at + rows])
            grad = jnp.concatenate(
                [ref[turn * rows : (turn + 1) * rows, col : col + span] for ref in grads], axis=0
            )
            value = bf16(inner_t(jnp.concatenate(pieces, axis=0), grad))
            side = turn
            if level < len(spans) - 1:
                side = jnp.bitwise_xor(bit_of(ids_ref[0], level), turn)
            both[side, :, col : col + span] = value
        col += span
    out_ref[...] = jnp.swapaxes(both[...], 0, 1)


def upper_grads(entries, far_got, near_got, grads, ids):
    depth = len(entries) - 1
    width = entries[0][0][0].shape[1]
    rows = sum(view.shape[0] for view in entries[0][0])
    spans = [width >> (level + 1) for level in range(depth)] + [width >> depth]
    views = [view for entry in entries for turn in entry for view in turn]
    starts = [[0, rows]]
    starts += [[(2 * level + 1) * rows, (2 * level + 2) * rows] for level in range(1, depth)]
    starts.append([2 * rows, 2 * rows])
    if all(view.aligned() for view in views) and spans[-1] % 128 == 0:
        arrays, flat = spots_of(views)
        spots = [
            [([flat.pop(0) for _ in entry[turn]], starts[level][turn]) for turn in range(2)]
            for level, entry in enumerate(entries)
        ]
        return pl.pallas_call(
            functools.partial(upper_grads_kernel, spots, spans, rows),
            out_shape=jax.ShapeDtypeStruct((width // 4, 2, width), jnp.bfloat16),
            in_specs=[smem_block()] + [whole_block()] * (len(arrays) + 7),
            out_specs=whole_block(),
            scratch_shapes=[pltpu.VMEM((2, width // 4, width), jnp.bfloat16)],
            compiler_params=pltpu.CompilerParams(vmem_limit_bytes=16 * MIB),
            name="upper_grads",
        )(ids, *far_got, near_got, *grads, *arrays)
    quarter = width // 4
    core, far = bit_of(ids[1], 0), bit_of(ids[1], 1)
    far_got = jnp.concatenate(far_got, axis=0)
    total = far_got.shape[0]
    parts, col = [], 0
    for level, span in enumerate(spans):
        both = []
        for turn in range(2):
            at = starts[level][turn]
            own = join_all([view.value() for view in entries[level][turn]])
            pieces = [
                lax.dynamic_slice_in_dim(own, (far * 2 + core) * quarter, quarter, 1),
                lax.dynamic_slice_in_dim(far_got[at : at + rows], core * quarter, quarter, 1),
                near_got[at : at + rows],
                near_got[total + at : total + at + rows],
            ]
            grad = [part[turn * rows : (turn + 1) * rows, col : col + span] for part in grads]
            both.append(bf16(inner_t(jnp.concatenate(pieces), jnp.concatenate(grad))))
        if level < depth:
            swap = bit_of(ids[0], level) == 1
            both = [jnp.where(swap, both[1 - i], both[i]) for i in range(2)]
        parts.append(jnp.stack(both, axis=1))
        col += span
    return jnp.concatenate(parts, axis=2)


def mid_forward(term, near, far, weight):
    product = (1.0 + f32(term)) * (1.0 + f32(near)) * f32(far)
    return up_product(bf16(product * rms_factor(product)), weight)


def up_product(message, weight):
    up = matmul(message, weight)
    keep = up.shape[0] // 2
    return message, up[:keep], bf16(up[keep:])


def up_forward(own_up, other_up, weight):
    joined = (1.0 + own_up) * (1.0 + f32(other_up))
    return up_product(bf16(joined * rms_factor(joined)), weight)


def top_forward(own_up, other_up):
    joined = (1.0 + own_up) * (1.0 + f32(other_up))
    return (bf16(joined * rms_factor(joined)),)


def head_body(low, high, maps, *cotangents):
    root = join([low, high])
    cotangent = jnp.concatenate(cotangents, axis=1)
    half = maps.shape[1] // 2
    both = matmul(root, maps)
    value, gating = both[:, :half], jax.nn.sigmoid(both[:, half:])
    grad_value = bf16(cotangent * gating)
    grad_gate = bf16(cotangent * value * gating * (1.0 - gating))
    back = matmul_t(grad_value, maps[:, :half]) + matmul_t(grad_gate, maps[:, half:])
    rows = root.shape[0] // 2
    return root, grad_value, grad_gate, back[:rows], bf16(back[rows:])


def level_back(grad_msg, own_up, other_up):
    own_up, other_up = 1.0 + own_up, 1.0 + f32(other_up)
    joined = own_up * other_up
    scaling = rms_factor(joined)
    grad = norm_back(grad_msg, joined * scaling, scaling)
    return bf16(grad * other_up), bf16(grad * own_up)


def top_back(own_up, other_up, own_part, got):
    return level_back(own_part + f32(got), own_up, other_up)


def down_back(own_up, other_up, weight, low, high):
    return level_back(matmul_t(join([low, high]), weight), own_up, other_up)


def mid_back(term, near, far, weight, low, high):
    own, near, far = 1.0 + f32(term), 1.0 + f32(near), f32(far)
    pair = own * near
    product = pair * far
    scale = rms_factor(product)
    grad_msg = matmul_t(join([low, high]), weight)
    grad = norm_back(grad_msg, product * scale, scale)
    grad_pair = grad * far
    return bf16(grad_pair * near), bf16(grad_pair * own), bf16(grad * pair)


def far_back(grad_pair, term, near):
    grad_pair = f32(grad_pair)
    return bf16(grad_pair * (1.0 + f32(near))), bf16(grad_pair * (1.0 + f32(term)))


def pair_product(term, near):
    return (bf16((1.0 + f32(term)) * (1.0 + f32(near))),)


def on_device(regions, leaf_map, leaf_bond_weight, mid_weight, upper_weight, head_cotangent):
    rows = regions.shape[0]
    sub_count = lax.axis_size("sub")
    depth = sub_count.bit_length() - 1
    ids = jnp.stack([lax.axis_index("sub"), lax.axis_index("rep")]).astype(jnp.int32)
    leaf_w = leaf_bond_weight[0]
    mid_w = mid_weight[0, 0]

    blocks, (head_left, head_right, head_half) = cut_maps(upper_weight[0], ids, depth)
    gather = MapGather(blocks, head_half, ids)

    *sent, cotangent, cotangent_sent = place(after(regions, head_right), leaf_map, head_cotangent, ids, depth)
    near = partner(sent[1], "rep", 1)
    far_both = partner(sent[3], "rep", 3)
    far_one = partner(sent[2], "rep", 2)
    placed = [sent[0], near, far_one, far_both]
    for level in reversed(range(1, depth)):
        value = gather.relay(level, level, near)
    msg0, msg1, term0, term1 = leaf_forward(placed[:2], leaf_w, mid_w)
    near0 = partner(term1, "rep", 1)
    for level in range(2, depth):
        for stage in reversed(range(1, level)):
            value = gather.relay(level, stage, term1)
    far_placed = [after(far_one, term1, value), far_both]
    msg2, msg3, term2, term3 = leaf_forward(far_placed, leaf_w, mid_w)
    near2 = partner(term3, "rep", 1)
    gather.relay(1, 0, term3)
    for level in range(2, depth):
        value = gather.relay(level, 0, term1)
    gather.exchange(0, term3)
    gather.relay(depth, depth - 1, term1)
    (pair,) = fused(pair_product, "pair_product", term2, after(near2, value))
    far_pair = partner(pair, "rep", 2)
    gather.exchange(1, pair)

    cotangents = {0: View(cotangent)}
    for stage in reversed(range(1, depth)):
        if stage == depth - 1:
            value = after(cotangent_sent, pair)
        else:
            half = next(iter(cotangents.values())).shape[0] // 2
            (value,) = step(
                lambda: (),
                "stack",
                [],
                stacks=[[view.part(half, 2 * half) for view in cotangents.values()]],
                ids=ids,
            )
            cotangents = {key: view.part(0, half) for key, view in cotangents.items()}
        got = partner(value, "sub", 1 << stage)
        half = cotangents[0].shape[0]
        for place_at, key in enumerate(list(cotangents)):
            cotangents[key ^ (1 << stage)] = View(got, (place_at * half, (place_at + 1) * half))

    weights, messages, own_ups, other_ups = [], [], [], []
    for level in range(depth):
        if level == 1:
            for later in range(2, depth):
                gather.exchange(later, own_ups[0])
            weights += [gather.weight(later) for later in range(1, depth)]
            weights[1] = after(weights[1], weights[2])
        if level == 2:
            gather.exchange(depth, other_ups[1])
        if level == 0:
            weights.append(gather.weight(0))
            for stage in reversed(range(1, depth - 1)):
                far_pair = after(far_pair, gather.relay(depth, stage, weights[0]))
            outs = fused(mid_forward, "mid_forward", term0, near0, far_pair, weights[0])
        else:
            outs = fused(up_forward, "up_forward", own_ups[-1], other_ups[-1], weights[level])
        messages.append(outs[0])
        own_ups.append(outs[1])
        other_ups.append(partner(outs[2], "sub", 1 << level))
    (root,) = fused(top_forward, "top_forward", own_ups[-1], other_ups[-1])

    turns = [[[View(message)], []] for message in messages]

    def gather_turns(stage, value, levels):
        got = partner(value, "sub", 1 << stage)
        at = 0
        for level in levels:
            count = sum(view.shape[0] for view in turns[level][0])
            turns[level][0 if level > stage else 1].append(View(got, (at, at + count)))
            at += count
            if stage < level < depth:
                turns[level][1].append(View(got, (at, at + count)))
                at += count

    def to_stack(stage, levels):
        return [
            view
            for level in levels
            for view in turns[level][0] + (turns[level][1] if stage < level < depth else [])
        ]

    def stack_turns(stage, levels):
        (value,) = step(lambda: (), "stack", [], stacks=[to_stack(stage, levels)], ids=ids)
        gather_turns(stage, value, levels)

    gather_turns(0, after(messages[0], other_ups[0]), [0])
    for level in range(1, depth):
        gather_turns(level, after(messages[level], own_ups[level]), [level])
    for stage in reversed(range(2, depth - 1)):
        stack_turns(stage, range(stage + 1, depth))

    head_maps = gather.head(head_left, head_right)
    root_high = partner(root, "sub", 1)
    root, grad_value, grad_gate, grad_msg, give, value = step(
        head_body,
        "head",
        [after(root, turns[0][1][0].array), root_high, head_maps],
        parts=[cotangents[2 * i] for i in range(sub_count // 2)],
        stacks=[to_stack(1, range(2, depth))],
        ids=ids,
        limit=12,
    )
    got = partner(give, "sub", 1)
    gather_turns(1, value, range(2, depth))
    turns.append([[View(root)], []])
    gather_turns(depth - 1, root, [depth])
    low, high, value, root_value = step(
        top_back,
        "top_back",
        [own_ups[-1], other_ups[-1], grad_msg, got],
        stacks=[to_stack(0, range(1, depth)), to_stack(depth - 2, [depth])],
        ids=ids,
    )
    gather_turns(0, value, range(1, depth))
    gather_turns(depth - 2, root_value, [depth])
    for stage in reversed(range(1, depth - 2)):
        stack_turns(stage, [depth])
    turns[depth][1] = turns[depth][0]
    first_inputs = turns[0][0] + turns[0][1] + turns[depth][0]
    second_inputs = [view for entry in turns[1:depth] for turn in entry for view in turn]

    lows, highs = [None] * depth, [None] * depth
    lows[-1], highs[-1] = low, partner(high, "sub", 1 << (depth - 1))
    columns = [None] * depth + [[View(grad_value)], [View(grad_gate)]]

    def groups_of(stage):
        return [
            [View(lows[level]), View(highs[level])] if columns[level] is None else columns[level]
            for level in range(stage, depth)
        ]

    def spread(stage, keeps, send):
        got = partner(send, "sub", 1 << stage)
        at = 0
        for level, keep in zip(range(stage, depth + 2), keeps):
            span = keep.shape[1]
            columns[level] = [View(keep), View(got, None, (at, at + span))]
            at += span

    def columns_of(level, turn):
        if level == depth:
            return columns[depth + turn]
        if level == 0:
            return [columns[0][turn]]
        count = rows >> level
        return [
            view.part(i * count, (i + 1) * count)
            for view in columns[level]
            for i in range(turn, view.shape[0] // count, 2)
        ]

    far_got = []
    for level in reversed(range(depth - 1)):
        above = level + 1
        far = {depth - 2: first_inputs, 0: second_inputs}.get(level)
        low, high, *rest = step(
            down_back,
            "down_back",
            [own_ups[level], other_ups[level], weights[above], lows[above], highs[above]],
            halves=groups_of(above),
            fixed=columns[depth:],
            level=above,
            far=far,
            ids=ids,
            limit=12,
        )
        lows[level] = low
        highs[level] = partner(high, "sub", 1 << level)
        if far:
            far_got.append(partner(rest.pop(), "rep", 2))
        spread(above, rest[:-1], rest[-1])

    lows[0] = after(lows[0], far_got[0])
    back0, back1, pair_back, *rest = step(
        mid_back,
        "mid_back",
        [term0, near0, far_pair, weights[0], lows[0], highs[0]],
        halves=groups_of(0),
        level=0,
        ids=ids,
        limit=12,
    )
    back1 = partner(back1, "rep", 1)
    pair_back = partner(pair_back, "rep", 2)
    spread(0, rest[:-1], rest[-1])
    first = leaf_first(placed[:2], [back0, back1], leaf_w, mid_w)
    groups = [
        [view for turn in range(2) for view in columns_of(level, turn)]
        for level in range(depth + 1)
    ]
    groups[0][0] = groups[0][0].gated(first)
    own_grads = side_by_side(groups)
    far_grads = partner(own_grads, "rep", 2)
    near_grads = partner(own_grads, "rep", 1)
    back2, back3 = fused(far_back, "far_back", after(pair_back, own_grads), term2, near2)
    back3 = partner(back3, "rep", 1)
    inputs = first_inputs + second_inputs
    near_got = partner(near_inputs([inputs[0].gated(back2)] + inputs[1:], far_got, ids), "rep", 1)
    leaf_grad, mid_grad = leaf_backward(
        placed, [msg0, msg1, msg2, msg3], [back0, back1, back2, back3], leaf_w, mid_w, first
    )
    grads = [own_grads, far_grads, near_grads]
    grads.append(partner(after(far_grads, leaf_grad), "rep", 1))
    upper = upper_grads(turns, far_got, near_got, grads, ids)
    return leaf_grad[None], mid_grad[None, None], upper[None]


def solution(mesh):
    placed = (
        P("rep", "sub", None),
        P("sub"),
        P(("sub", "rep"), None, None, None),
        P("sub", "rep", None, None),
        P("sub", None, None, None),
        P("rep", "sub"),
    )
    return jax.shard_map(
        on_device,
        mesh=mesh,
        in_specs=placed,
        out_specs=(
            P(("sub", "rep"), None, None, None),
            P("sub", "rep", None, None),
            P("sub", "rep", None, None),
        ),
        check_vma=False,
    )
```

```python
import functools

import jax
import jax.numpy as jnp
from jax import lax
from jax.experimental import pallas as pl
from jax.experimental.pallas import tpu as pltpu
from jax.sharding import PartitionSpec as P

EPSILON = 1e-06
CHILDREN = 4
MIB = 1024 * 1024


def partner(value, axis, offset):
    return lax.ppermute(value, axis, [(i, i ^ offset) for i in range(lax.axis_size(axis))])


def rms_factor(values):
    return lax.rsqrt(jnp.mean(values * values, axis=-1, keepdims=True) + EPSILON)


def norm_back(gradient, normed, factor):
    return factor * (gradient - normed * jnp.mean(gradient * normed, axis=-1, keepdims=True))


def matmul(left_arr, right_arr):
    return jnp.dot(left_arr, right_arr, preferred_element_type=jnp.float32)


def matmul_t(left_arr, right_arr):
    return lax.dot_general(
        left_arr, right_arr, (((1,), (1,)), ((), ())), preferred_element_type=jnp.float32
    )


def inner_t(left_arr, right_arr):
    return lax.dot_general(
        left_arr, right_arr, (((0,), (0,)), ((), ())), preferred_element_type=jnp.float32
    )


def bf16(value):
    return value.astype(jnp.bfloat16)


def f32(value):
    return value.astype(jnp.float32)


def whole_block():
    return pl.BlockSpec(memory_space=pltpu.VMEM)


def smem_block():
    return pl.BlockSpec(memory_space=pltpu.SMEM)


def bit_of(value, level):
    return jnp.bitwise_and(jnp.right_shift(value, level), 1)


def place_kernel(slots, depth, ids_ref, map_ref, regions_ref, cotangent_ref, *rest):
    outs, keep_ref, send_ref, wide = rest[:CHILDREN], *rest[CHILDREN:]
    rows = regions_ref.shape[0] // slots
    parts = wide.shape[0]
    for part in range(parts):
        wide[part] = regions_ref[:, part * 128 : (part + 1) * 128].astype(jnp.float32)
    flip = 0
    for level in range(depth):
        flip = flip + bit_of(ids_ref[0], level) * (rows >> (level + 1))
    row = lax.broadcasted_iota(jnp.int32, (rows, rows), 0)
    col = lax.broadcasted_iota(jnp.int32, (rows, rows), 1)
    select = bf16(jnp.bitwise_xor(row, flip) == col)
    block = rows >> depth
    wanted = jnp.bitwise_and(row, block - 1)
    for level in range(depth):
        wanted = wanted + bit_of(row // block, level) * (block << (depth - 1 - level))
    pick = bf16(jnp.bitwise_xor(wanted, flip) == col)
    left = cotangent_ref[...]
    picked = 0.0
    for _ in range(3):
        top = bf16(left)
        left = left - f32(top)
        picked = picked + matmul(pick, top)
    keep_ref[...] = picked[: rows // 2]
    send_ref[...] = picked[rows // 2 :]
    for offset in range(CHILDREN):
        node = jnp.bitwise_xor(ids_ref[1], offset)
        for child in range(CHILDREN):
            region = map_ref[node * CHILDREN + child]
            for part in range(parts):
                values = bf16(wide[part, pl.ds(region, rows, stride=slots), :])
                outs[offset][child, :, part * 128 : (part + 1) * 128] = bf16(
                    matmul(select, values)
                )


def place(regions, leaf_map, cotangent, ids, depth):
    rows, slots, feats = regions.shape
    flat = regions.reshape(rows * slots, feats)
    return pl.pallas_call(
        functools.partial(place_kernel, slots, depth),
        out_shape=[jax.ShapeDtypeStruct((CHILDREN, rows, feats), jnp.bfloat16)] * CHILDREN
        + [jax.ShapeDtypeStruct((rows // 2, cotangent.shape[1]), cotangent.dtype)] * 2,
        in_specs=[smem_block(), smem_block(), whole_block(), whole_block()],
        out_specs=[whole_block()] * (CHILDREN + 2),
        scratch_shapes=[pltpu.VMEM((feats // 128, rows * slots, 128), jnp.float32)],
        compiler_params=pltpu.CompilerParams(vmem_limit_bytes=7 * MIB),
        name="place",
    )(ids, leaf_map, flat, cotangent)


def leaf_forward_kernel(count, *refs):
    placed, leaf_w, mid_w = refs[:count], refs[count], refs[count + 1]
    msgs, terms = refs[count + 2 : 2 * count + 2], refs[2 * count + 2 :]
    rows = placed[0].shape[1]
    product = None
    for child in range(CHILDREN):
        values = jnp.concatenate([ref[child] for ref in placed], axis=0)
        factor = 1.0 + matmul(values, leaf_w[child])
        product = factor if product is None else product * factor
    message = bf16(product * rms_factor(product))
    out = bf16(matmul(message, mid_w[...]))
    for i in range(count):
        msgs[i][...] = message[i * rows : (i + 1) * rows]
        terms[i][...] = out[i * rows : (i + 1) * rows]


def leaf_forward(placed, leaf_w, mid_w):
    count = len(placed)
    rows = placed[0].shape[1]
    width = mid_w.shape[0]
    return pl.pallas_call(
        functools.partial(leaf_forward_kernel, count),
        out_shape=[jax.ShapeDtypeStruct((rows, width), jnp.bfloat16)] * (2 * count),
        in_specs=[whole_block()] * (count + 2),
        out_specs=[whole_block()] * (2 * count),
        compiler_params=pltpu.CompilerParams(vmem_limit_bytes=14 * MIB),
        name="leaf_forward",
    )(*placed, leaf_w, mid_w)


def leaf_cotangents(placed, grads, leaf_w, mid_w):
    factors = [
        1.0 + matmul(jnp.concatenate([ref[child] for ref in placed], axis=0), leaf_w[child])
        for child in range(CHILDREN)
    ]
    low = factors[0] * factors[1]
    high = factors[2] * factors[3]
    product = low * high
    scale = rms_factor(product)
    back = matmul_t(jnp.concatenate([ref[...] for ref in grads], axis=0), mid_w[...])
    node = norm_back(back, product * scale, scale)
    high, low = node * high, node * low
    return [
        bf16(high * factors[1]),
        bf16(high * factors[0]),
        bf16(low * factors[3]),
        bf16(low * factors[2]),
    ]


def leaf_first_kernel(*refs):
    placed, grads, leaf_w, mid_w, out = refs[0:2], refs[2:4], refs[4], refs[5], refs[6]
    for child, value in enumerate(leaf_cotangents(placed, grads, leaf_w, mid_w)):
        out[child] = value


def leaf_first(placed, grads, leaf_w, mid_w):
    rows = placed[0].shape[1]
    return pl.pallas_call(
        leaf_first_kernel,
        out_shape=jax.ShapeDtypeStruct((CHILDREN, 2 * rows, mid_w.shape[0]), jnp.bfloat16),
        in_specs=[whole_block()] * 6,
        out_specs=whole_block(),
        compiler_params=pltpu.CompilerParams(vmem_limit_bytes=18 * MIB),
        name="leaf_first",
    )(*placed, *grads, leaf_w, mid_w)


def leaf_backward_kernel(*refs):
    placed, msgs, grads = refs[0:4], refs[4:8], refs[8:12]
    leaf_w, mid_w, first, leaf_out, mid_out = refs[12:17]
    all_grads = jnp.concatenate([ref[...] for ref in grads], axis=0)
    all_msgs = jnp.concatenate([ref[...] for ref in msgs], axis=0)
    mid_out[...] = bf16(inner_t(all_msgs, all_grads))
    second = leaf_cotangents(placed[2:], grads[2:], leaf_w, mid_w)
    for child in range(CHILDREN):
        values = jnp.concatenate([ref[child] for ref in placed], axis=0)
        cot = jnp.concatenate([first[child], second[child]], axis=0)
        leaf_out[child] = bf16(inner_t(values, cot))


def leaf_backward(placed, msgs, grads, leaf_w, mid_w, first):
    return pl.pallas_call(
        leaf_backward_kernel,
        out_shape=[
            jax.ShapeDtypeStruct(leaf_w.shape, jnp.bfloat16),
            jax.ShapeDtypeStruct(mid_w.shape, jnp.bfloat16),
        ],
        in_specs=[whole_block()] * 15,
        out_specs=[whole_block()] * 2,
        compiler_params=pltpu.CompilerParams(vmem_limit_bytes=30 * MIB),
        name="leaf_backward",
    )(*placed, *msgs, *grads, leaf_w, mid_w, first)


def fused(body, name, *args, limit=8, ids=None, plain=False):
    if plain or any(arg.shape[-2] % 16 or arg.shape[-1] % 128 for arg in args):
        return body(*args) if ids is None else body(ids, *args)
    count = len(args)
    if ids is None:
        shapes = jax.eval_shape(body, *args)
    else:
        shapes = jax.eval_shape(body, ids, *args)
        args = (ids, *args)

    def kernel(*refs):
        outs = refs[len(args) :]
        values = [ref[...] for ref in refs[len(args) - count : len(args)]]
        results = body(*values) if ids is None else body(refs[0], *values)
        for ref, result in zip(outs, results):
            ref[...] = result

    return pl.pallas_call(
        kernel,
        out_shape=shapes,
        in_specs=[smem_block()] * (len(args) - count) + [whole_block()] * count,
        out_specs=[whole_block()] * len(shapes),
        compiler_params=pltpu.CompilerParams(vmem_limit_bytes=limit * MIB),
        name=name,
    )(*args)


def join(pieces):
    if pieces[0].shape[0] % 16 == 0:
        return jnp.concatenate(pieces, axis=0)
    wide = lax.optimization_barrier(tuple(f32(piece) for piece in pieces))
    return bf16(lax.optimization_barrier(jnp.concatenate(wide, axis=0)))


def pack(pieces):
    arrays = []
    for array, _, _ in pieces:
        if not any(array is known for known in arrays):
            arrays.append(array)
    spots = [next(i for i, known in enumerate(arrays) if known is piece[0]) for piece in pieces]

    def body(*values):
        parts = [values[i][:, at : at + span] for i, (_, at, span) in zip(spots, pieces)]
        return (jnp.concatenate(parts, axis=1),)

    if any(piece[2] % 128 for piece in pieces):
        return body(*arrays)[0]
    return fused(body, "pack", *arrays, limit=6)[0]


def cut_kernel(depth, ids_ref, maps_ref, *refs):
    outs, split = refs[:-1], refs[-1]
    split[...] = jnp.swapaxes(maps_ref[...], 0, 1)
    width = maps_ref.shape[0]
    half = width // 2
    rows = pl.ds(pl.multiple_of(bit_of(ids_ref[1], 0) * half, half), half)
    for level in range(depth):
        span = width >> (level + 1)
        cols = pl.ds(width - 2 * span, span)
        side = bit_of(ids_ref[0], level)
        outs[3 * level][...] = split[side, :, cols]
        outs[3 * level + 1][...] = split[side, rows, cols]
        outs[3 * level + 2][...] = split[1 - side, rows, cols]
    span = width >> depth
    for side in range(2):
        outs[3 * depth + side][...] = split[side, :, width - span :]
        outs[3 * depth + 2][:, side * span : (side + 1) * span] = split[side, rows, width - span :]


def cut_maps(maps, ids, depth):
    width = maps.shape[0]
    half = width // 2
    spans = [width >> (level + 1) for level in range(depth)]
    if spans[-1] % 128 == 0:
        shapes = []
        for span in spans:
            shapes += [(width, span), (half, span), (half, span)]
        shapes += [(width, spans[-1])] * 2 + [(half, 2 * spans[-1])]
        outs = pl.pallas_call(
            functools.partial(cut_kernel, depth),
            out_shape=[jax.ShapeDtypeStruct(shape, maps.dtype) for shape in shapes],
            in_specs=[smem_block(), whole_block()],
            out_specs=[whole_block()] * len(shapes),
            scratch_shapes=[pltpu.VMEM((2, width, width), maps.dtype)],
            compiler_params=pltpu.CompilerParams(vmem_limit_bytes=18 * MIB),
            name="cut_maps",
        )(ids, maps)
    else:
        maps = jnp.transpose(maps, (1, 0, 2))
        outs = []
        core = bit_of(ids[1], 0)
        for level, span in enumerate(spans):
            side = bit_of(ids[0], level)
            first = width - 2 * span
            outs.append(lax.dynamic_slice(maps, (side, 0, first), (1, width, span))[0])
            for which in (side, 1 - side):
                outs.append(lax.dynamic_slice(maps, (which, core * half, first), (1, half, span))[0])
        outs += [maps[0, :, width - spans[-1] :], maps[1, :, width - spans[-1] :]]
        both = jnp.concatenate(outs[-2:], axis=1)
        outs.append(lax.dynamic_slice_in_dim(both, core * half, half, 0))
    return [outs[3 * i : 3 * i + 3] for i in range(depth)], outs[3 * depth :]


def assemble_kernel(spots, count, ids_ref, own_ref, *refs):
    out_ref = refs[-1]
    width, span = own_ref.shape
    half = width // 2
    block = jnp.bitwise_and(ids_ref[0], out_ref.shape[1] // span - 1)
    own_core = bit_of(ids_ref[1], 0)
    out_ref[:, pl.ds(pl.multiple_of(block * span, span), span)] = own_ref[...]
    for offset, index, at in spots:
        col = jnp.bitwise_xor(block, offset) * span
        for ref, core in ((refs[index], own_core), (refs[count + index], 1 - own_core)):
            out_ref[
                pl.ds(pl.multiple_of(core * half, half), half),
                pl.ds(pl.multiple_of(col, span), span),
            ] = ref[:, at : at + span]


def assemble(own, pieces, ids):
    width, span = own.shape
    count = len(pieces) + 1
    if span % 128 == 0:
        mine, other, spots = [], [], []
        for offset, (near_half, far_half, at) in pieces.items():
            known = [i for i, array in enumerate(mine) if array is near_half]
            if not known:
                mine.append(near_half)
                other.append(far_half)
                known = [len(mine) - 1]
            spots.append((offset, known[0], at))
        return pl.pallas_call(
            functools.partial(assemble_kernel, spots, len(mine)),
            out_shape=jax.ShapeDtypeStruct((width, span * count), own.dtype),
            in_specs=[smem_block()] + [whole_block()] * (2 * len(mine) + 1),
            out_specs=whole_block(),
            compiler_params=pltpu.CompilerParams(vmem_limit_bytes=8 * MIB),
            name="assemble",
        )(ids, own, *mine, *other)
    block = jnp.bitwise_and(ids[0], count - 1)
    core = bit_of(ids[1], 0)
    out = jnp.zeros((width, span * count), own.dtype)
    out = lax.dynamic_update_slice(out, own, (0, block * span))
    for offset, (near_half, far_half, at) in pieces.items():
        col = (block ^ offset) * span
        for array, which in ((near_half, core), (far_half, 1 - core)):
            part = array[:, at : at + span]
            out = lax.dynamic_update_slice(out, part, (which * (width // 2), col))
    return out


def assemble_head_kernel(spots, count, ids_ref, left_ref, right_ref, *refs):
    out_ref = refs[-1]
    width, span = left_ref.shape
    half, total = width // 2, out_ref.shape[1] // 2
    out_ref[:, :span] = left_ref[...]
    out_ref[:, total : total + span] = right_ref[...]
    own_core = bit_of(ids_ref[1], 0)
    for offset, index, at in spots:
        for ref, core in ((refs[index], own_core), (refs[count + index], 1 - own_core)):
            rows = pl.ds(pl.multiple_of(core * half, half), half)
            for side in range(2):
                col = side * total + (offset // 2) * span
                out_ref[rows, col : col + span] = ref[:, at + side * span : at + (side + 1) * span]


def assemble_head(left, right, pieces, ids):
    width, span = left.shape
    total = span * (len(pieces) + 1)
    mine, other, spots = [], [], []
    for offset, (near_half, far_half, at) in pieces.items():
        known = [i for i, array in enumerate(mine) if array is near_half]
        if not known:
            mine.append(near_half)
            other.append(far_half)
            known = [len(mine) - 1]
        spots.append((offset, known[0], at))
    if span % 128 == 0:
        return pl.pallas_call(
            functools.partial(assemble_head_kernel, spots, len(mine)),
            out_shape=jax.ShapeDtypeStruct((width, 2 * total), left.dtype),
            in_specs=[smem_block()] + [whole_block()] * (2 * len(mine) + 2),
            out_specs=whole_block(),
            compiler_params=pltpu.CompilerParams(vmem_limit_bytes=8 * MIB),
            name="assemble_head",
        )(ids, left, right, *mine, *other)
    core = bit_of(ids[1], 0)
    out = jnp.zeros((width, 2 * total), left.dtype)
    out = lax.dynamic_update_slice(out, left, (0, 0))
    out = lax.dynamic_update_slice(out, right, (0, total))
    for offset, index, at in spots:
        for array, which in ((mine[index], core), (other[index], 1 - core)):
            for side in range(2):
                part = array[:, at + side * span : at + (side + 1) * span]
                col = side * total + (offset // 2) * span
                out = lax.dynamic_update_slice(out, part, (which * (width // 2), col))
    return out


def after(value, *others):
    return lax.optimization_barrier((value, *others))[0]


class MapGather:
    def __init__(self, blocks, head_half, ids):
        self.blocks, self.ids = blocks + [(None, head_half, None)], ids
        self.depth = len(blocks)
        blocks = self.blocks
        self.spans = [block[1].shape[1] for block in blocks]
        self.held = [{0: (block[1], 0)} for block in blocks]
        self.other = {}
        pieces = [(blocks[0][2], 0, self.spans[0])]
        pieces += [(blocks[i][1], 0, self.spans[i]) for i in range(1, self.depth)]
        self.first = pack(pieces)
        got = partner(self.first, "sub", 1)
        self.received = got
        at = 0
        for level in range(self.depth):
            self.held[level][1] = (got, at)
            at += self.spans[level]

    def relay(self, level, stage, gate=None):
        if stage == level:
            offsets, value = [0], self.blocks[level][2]
            if gate is not None:
                value = after(value, gate)
        else:
            offsets = [i for i in self.held[level] if i % (2 << stage) == 0]
            if stage == 0:
                offsets = [i for i in offsets if i > 0]
            pieces = [(*self.held[level][i], self.spans[level]) for i in offsets]
            if gate is not None:
                pieces[-1] = (after(pieces[-1][0], gate), *pieces[-1][1:])
            if len(pieces) == 1 and pieces[0][0].shape[1] == pieces[0][2]:
                value = pieces[0][0]
            else:
                value = pack(pieces)
            if 0 not in offsets:
                for place, offset in enumerate(offsets):
                    self.held[level][offset] = (value, place * self.spans[level])
        got = partner(value, "sub", 1 << stage)
        for place, offset in enumerate(offsets):
            self.held[level][offset ^ (1 << stage)] = (got, place * self.spans[level])
        return value

    def top_relay(self, gate):
        level, stage = self.depth - 1, self.depth - 1
        pieces = [
            (after(self.blocks[level][2], gate), 0, self.spans[level]),
            (self.blocks[self.depth][1], 0, self.spans[self.depth]),
        ]
        got = partner(pack(pieces), "sub", 1 << stage)
        self.held[level][1 << stage] = (got, 0)
        self.held[self.depth][1 << stage] = (got, self.spans[level])

    def exchange(self, level, gate):
        for offset, (array, _) in self.held[level].items():
            if offset > 0 and id(array) not in self.other:
                self.other[id(array)] = (array, partner(after(array, gate), "rep", 1))

    def head(self, left, right):
        return assemble_head(left, right, self.pieces(self.depth), self.ids)

    def weight(self, level):
        return assemble(self.blocks[level][0], self.pieces(level), self.ids)

    def pieces(self, level):
        pieces = {}
        for offset, (array, at) in self.held[level].items():
            if offset > 0:
                pieces[offset] = (array, self.other[id(array)][1], at)
        return pieces


class View:
    def __init__(self, array, rows=None, cols=None):
        self.array = array
        self.rows = (0, array.shape[0]) if rows is None else rows
        self.cols = (0, array.shape[1]) if cols is None else cols
        self.shape = (self.rows[1] - self.rows[0], self.cols[1] - self.cols[0])

    def value(self):
        return self.array[slice(*self.rows), slice(*self.cols)]

    def part(self, first, last):
        return View(self.array, (self.rows[0] + first, self.rows[0] + last), self.cols)

    def gated(self, *gates):
        return View(after(self.array, *gates), self.rows, self.cols)

    def aligned(self):
        edges = (*self.rows, *self.cols)
        return all(edge % unit == 0 for edge, unit in zip(edges, (16, 16, 128, 128)))


def spots_of(views):
    arrays, spots = [], []
    for view in views:
        known = [i for i, array in enumerate(arrays) if array is view.array]
        if not known:
            arrays.append(view.array)
            known = [len(arrays) - 1]
        spots.append((known[0], view.rows, view.cols))
    return arrays, spots


def join_all(pieces):
    if len(pieces) == 1:
        return pieces[0]
    if pieces[0].dtype == jnp.float32 or all(piece.shape[0] % 16 == 0 for piece in pieces):
        return jnp.concatenate(pieces, axis=0)
    wide = lax.optimization_barrier(tuple(f32(piece) for piece in pieces))
    return bf16(lax.optimization_barrier(jnp.concatenate(wide, axis=0)))


def step(body, name, args, parts=(), stacks=(), halves=(), fixed=(), level=0, far=None, **options):
    groups = [[view] for view in parts] + [list(group) for group in stacks]
    halved = [list(group) for group in (*halves, *fixed)]
    views = [view for group in (*groups, *halved, far or ()) for view in group]
    arrays = list(args)
    for view in views:
        if not any(array is view.array for array in arrays):
            arrays.append(view.array)

    def cut(values, group):
        pieces = []
        for view in group:
            index = next(i for i, array in enumerate(arrays) if array is view.array)
            pieces.append(values[index][slice(*view.rows), slice(*view.cols)])
        return join_all(pieces)

    def whole(ids, *values):
        given = [cut(values, group) for group in groups[: len(parts)]]
        results = list(body(*values[: len(args)], *given))
        results += [cut(values, group) for group in groups[len(parts) :]]
        sends = []
        for index, group in enumerate(halved):
            full = cut(values, group)
            half = full.shape[1] // 2
            low, high = full[:, :half], full[:, half:]
            if index < len(halves):
                own = bit_of(ids[0], level) == 1
                low, high = jnp.where(own, high, low), jnp.where(own, low, high)
            results.append(low)
            sends.append(high)
        if sends:
            results.append(jnp.concatenate(sends, axis=1))
        if far:
            full = cut(values, far)
            half = full.shape[1] // 2
            results.append(jnp.where(bit_of(ids[1], 1) == 1, full[:, :half], full[:, half:]))
        return results

    plain = not all(view.aligned() for view in views)
    return fused(whole, name, *arrays, plain=plain, **options)


def near_inputs_kernel(spots, ids_ref, first_ref, second_ref, *refs):
    out_ref = refs[-1]
    quarter = out_ref.shape[1]
    other = 1 - bit_of(ids_ref[1], 0)
    lanes = pl.ds(pl.multiple_of((bit_of(ids_ref[1], 1) * 2 + other) * quarter, quarter), quarter)
    at = 0
    for index, (first, last), _ in spots:
        out_ref[at : at + last - first] = refs[index][first:last, lanes]
        at += last - first
    for ref in (first_ref, second_ref):
        count = ref.shape[0]
        lanes = pl.ds(pl.multiple_of(other * quarter, quarter), quarter)
        out_ref[at : at + count] = ref[:, lanes]
        at += count


def near_inputs(views, got, ids):
    quarter = views[0].shape[1] // 4
    if not all(view.aligned() for view in views):
        full = join_all([view.value() for view in views])
        other = 1 - bit_of(ids[1], 0)
        where = (bit_of(ids[1], 1) * 2 + other) * quarter
        own = lax.dynamic_slice_in_dim(full, where, quarter, 1)
        far = jnp.concatenate(got, axis=0)
        return jnp.concatenate(
            [own, lax.dynamic_slice_in_dim(far, other * quarter, quarter, 1)], axis=0
        )
    arrays, spots = spots_of(views)
    return pl.pallas_call(
        functools.partial(near_inputs_kernel, spots),
        out_shape=jax.ShapeDtypeStruct(
            (2 * sum(array.shape[0] for array in got), quarter), jnp.bfloat16
        ),
        in_specs=[smem_block()] + [whole_block()] * (len(arrays) + 2),
        out_specs=whole_block(),
        compiler_params=pltpu.CompilerParams(vmem_limit_bytes=8 * MIB),
        name="near_inputs",
    )(ids, *got, *arrays)


def side_by_side_kernel(groups, *refs):
    out_ref = refs[-1]
    col = 0
    for spots in groups:
        at = 0
        for index, rows, cols in spots:
            span = cols[1] - cols[0]
            count = rows[1] - rows[0]
            out_ref[at : at + count, col : col + span] = refs[index][slice(*rows), slice(*cols)]
            at += count
        col += span


def side_by_side(groups):
    views = [view for group in groups for view in group]
    if not all(view.aligned() for view in views):
        return jnp.concatenate(
            [join_all([view.value() for view in group]) for group in groups], axis=1
        )
    arrays, spots = spots_of(views)
    by_group = [[spots.pop(0) for _ in group] for group in groups]
    shape = (
        sum(view.shape[0] for view in groups[0]),
        sum(group[0].shape[1] for group in groups),
    )
    return pl.pallas_call(
        functools.partial(side_by_side_kernel, by_group),
        out_shape=jax.ShapeDtypeStruct(shape, jnp.bfloat16),
        in_specs=[whole_block()] * len(arrays),
        out_specs=whole_block(),
        compiler_params=pltpu.CompilerParams(vmem_limit_bytes=6 * MIB),
        name="side_by_side",
    )(*arrays)


def upper_grads_kernel(spots, spans, rows, ids_ref, first_ref, second_ref, near_ref, *refs):
    grads, inputs, out_ref, both = refs[:4], refs[4:-2], refs[-2], refs[-1]
    quarter = out_ref.shape[0]
    core, far = bit_of(ids_ref[1], 0), bit_of(ids_ref[1], 1)
    lanes = pl.ds(pl.multiple_of((far * 2 + core) * quarter, quarter), quarter)
    far_lanes = pl.ds(pl.multiple_of(core * quarter, quarter), quarter)
    total = first_ref.shape[0] + second_ref.shape[0]
    col = 0
    for level, span in enumerate(spans):
        for turn in range(2):
            here, at = spots[level][turn]
            pieces = [inputs[i][slice(*edges), lanes] for i, edges, _ in here]
            if at < first_ref.shape[0]:
                pieces.append(first_ref[at : at + rows, far_lanes])
            else:
                there = at - first_ref.shape[0]
                pieces.append(second_ref[there : there + rows, far_lanes])
            pieces.append(near_ref[at : at + rows])
            pieces.append(near_ref[total + at : total + at + rows])
            grad = jnp.concatenate(
                [ref[turn * rows : (turn + 1) * rows, col : col + span] for ref in grads], axis=0
            )
            value = bf16(inner_t(jnp.concatenate(pieces, axis=0), grad))
            side = turn
            if level < len(spans) - 1:
                side = jnp.bitwise_xor(bit_of(ids_ref[0], level), turn)
            both[side, :, col : col + span] = value
        col += span
    out_ref[...] = jnp.swapaxes(both[...], 0, 1)


def upper_grads(entries, far_got, near_got, grads, ids):
    depth = len(entries) - 1
    width = entries[0][0][0].shape[1]
    rows = sum(view.shape[0] for view in entries[0][0])
    spans = [width >> (level + 1) for level in range(depth)] + [width >> depth]
    views = [view for entry in entries for turn in entry for view in turn]
    starts = [[0, rows]]
    starts += [[(2 * level + 1) * rows, (2 * level + 2) * rows] for level in range(1, depth)]
    starts.append([2 * rows, 2 * rows])
    if all(view.aligned() for view in views) and spans[-1] % 128 == 0:
        arrays, flat = spots_of(views)
        spots = [
            [([flat.pop(0) for _ in entry[turn]], starts[level][turn]) for turn in range(2)]
            for level, entry in enumerate(entries)
        ]
        return pl.pallas_call(
            functools.partial(upper_grads_kernel, spots, spans, rows),
            out_shape=jax.ShapeDtypeStruct((width // 4, 2, width), jnp.bfloat16),
            in_specs=[smem_block()] + [whole_block()] * (len(arrays) + 7),
            out_specs=whole_block(),
            scratch_shapes=[pltpu.VMEM((2, width // 4, width), jnp.bfloat16)],
            compiler_params=pltpu.CompilerParams(vmem_limit_bytes=16 * MIB),
            name="upper_grads",
        )(ids, *far_got, near_got, *grads, *arrays)
    quarter = width // 4
    core, far = bit_of(ids[1], 0), bit_of(ids[1], 1)
    far_got = jnp.concatenate(far_got, axis=0)
    total = far_got.shape[0]
    parts, col = [], 0
    for level, span in enumerate(spans):
        both = []
        for turn in range(2):
            at = starts[level][turn]
            own = join_all([view.value() for view in entries[level][turn]])
            pieces = [
                lax.dynamic_slice_in_dim(own, (far * 2 + core) * quarter, quarter, 1),
                lax.dynamic_slice_in_dim(far_got[at : at + rows], core * quarter, quarter, 1),
                near_got[at : at + rows],
                near_got[total + at : total + at + rows],
            ]
            grad = [part[turn * rows : (turn + 1) * rows, col : col + span] for part in grads]
            both.append(bf16(inner_t(jnp.concatenate(pieces), jnp.concatenate(grad))))
        if level < depth:
            swap = bit_of(ids[0], level) == 1
            both = [jnp.where(swap, both[1 - i], both[i]) for i in range(2)]
        parts.append(jnp.stack(both, axis=1))
        col += span
    return jnp.concatenate(parts, axis=2)


def mid_forward(term, near, far, weight):
    product = (1.0 + f32(term)) * (1.0 + f32(near)) * f32(far)
    return up_product(bf16(product * rms_factor(product)), weight)


def up_product(message, weight):
    up = matmul(message, weight)
    keep = up.shape[0] // 2
    return message, up[:keep], bf16(up[keep:])


def up_forward(own_up, other_up, weight):
    joined = (1.0 + own_up) * (1.0 + f32(other_up))
    return up_product(bf16(joined * rms_factor(joined)), weight)


def top_forward(own_up, other_up):
    joined = (1.0 + own_up) * (1.0 + f32(other_up))
    return (bf16(joined * rms_factor(joined)),)


def head_body(low, high, maps, *cotangents):
    root = join([low, high])
    cotangent = jnp.concatenate(cotangents, axis=1)
    half = maps.shape[1] // 2
    both = matmul(root, maps)
    value, gating = both[:, :half], jax.nn.sigmoid(both[:, half:])
    grad_value = bf16(cotangent * gating)
    grad_gate = bf16(cotangent * value * gating * (1.0 - gating))
    back = matmul_t(grad_value, maps[:, :half]) + matmul_t(grad_gate, maps[:, half:])
    rows = root.shape[0] // 2
    return root, grad_value, grad_gate, back[:rows], bf16(back[rows:])


def level_back(grad_msg, own_up, other_up):
    own_up, other_up = 1.0 + own_up, 1.0 + f32(other_up)
    joined = own_up * other_up
    scaling = rms_factor(joined)
    grad = norm_back(grad_msg, joined * scaling, scaling)
    return bf16(grad * other_up), bf16(grad * own_up)


def top_back(own_up, other_up, own_part, got):
    return level_back(own_part + f32(got), own_up, other_up)


def down_back(own_up, other_up, weight, low, high):
    return level_back(matmul_t(join([low, high]), weight), own_up, other_up)


def mid_back(term, near, far, weight, low, high):
    own, near, far = 1.0 + f32(term), 1.0 + f32(near), f32(far)
    pair = own * near
    product = pair * far
    scale = rms_factor(product)
    grad_msg = matmul_t(join([low, high]), weight)
    grad = norm_back(grad_msg, product * scale, scale)
    grad_pair = grad * far
    return bf16(grad_pair * near), bf16(grad_pair * own), bf16(grad * pair)


def far_back(grad_pair, term, near):
    grad_pair = f32(grad_pair)
    return bf16(grad_pair * (1.0 + f32(near))), bf16(grad_pair * (1.0 + f32(term)))


def pair_product(term, near):
    return (bf16((1.0 + f32(term)) * (1.0 + f32(near))),)


def on_device(regions, leaf_map, leaf_bond_weight, mid_weight, upper_weight, head_cotangent):
    rows = regions.shape[0]
    sub_count = lax.axis_size("sub")
    depth = sub_count.bit_length() - 1
    ids = jnp.stack([lax.axis_index("sub"), lax.axis_index("rep")]).astype(jnp.int32)
    leaf_w = leaf_bond_weight[0]
    mid_w = mid_weight[0, 0]

    blocks, (head_left, head_right, head_half) = cut_maps(upper_weight[0], ids, depth)
    gather = MapGather(blocks, head_half, ids)

    *sent, cotangent, cotangent_sent = place(after(regions, head_right), leaf_map, head_cotangent, ids, depth)
    near = partner(sent[1], "rep", 1)
    far_both = partner(sent[3], "rep", 3)
    far_one = partner(sent[2], "rep", 2)
    placed = [sent[0], near, far_one, far_both]
    gather.top_relay(near)
    for level in reversed(range(1, depth - 1)):
        gather.relay(level, level, near)
    msg0, msg1, term0, term1 = leaf_forward(placed[:2], leaf_w, mid_w)
    near0 = partner(term1, "rep", 1)
    packed = []
    for level in range(2, depth):
        packed += [gather.relay(level, stage, term1) for stage in reversed(range(1, level))]
    packed += [gather.relay(depth, stage, term1) for stage in reversed(range(1, depth - 1))]
    gather.relay(1, 0, term1)
    far_placed = [after(far_one, term1, gather.held[1][3][0], *packed), far_both]
    msg2, msg3, term2, term3 = leaf_forward(far_placed, leaf_w, mid_w)
    near2 = partner(term3, "rep", 1)
    near2 = after(near2, gather.held[depth - 1][2][0])
    gather.exchange(0, near2)
    first_map = gather.weight(0)
    (pair,) = fused(pair_product, "pair_product", term2, near2)
    far_pair = partner(pair, "rep", 2)
    packed = [gather.relay(level, 0, pair) for level in range(2, depth)]
    far_pair = after(far_pair, *packed)

    cotangents = {0: View(cotangent)}
    for stage in reversed(range(1, depth)):
        if stage == depth - 1:
            value = after(cotangent_sent, pair)
        else:
            half = next(iter(cotangents.values())).shape[0] // 2
            (value,) = step(
                lambda: (),
                "stack",
                [],
                stacks=[[view.part(half, 2 * half) for view in cotangents.values()]],
                ids=ids,
            )
            far_pair = after(far_pair, value)
            cotangents = {key: view.part(0, half) for key, view in cotangents.items()}
        got = partner(value, "sub", 1 << stage)
        half = cotangents[0].shape[0]
        for place_at, key in enumerate(list(cotangents)):
            cotangents[key ^ (1 << stage)] = View(got, (place_at * half, (place_at + 1) * half))

    weights, messages, own_ups, other_ups = [], [], [], []
    for level in range(depth):
        if level == 1:
            for later in range(1, depth):
                gather.exchange(later, own_ups[0])
            weights += [gather.weight(later) for later in range(1, depth)]
            weights[1] = after(weights[1], weights[2])
        if level == 0:
            weights.append(first_map)
            outs = fused(mid_forward, "mid_forward", term0, near0, far_pair, weights[0])
        else:
            outs = fused(up_forward, "up_forward", own_ups[-1], other_ups[-1], weights[level])
        messages.append(outs[0])
        own_ups.append(outs[1])
        other_ups.append(partner(outs[2], "sub", 1 << level))
        if level == 0:
            early = partner(after(messages[0], other_ups[0]), "sub", 1)
        if level == 1:
            other_ups[1] = after(other_ups[1], early)
    gather.exchange(depth, other_ups[-1])
    (root,) = fused(top_forward, "top_forward", own_ups[-1], other_ups[-1])

    turns = [[[View(message)], []] for message in messages]

    def gather_turns(stage, value, levels):
        got = partner(value, "sub", 1 << stage)
        at = 0
        for level in levels:
            count = sum(view.shape[0] for view in turns[level][0])
            turns[level][0 if level > stage else 1].append(View(got, (at, at + count)))
            at += count
            if stage < level < depth:
                turns[level][1].append(View(got, (at, at + count)))
                at += count

    def to_stack(stage, levels):
        return [
            view
            for level in levels
            for view in turns[level][0] + (turns[level][1] if stage < level < depth else [])
        ]

    def stack_turns(stage, levels):
        (value,) = step(lambda: (), "stack", [], stacks=[to_stack(stage, levels)], ids=ids)
        gather_turns(stage, value, levels)

    turns[0][1].append(View(early))
    for level in range(1, depth):
        gather_turns(level, after(messages[level], own_ups[level]), [level])
    for stage in reversed(range(2, depth - 1)):
        stack_turns(stage, range(stage + 1, depth))

    head_maps = gather.head(head_left, head_right)
    root_high = partner(root, "sub", 1)
    root, grad_value, grad_gate, grad_msg, give, value = step(
        head_body,
        "head",
        [root, root_high, head_maps],
        parts=[cotangents[2 * i] for i in range(sub_count // 2)],
        stacks=[to_stack(1, range(2, depth))],
        ids=ids,
        limit=12,
    )
    got = partner(give, "sub", 1)
    gather_turns(1, value, range(2, depth))
    turns.append([[View(root)], []])
    gather_turns(depth - 1, root, [depth])
    low, high, value, root_value = step(
        top_back,
        "top_back",
        [own_ups[-1], other_ups[-1], grad_msg, got],
        stacks=[to_stack(0, range(1, depth)), to_stack(depth - 2, [depth])],
        ids=ids,
    )
    gather_turns(0, value, range(1, depth))
    gather_turns(depth - 2, root_value, [depth])
    for stage in reversed(range(1, depth - 2)):
        stack_turns(stage, [depth])
    turns[depth][1] = turns[depth][0]
    first_inputs = turns[0][0] + turns[0][1] + turns[depth][0]
    second_inputs = [view for entry in turns[1:depth] for turn in entry for view in turn]

    lows, highs = [None] * depth, [None] * depth
    lows[-1], highs[-1] = low, partner(high, "sub", 1 << (depth - 1))
    columns = [None] * depth + [[View(grad_value)], [View(grad_gate)]]

    def groups_of(stage):
        return [
            [View(lows[level]), View(highs[level])] if columns[level] is None else columns[level]
            for level in range(stage, depth)
        ]

    def spread(stage, keeps, send):
        got = partner(send, "sub", 1 << stage)
        at = 0
        for level, keep in zip(range(stage, depth + 2), keeps):
            span = keep.shape[1]
            columns[level] = [View(keep), View(got, None, (at, at + span))]
            at += span

    def columns_of(level, turn):
        if level == depth:
            return columns[depth + turn]
        if level == 0:
            return [columns[0][turn]]
        count = rows >> level
        return [
            view.part(i * count, (i + 1) * count)
            for view in columns[level]
            for i in range(turn, view.shape[0] // count, 2)
        ]

    far_got = []
    for level in reversed(range(depth - 1)):
        above = level + 1
        far = {depth - 2: first_inputs, 0: second_inputs}.get(level)
        low, high, *rest = step(
            down_back,
            "down_back",
            [own_ups[level], other_ups[level], weights[above], lows[above], highs[above]],
            halves=groups_of(above),
            fixed=columns[depth:],
            level=above,
            far=far,
            ids=ids,
            limit=12,
        )
        lows[level] = low
        highs[level] = partner(high, "sub", 1 << level)
        if far:
            far_got.append(partner(rest.pop(), "rep", 2))
        spread(above, rest[:-1], rest[-1])

    lows[0] = after(lows[0], far_got[0])
    back0, back1, pair_back, *rest = step(
        mid_back,
        "mid_back",
        [term0, near0, far_pair, weights[0], lows[0], highs[0]],
        halves=groups_of(0),
        level=0,
        ids=ids,
        limit=12,
    )
    back1 = partner(back1, "rep", 1)
    pair_back = partner(pair_back, "rep", 2)
    spread(0, rest[:-1], rest[-1])
    first = leaf_first(placed[:2], [back0, back1], leaf_w, mid_w)
    groups = [
        [view for turn in range(2) for view in columns_of(level, turn)]
        for level in range(depth + 1)
    ]
    groups[0][0] = groups[0][0].gated(first)
    own_grads = side_by_side(groups)
    far_grads = partner(own_grads, "rep", 2)
    near_grads = partner(own_grads, "rep", 1)
    back2, back3 = fused(far_back, "far_back", after(pair_back, own_grads), term2, near2)
    back3 = partner(back3, "rep", 1)
    inputs = first_inputs + second_inputs
    near_got = partner(near_inputs([inputs[0].gated(back2)] + inputs[1:], far_got, ids), "rep", 1)
    leaf_grad, mid_grad = leaf_backward(
        placed, [msg0, msg1, msg2, msg3], [back0, back1, back2, back3], leaf_w, mid_w, first
    )
    grads = [own_grads, far_grads, near_grads]
    grads.append(partner(after(far_grads, leaf_grad), "rep", 1))
    upper = upper_grads(turns, far_got, near_got, grads, ids)
    return leaf_grad[None], mid_grad[None, None], upper[None]


def solution(mesh):
    placed = (
        P("rep", "sub", None),
        P("sub"),
        P(("sub", "rep"), None, None, None),
        P("sub", "rep", None, None),
        P("sub", None, None, None),
        P("rep", "sub"),
    )
    return jax.shard_map(
        on_device,
        mesh=mesh,
        in_specs=placed,
        out_specs=(
            P(("sub", "rep"), None, None, None),
            P("sub", "rep", None, None),
            P("sub", "rep", None, None),
        ),
        check_vma=False,
    )
```

```python
import functools

import jax
import jax.numpy as jnp
from jax import lax
from jax.experimental import pallas as pl
from jax.experimental.pallas import tpu as pltpu
from jax.sharding import PartitionSpec as P

EPSILON = 1e-06
CHILDREN = 4
MIB = 1024 * 1024


def partner(value, axis, offset):
    return lax.ppermute(value, axis, [(i, i ^ offset) for i in range(lax.axis_size(axis))])


def rms_factor(values):
    return lax.rsqrt(jnp.mean(values * values, axis=-1, keepdims=True) + EPSILON)


def norm_back(gradient, normed, factor):
    return factor * (gradient - normed * jnp.mean(gradient * normed, axis=-1, keepdims=True))


def matmul(left_arr, right_arr):
    return jnp.dot(left_arr, right_arr, preferred_element_type=jnp.float32)


def matmul_t(left_arr, right_arr):
    return lax.dot_general(
        left_arr, right_arr, (((1,), (1,)), ((), ())), preferred_element_type=jnp.float32
    )


def inner_t(left_arr, right_arr):
    return lax.dot_general(
        left_arr, right_arr, (((0,), (0,)), ((), ())), preferred_element_type=jnp.float32
    )


def bf16(value):
    return value.astype(jnp.bfloat16)


def f32(value):
    return value.astype(jnp.float32)


def whole_block():
    return pl.BlockSpec(memory_space=pltpu.VMEM)


def smem_block():
    return pl.BlockSpec(memory_space=pltpu.SMEM)


def bit_of(value, level):
    return jnp.bitwise_and(jnp.right_shift(value, level), 1)


def place_kernel(slots, depth, ids_ref, map_ref, regions_ref, cotangent_ref, *rest):
    outs, keep_ref, send_ref, wide = rest[:CHILDREN], *rest[CHILDREN:]
    rows = regions_ref.shape[0] // slots
    parts = wide.shape[0]
    for part in range(parts):
        wide[part] = regions_ref[:, part * 128 : (part + 1) * 128].astype(jnp.float32)
    flip = 0
    for level in range(depth):
        flip = flip + bit_of(ids_ref[0], level) * (rows >> (level + 1))
    row = lax.broadcasted_iota(jnp.int32, (rows, rows), 0)
    col = lax.broadcasted_iota(jnp.int32, (rows, rows), 1)
    select = bf16(jnp.bitwise_xor(row, flip) == col)
    block = rows >> depth
    wanted = jnp.bitwise_and(row, block - 1)
    for level in range(depth):
        wanted = wanted + bit_of(row // block, level) * (block << (depth - 1 - level))
    pick = bf16(jnp.bitwise_xor(wanted, flip) == col)
    left = cotangent_ref[...]
    picked = 0.0
    for _ in range(3):
        top = bf16(left)
        left = left - f32(top)
        picked = picked + matmul(pick, top)
    keep_ref[...] = picked[: rows // 2]
    send_ref[...] = picked[rows // 2 :]
    for offset in range(CHILDREN):
        node = jnp.bitwise_xor(ids_ref[1], offset)
        for child in range(CHILDREN):
            region = map_ref[node * CHILDREN + child]
            for part in range(parts):
                values = bf16(wide[part, pl.ds(region, rows, stride=slots), :])
                outs[offset][child, :, part * 128 : (part + 1) * 128] = bf16(
                    matmul(select, values)
                )


def place(regions, leaf_map, cotangent, ids, depth):
    rows, slots, feats = regions.shape
    flat = regions.reshape(rows * slots, feats)
    return pl.pallas_call(
        functools.partial(place_kernel, slots, depth),
        out_shape=[jax.ShapeDtypeStruct((CHILDREN, rows, feats), jnp.bfloat16)] * CHILDREN
        + [jax.ShapeDtypeStruct((rows // 2, cotangent.shape[1]), cotangent.dtype)] * 2,
        in_specs=[smem_block(), smem_block(), whole_block(), whole_block()],
        out_specs=[whole_block()] * (CHILDREN + 2),
        scratch_shapes=[pltpu.VMEM((feats // 128, rows * slots, 128), jnp.float32)],
        compiler_params=pltpu.CompilerParams(vmem_limit_bytes=7 * MIB),
        name="place",
    )(ids, leaf_map, flat, cotangent)


def leaf_forward_kernel(count, *refs):
    placed, leaf_w, mid_w = refs[:count], refs[count], refs[count + 1]
    msgs, terms = refs[count + 2 : 2 * count + 2], refs[2 * count + 2 :]
    rows = placed[0].shape[1]
    product = None
    for child in range(CHILDREN):
        values = jnp.concatenate([ref[child] for ref in placed], axis=0)
        factor = 1.0 + matmul(values, leaf_w[child])
        product = factor if product is None else product * factor
    message = bf16(product * rms_factor(product))
    out = bf16(matmul(message, mid_w[...]))
    for i in range(count):
        msgs[i][...] = message[i * rows : (i + 1) * rows]
        terms[i][...] = out[i * rows : (i + 1) * rows]


def leaf_forward(placed, leaf_w, mid_w):
    count = len(placed)
    rows = placed[0].shape[1]
    width = mid_w.shape[0]
    return pl.pallas_call(
        functools.partial(leaf_forward_kernel, count),
        out_shape=[jax.ShapeDtypeStruct((rows, width), jnp.bfloat16)] * (2 * count),
        in_specs=[whole_block()] * (count + 2),
        out_specs=[whole_block()] * (2 * count),
        compiler_params=pltpu.CompilerParams(vmem_limit_bytes=14 * MIB),
        name="leaf_forward",
    )(*placed, leaf_w, mid_w)


def leaf_cotangents(placed, grads, leaf_w, mid_w):
    factors = [
        1.0 + matmul(jnp.concatenate([ref[child] for ref in placed], axis=0), leaf_w[child])
        for child in range(CHILDREN)
    ]
    low = factors[0] * factors[1]
    high = factors[2] * factors[3]
    product = low * high
    scale = rms_factor(product)
    back = matmul_t(jnp.concatenate([ref[...] for ref in grads], axis=0), mid_w[...])
    node = norm_back(back, product * scale, scale)
    high, low = node * high, node * low
    return [
        bf16(high * factors[1]),
        bf16(high * factors[0]),
        bf16(low * factors[3]),
        bf16(low * factors[2]),
    ]


def leaf_first_kernel(*refs):
    placed, grads, leaf_w, mid_w, out = refs[0:2], refs[2:4], refs[4], refs[5], refs[6]
    for child, value in enumerate(leaf_cotangents(placed, grads, leaf_w, mid_w)):
        out[child] = value


def leaf_first(placed, grads, leaf_w, mid_w):
    rows = placed[0].shape[1]
    return pl.pallas_call(
        leaf_first_kernel,
        out_shape=jax.ShapeDtypeStruct((CHILDREN, 2 * rows, mid_w.shape[0]), jnp.bfloat16),
        in_specs=[whole_block()] * 6,
        out_specs=whole_block(),
        compiler_params=pltpu.CompilerParams(vmem_limit_bytes=18 * MIB),
        name="leaf_first",
    )(*placed, *grads, leaf_w, mid_w)


def leaf_backward_kernel(*refs):
    placed, msgs, grads = refs[0:4], refs[4:8], refs[8:12]
    leaf_w, mid_w, first, leaf_out, mid_out = refs[12:17]
    all_grads = jnp.concatenate([ref[...] for ref in grads], axis=0)
    all_msgs = jnp.concatenate([ref[...] for ref in msgs], axis=0)
    mid_out[...] = bf16(inner_t(all_msgs, all_grads))
    second = leaf_cotangents(placed[2:], grads[2:], leaf_w, mid_w)
    for child in range(CHILDREN):
        values = jnp.concatenate([ref[child] for ref in placed], axis=0)
        cot = jnp.concatenate([first[child], second[child]], axis=0)
        leaf_out[child] = bf16(inner_t(values, cot))


def leaf_backward(placed, msgs, grads, leaf_w, mid_w, first):
    return pl.pallas_call(
        leaf_backward_kernel,
        out_shape=[
            jax.ShapeDtypeStruct(leaf_w.shape, jnp.bfloat16),
            jax.ShapeDtypeStruct(mid_w.shape, jnp.bfloat16),
        ],
        in_specs=[whole_block()] * 15,
        out_specs=[whole_block()] * 2,
        compiler_params=pltpu.CompilerParams(vmem_limit_bytes=30 * MIB),
        name="leaf_backward",
    )(*placed, *msgs, *grads, leaf_w, mid_w, first)


def fused(body, name, *args, limit=8, ids=None, plain=False):
    if plain or any(arg.shape[-2] % 16 or arg.shape[-1] % 128 for arg in args):
        return body(*args) if ids is None else body(ids, *args)
    count = len(args)
    if ids is None:
        shapes = jax.eval_shape(body, *args)
    else:
        shapes = jax.eval_shape(body, ids, *args)
        args = (ids, *args)

    def kernel(*refs):
        outs = refs[len(args) :]
        values = [ref[...] for ref in refs[len(args) - count : len(args)]]
        results = body(*values) if ids is None else body(refs[0], *values)
        for ref, result in zip(outs, results):
            ref[...] = result

    return pl.pallas_call(
        kernel,
        out_shape=shapes,
        in_specs=[smem_block()] * (len(args) - count) + [whole_block()] * count,
        out_specs=[whole_block()] * len(shapes),
        compiler_params=pltpu.CompilerParams(vmem_limit_bytes=limit * MIB),
        name=name,
    )(*args)


def join(pieces):
    if pieces[0].shape[0] % 16 == 0:
        return jnp.concatenate(pieces, axis=0)
    wide = lax.optimization_barrier(tuple(f32(piece) for piece in pieces))
    return bf16(lax.optimization_barrier(jnp.concatenate(wide, axis=0)))


def pack(pieces):
    arrays = []
    for array, _, _ in pieces:
        if not any(array is known for known in arrays):
            arrays.append(array)
    spots = [next(i for i, known in enumerate(arrays) if known is piece[0]) for piece in pieces]

    def body(*values):
        parts = [values[i][:, at : at + span] for i, (_, at, span) in zip(spots, pieces)]
        return (jnp.concatenate(parts, axis=1),)

    if any(piece[2] % 128 for piece in pieces):
        return body(*arrays)[0]
    return fused(body, "pack", *arrays, limit=6)[0]


def cut_kernel(depth, ids_ref, maps_ref, *refs):
    outs, split = refs[:-1], refs[-1]
    split[...] = jnp.swapaxes(maps_ref[...], 0, 1)
    width = maps_ref.shape[0]
    half = width // 2
    rows = pl.ds(pl.multiple_of(bit_of(ids_ref[1], 0) * half, half), half)
    for level in range(depth):
        span = width >> (level + 1)
        cols = pl.ds(width - 2 * span, span)
        side = bit_of(ids_ref[0], level)
        outs[3 * level][...] = split[side, :, cols]
        outs[3 * level + 1][...] = split[side, rows, cols]
        outs[3 * level + 2][...] = split[1 - side, rows, cols]
    span = width >> depth
    for side in range(2):
        outs[3 * depth + side][...] = split[side, :, width - span :]
        outs[3 * depth + 2][:, side * span : (side + 1) * span] = split[side, rows, width - span :]


def cut_maps(maps, ids, depth):
    width = maps.shape[0]
    half = width // 2
    spans = [width >> (level + 1) for level in range(depth)]
    if spans[-1] % 128 == 0:
        shapes = []
        for span in spans:
            shapes += [(width, span), (half, span), (half, span)]
        shapes += [(width, spans[-1])] * 2 + [(half, 2 * spans[-1])]
        outs = pl.pallas_call(
            functools.partial(cut_kernel, depth),
            out_shape=[jax.ShapeDtypeStruct(shape, maps.dtype) for shape in shapes],
            in_specs=[smem_block(), whole_block()],
            out_specs=[whole_block()] * len(shapes),
            scratch_shapes=[pltpu.VMEM((2, width, width), maps.dtype)],
            compiler_params=pltpu.CompilerParams(vmem_limit_bytes=18 * MIB),
            name="cut_maps",
        )(ids, maps)
    else:
        maps = jnp.transpose(maps, (1, 0, 2))
        outs = []
        core = bit_of(ids[1], 0)
        for level, span in enumerate(spans):
            side = bit_of(ids[0], level)
            first = width - 2 * span
            outs.append(lax.dynamic_slice(maps, (side, 0, first), (1, width, span))[0])
            for which in (side, 1 - side):
                outs.append(lax.dynamic_slice(maps, (which, core * half, first), (1, half, span))[0])
        outs += [maps[0, :, width - spans[-1] :], maps[1, :, width - spans[-1] :]]
        both = jnp.concatenate(outs[-2:], axis=1)
        outs.append(lax.dynamic_slice_in_dim(both, core * half, half, 0))
    return [outs[3 * i : 3 * i + 3] for i in range(depth)], outs[3 * depth :]


def assemble_kernel(spots, count, ids_ref, own_ref, *refs):
    out_ref = refs[-1]
    width, span = own_ref.shape
    half = width // 2
    block = jnp.bitwise_and(ids_ref[0], out_ref.shape[1] // span - 1)
    own_core = bit_of(ids_ref[1], 0)
    out_ref[:, pl.ds(pl.multiple_of(block * span, span), span)] = own_ref[...]
    for offset, index, at in spots:
        col = jnp.bitwise_xor(block, offset) * span
        for ref, core in ((refs[index], own_core), (refs[count + index], 1 - own_core)):
            out_ref[
                pl.ds(pl.multiple_of(core * half, half), half),
                pl.ds(pl.multiple_of(col, span), span),
            ] = ref[:, at : at + span]


def assemble(own, pieces, ids):
    width, span = own.shape
    count = len(pieces) + 1
    if span % 128 == 0:
        mine, other, spots = [], [], []
        for offset, (near_half, far_half, at) in pieces.items():
            known = [i for i, array in enumerate(mine) if array is near_half]
            if not known:
                mine.append(near_half)
                other.append(far_half)
                known = [len(mine) - 1]
            spots.append((offset, known[0], at))
        return pl.pallas_call(
            functools.partial(assemble_kernel, spots, len(mine)),
            out_shape=jax.ShapeDtypeStruct((width, span * count), own.dtype),
            in_specs=[smem_block()] + [whole_block()] * (2 * len(mine) + 1),
            out_specs=whole_block(),
            compiler_params=pltpu.CompilerParams(vmem_limit_bytes=8 * MIB),
            name="assemble",
        )(ids, own, *mine, *other)
    block = jnp.bitwise_and(ids[0], count - 1)
    core = bit_of(ids[1], 0)
    out = jnp.zeros((width, span * count), own.dtype)
    out = lax.dynamic_update_slice(out, own, (0, block * span))
    for offset, (near_half, far_half, at) in pieces.items():
        col = (block ^ offset) * span
        for array, which in ((near_half, core), (far_half, 1 - core)):
            part = array[:, at : at + span]
            out = lax.dynamic_update_slice(out, part, (which * (width // 2), col))
    return out


def assemble_head_kernel(spots, count, ids_ref, left_ref, right_ref, *refs):
    out_ref = refs[-1]
    width, span = left_ref.shape
    half, total = width // 2, out_ref.shape[1] // 2
    out_ref[:, :span] = left_ref[...]
    out_ref[:, total : total + span] = right_ref[...]
    own_core = bit_of(ids_ref[1], 0)
    for offset, index, at in spots:
        for ref, core in ((refs[index], own_core), (refs[count + index], 1 - own_core)):
            rows = pl.ds(pl.multiple_of(core * half, half), half)
            for side in range(2):
                col = side * total + (offset // 2) * span
                out_ref[rows, col : col + span] = ref[:, at + side * span : at + (side + 1) * span]


def assemble_head(left, right, pieces, ids):
    width, span = left.shape
    total = span * (len(pieces) + 1)
    mine, other, spots = [], [], []
    for offset, (near_half, far_half, at) in pieces.items():
        known = [i for i, array in enumerate(mine) if array is near_half]
        if not known:
            mine.append(near_half)
            other.append(far_half)
            known = [len(mine) - 1]
        spots.append((offset, known[0], at))
    if span % 128 == 0:
        return pl.pallas_call(
            functools.partial(assemble_head_kernel, spots, len(mine)),
            out_shape=jax.ShapeDtypeStruct((width, 2 * total), left.dtype),
            in_specs=[smem_block()] + [whole_block()] * (2 * len(mine) + 2),
            out_specs=whole_block(),
            compiler_params=pltpu.CompilerParams(vmem_limit_bytes=8 * MIB),
            name="assemble_head",
        )(ids, left, right, *mine, *other)
    core = bit_of(ids[1], 0)
    out = jnp.zeros((width, 2 * total), left.dtype)
    out = lax.dynamic_update_slice(out, left, (0, 0))
    out = lax.dynamic_update_slice(out, right, (0, total))
    for offset, index, at in spots:
        for array, which in ((mine[index], core), (other[index], 1 - core)):
            for side in range(2):
                part = array[:, at + side * span : at + (side + 1) * span]
                col = side * total + (offset // 2) * span
                out = lax.dynamic_update_slice(out, part, (which * (width // 2), col))
    return out


def after(value, *others):
    return lax.optimization_barrier((value, *others))[0]


class MapGather:
    def __init__(self, blocks, head_half, ids):
        self.blocks, self.ids = blocks + [(None, head_half, None)], ids
        self.depth = len(blocks)
        blocks = self.blocks
        self.spans = [block[1].shape[1] for block in blocks]
        self.held = [{0: (block[1], 0)} for block in blocks]
        self.other = {}
        pieces = [(blocks[0][2], 0, self.spans[0])]
        pieces += [(blocks[i][1], 0, self.spans[i]) for i in range(1, self.depth)]
        self.first = pack(pieces)
        got = partner(self.first, "sub", 1)
        self.received = got
        at = 0
        for level in range(self.depth):
            self.held[level][1] = (got, at)
            at += self.spans[level]

    def relay(self, level, stage, gate=None):
        if stage == level:
            offsets, value = [0], self.blocks[level][2]
            if gate is not None:
                value = after(value, gate)
        else:
            offsets = [i for i in self.held[level] if i % (2 << stage) == 0]
            if stage == 0:
                offsets = [i for i in offsets if i > 0]
            pieces = [(*self.held[level][i], self.spans[level]) for i in offsets]
            if gate is not None:
                pieces[-1] = (after(pieces[-1][0], gate), *pieces[-1][1:])
            if len(pieces) == 1 and pieces[0][0].shape[1] == pieces[0][2]:
                value = pieces[0][0]
            else:
                value = pack(pieces)
            if 0 not in offsets:
                for place, offset in enumerate(offsets):
                    self.held[level][offset] = (value, place * self.spans[level])
        got = partner(value, "sub", 1 << stage)
        for place, offset in enumerate(offsets):
            self.held[level][offset ^ (1 << stage)] = (got, place * self.spans[level])
        return value

    def exchange(self, level, gate):
        for offset, (array, _) in self.held[level].items():
            if offset > 0 and id(array) not in self.other:
                self.other[id(array)] = (array, partner(after(array, gate), "rep", 1))

    def head(self, left, right):
        return assemble_head(left, right, self.pieces(self.depth), self.ids)

    def weight(self, level):
        return assemble(self.blocks[level][0], self.pieces(level), self.ids)

    def pieces(self, level):
        pieces = {}
        for offset, (array, at) in self.held[level].items():
            if offset > 0:
                pieces[offset] = (array, self.other[id(array)][1], at)
        return pieces


class View:
    def __init__(self, array, rows=None, cols=None):
        self.array = array
        self.rows = (0, array.shape[0]) if rows is None else rows
        self.cols = (0, array.shape[1]) if cols is None else cols
        self.shape = (self.rows[1] - self.rows[0], self.cols[1] - self.cols[0])

    def value(self):
        return self.array[slice(*self.rows), slice(*self.cols)]

    def part(self, first, last):
        return View(self.array, (self.rows[0] + first, self.rows[0] + last), self.cols)

    def gated(self, *gates):
        return View(after(self.array, *gates), self.rows, self.cols)

    def aligned(self):
        edges = (*self.rows, *self.cols)
        return all(edge % unit == 0 for edge, unit in zip(edges, (16, 16, 128, 128)))


def spots_of(views):
    arrays, spots = [], []
    for view in views:
        known = [i for i, array in enumerate(arrays) if array is view.array]
        if not known:
            arrays.append(view.array)
            known = [len(arrays) - 1]
        spots.append((known[0], view.rows, view.cols))
    return arrays, spots


def join_all(pieces):
    if len(pieces) == 1:
        return pieces[0]
    if pieces[0].dtype == jnp.float32 or all(piece.shape[0] % 16 == 0 for piece in pieces):
        return jnp.concatenate(pieces, axis=0)
    wide = lax.optimization_barrier(tuple(f32(piece) for piece in pieces))
    return bf16(lax.optimization_barrier(jnp.concatenate(wide, axis=0)))


def step(body, name, args, parts=(), stacks=(), halves=(), fixed=(), level=0, far=None, **options):
    groups = [[view] for view in parts] + [list(group) for group in stacks]
    halved = [list(group) for group in (*halves, *fixed)]
    views = [view for group in (*groups, *halved, far or ()) for view in group]
    arrays = list(args)
    for view in views:
        if not any(array is view.array for array in arrays):
            arrays.append(view.array)

    def cut(values, group):
        pieces = []
        for view in group:
            index = next(i for i, array in enumerate(arrays) if array is view.array)
            pieces.append(values[index][slice(*view.rows), slice(*view.cols)])
        return join_all(pieces)

    def whole(ids, *values):
        given = [cut(values, group) for group in groups[: len(parts)]]
        results = list(body(*values[: len(args)], *given))
        results += [cut(values, group) for group in groups[len(parts) :]]
        sends = []
        for index, group in enumerate(halved):
            full = cut(values, group)
            half = full.shape[1] // 2
            low, high = full[:, :half], full[:, half:]
            if index < len(halves):
                own = bit_of(ids[0], level) == 1
                low, high = jnp.where(own, high, low), jnp.where(own, low, high)
            results.append(low)
            sends.append(high)
        if sends:
            results.append(jnp.concatenate(sends, axis=1))
        if far:
            full = cut(values, far)
            half = full.shape[1] // 2
            results.append(jnp.where(bit_of(ids[1], 1) == 1, full[:, :half], full[:, half:]))
        return results

    plain = not all(view.aligned() for view in views)
    return fused(whole, name, *arrays, plain=plain, **options)


def near_inputs_kernel(spots, ids_ref, first_ref, second_ref, *refs):
    out_ref = refs[-1]
    quarter = out_ref.shape[1]
    other = 1 - bit_of(ids_ref[1], 0)
    lanes = pl.ds(pl.multiple_of((bit_of(ids_ref[1], 1) * 2 + other) * quarter, quarter), quarter)
    at = 0
    for index, (first, last), _ in spots:
        out_ref[at : at + last - first] = refs[index][first:last, lanes]
        at += last - first
    for ref in (first_ref, second_ref):
        count = ref.shape[0]
        lanes = pl.ds(pl.multiple_of(other * quarter, quarter), quarter)
        out_ref[at : at + count] = ref[:, lanes]
        at += count


def near_inputs(views, got, ids):
    quarter = views[0].shape[1] // 4
    if not all(view.aligned() for view in views):
        full = join_all([view.value() for view in views])
        other = 1 - bit_of(ids[1], 0)
        where = (bit_of(ids[1], 1) * 2 + other) * quarter
        own = lax.dynamic_slice_in_dim(full, where, quarter, 1)
        far = jnp.concatenate(got, axis=0)
        return jnp.concatenate(
            [own, lax.dynamic_slice_in_dim(far, other * quarter, quarter, 1)], axis=0
        )
    arrays, spots = spots_of(views)
    return pl.pallas_call(
        functools.partial(near_inputs_kernel, spots),
        out_shape=jax.ShapeDtypeStruct(
            (2 * sum(array.shape[0] for array in got), quarter), jnp.bfloat16
        ),
        in_specs=[smem_block()] + [whole_block()] * (len(arrays) + 2),
        out_specs=whole_block(),
        compiler_params=pltpu.CompilerParams(vmem_limit_bytes=8 * MIB),
        name="near_inputs",
    )(ids, *got, *arrays)


def side_by_side_kernel(groups, *refs):
    out_ref = refs[-1]
    col = 0
    for spots in groups:
        at = 0
        for index, rows, cols in spots:
            span = cols[1] - cols[0]
            count = rows[1] - rows[0]
            out_ref[at : at + count, col : col + span] = refs[index][slice(*rows), slice(*cols)]
            at += count
        col += span


def side_by_side(groups):
    views = [view for group in groups for view in group]
    if not all(view.aligned() for view in views):
        return jnp.concatenate(
            [join_all([view.value() for view in group]) for group in groups], axis=1
        )
    arrays, spots = spots_of(views)
    by_group = [[spots.pop(0) for _ in group] for group in groups]
    shape = (
        sum(view.shape[0] for view in groups[0]),
        sum(group[0].shape[1] for group in groups),
    )
    return pl.pallas_call(
        functools.partial(side_by_side_kernel, by_group),
        out_shape=jax.ShapeDtypeStruct(shape, jnp.bfloat16),
        in_specs=[whole_block()] * len(arrays),
        out_specs=whole_block(),
        compiler_params=pltpu.CompilerParams(vmem_limit_bytes=6 * MIB),
        name="side_by_side",
    )(*arrays)


def upper_grads_kernel(spots, spans, rows, ids_ref, first_ref, second_ref, near_ref, *refs):
    grads, inputs, out_ref, both = refs[:4], refs[4:-2], refs[-2], refs[-1]
    quarter = out_ref.shape[0]
    core, far = bit_of(ids_ref[1], 0), bit_of(ids_ref[1], 1)
    lanes = pl.ds(pl.multiple_of((far * 2 + core) * quarter, quarter), quarter)
    far_lanes = pl.ds(pl.multiple_of(core * quarter, quarter), quarter)
    total = first_ref.shape[0] + second_ref.shape[0]
    col = 0
    for level, span in enumerate(spans):
        for turn in range(2):
            here, at = spots[level][turn]
            pieces = [inputs[i][slice(*edges), lanes] for i, edges, _ in here]
            if at < first_ref.shape[0]:
                pieces.append(first_ref[at : at + rows, far_lanes])
            else:
                there = at - first_ref.shape[0]
                pieces.append(second_ref[there : there + rows, far_lanes])
            pieces.append(near_ref[at : at + rows])
            pieces.append(near_ref[total + at : total + at + rows])
            grad = jnp.concatenate(
                [ref[turn * rows : (turn + 1) * rows, col : col + span] for ref in grads], axis=0
            )
            value = bf16(inner_t(jnp.concatenate(pieces, axis=0), grad))
            side = turn
            if level < len(spans) - 1:
                side = jnp.bitwise_xor(bit_of(ids_ref[0], level), turn)
            both[side, :, col : col + span] = value
        col += span
    out_ref[...] = jnp.swapaxes(both[...], 0, 1)


def upper_grads(entries, far_got, near_got, grads, ids):
    depth = len(entries) - 1
    width = entries[0][0][0].shape[1]
    rows = sum(view.shape[0] for view in entries[0][0])
    spans = [width >> (level + 1) for level in range(depth)] + [width >> depth]
    views = [view for entry in entries for turn in entry for view in turn]
    starts = [[0, rows]]
    starts += [[(2 * level + 1) * rows, (2 * level + 2) * rows] for level in range(1, depth)]
    starts.append([2 * rows, 2 * rows])
    if all(view.aligned() for view in views) and spans[-1] % 128 == 0:
        arrays, flat = spots_of(views)
        spots = [
            [([flat.pop(0) for _ in entry[turn]], starts[level][turn]) for turn in range(2)]
            for level, entry in enumerate(entries)
        ]
        return pl.pallas_call(
            functools.partial(upper_grads_kernel, spots, spans, rows),
            out_shape=jax.ShapeDtypeStruct((width // 4, 2, width), jnp.bfloat16),
            in_specs=[smem_block()] + [whole_block()] * (len(arrays) + 7),
            out_specs=whole_block(),
            scratch_shapes=[pltpu.VMEM((2, width // 4, width), jnp.bfloat16)],
            compiler_params=pltpu.CompilerParams(vmem_limit_bytes=16 * MIB),
            name="upper_grads",
        )(ids, *far_got, near_got, *grads, *arrays)
    quarter = width // 4
    core, far = bit_of(ids[1], 0), bit_of(ids[1], 1)
    far_got = jnp.concatenate(far_got, axis=0)
    total = far_got.shape[0]
    parts, col = [], 0
    for level, span in enumerate(spans):
        both = []
        for turn in range(2):
            at = starts[level][turn]
            own = join_all([view.value() for view in entries[level][turn]])
            pieces = [
                lax.dynamic_slice_in_dim(own, (far * 2 + core) * quarter, quarter, 1),
                lax.dynamic_slice_in_dim(far_got[at : at + rows], core * quarter, quarter, 1),
                near_got[at : at + rows],
                near_got[total + at : total + at + rows],
            ]
            grad = [part[turn * rows : (turn + 1) * rows, col : col + span] for part in grads]
            both.append(bf16(inner_t(jnp.concatenate(pieces), jnp.concatenate(grad))))
        if level < depth:
            swap = bit_of(ids[0], level) == 1
            both = [jnp.where(swap, both[1 - i], both[i]) for i in range(2)]
        parts.append(jnp.stack(both, axis=1))
        col += span
    return jnp.concatenate(parts, axis=2)


def mid_forward(term, near, far, weight):
    product = (1.0 + f32(term)) * (1.0 + f32(near)) * f32(far)
    return up_product(bf16(product * rms_factor(product)), weight)


def up_product(message, weight):
    up = matmul(message, weight)
    keep = up.shape[0] // 2
    return message, up[:keep], bf16(up[keep:])


def up_forward(own_up, other_up, weight):
    joined = (1.0 + own_up) * (1.0 + f32(other_up))
    return up_product(bf16(joined * rms_factor(joined)), weight)


def top_forward(own_up, other_up):
    joined = (1.0 + own_up) * (1.0 + f32(other_up))
    return (bf16(joined * rms_factor(joined)),)


def head_body(low, high, maps, *cotangents):
    root = join([low, high])
    cotangent = jnp.concatenate(cotangents, axis=1)
    half = maps.shape[1] // 2
    both = matmul(root, maps)
    value, gating = both[:, :half], jax.nn.sigmoid(both[:, half:])
    grad_value = bf16(cotangent * gating)
    grad_gate = bf16(cotangent * value * gating * (1.0 - gating))
    back = matmul_t(grad_value, maps[:, :half]) + matmul_t(grad_gate, maps[:, half:])
    rows = root.shape[0] // 2
    return root, grad_value, grad_gate, back[:rows], bf16(back[rows:])


def level_back(grad_msg, own_up, other_up):
    own_up, other_up = 1.0 + own_up, 1.0 + f32(other_up)
    joined = own_up * other_up
    scaling = rms_factor(joined)
    grad = norm_back(grad_msg, joined * scaling, scaling)
    return bf16(grad * other_up), bf16(grad * own_up)


def top_back(own_up, other_up, own_part, got):
    return level_back(own_part + f32(got), own_up, other_up)


def down_back(own_up, other_up, weight, low, high):
    return level_back(matmul_t(join([low, high]), weight), own_up, other_up)


def mid_back(term, near, far, weight, low, high):
    own, near, far = 1.0 + f32(term), 1.0 + f32(near), f32(far)
    pair = own * near
    product = pair * far
    scale = rms_factor(product)
    grad_msg = matmul_t(join([low, high]), weight)
    grad = norm_back(grad_msg, product * scale, scale)
    grad_pair = grad * far
    return bf16(grad_pair * near), bf16(grad_pair * own), bf16(grad * pair)


def far_back(grad_pair, term, near):
    grad_pair = f32(grad_pair)
    return bf16(grad_pair * (1.0 + f32(near))), bf16(grad_pair * (1.0 + f32(term)))


def pair_product(term, near):
    return (bf16((1.0 + f32(term)) * (1.0 + f32(near))),)


def on_device(regions, leaf_map, leaf_bond_weight, mid_weight, upper_weight, head_cotangent):
    rows = regions.shape[0]
    sub_count = lax.axis_size("sub")
    depth = sub_count.bit_length() - 1
    ids = jnp.stack([lax.axis_index("sub"), lax.axis_index("rep")]).astype(jnp.int32)
    leaf_w = leaf_bond_weight[0]
    mid_w = mid_weight[0, 0]

    blocks, (head_left, head_right, head_half) = cut_maps(upper_weight[0], ids, depth)
    gather = MapGather(blocks, head_half, ids)

    *sent, cotangent, cotangent_sent = place(after(regions, head_right), leaf_map, head_cotangent, ids, depth)
    near = partner(sent[1], "rep", 1)
    far_both = partner(sent[3], "rep", 3)
    far_one = partner(sent[2], "rep", 2)
    placed = [sent[0], near, far_one, far_both]
    for level in reversed(range(1, depth)):
        gather.relay(level, level, near)
    msg0, msg1, term0, term1 = leaf_forward(placed[:2], leaf_w, mid_w)
    near0 = partner(term1, "rep", 1)
    packed = []
    for level in range(2, depth):
        packed += [gather.relay(level, stage, term1) for stage in reversed(range(1, level))]
    far_placed = [after(far_one, term1, gather.held[1][2][0], *packed), far_both]
    msg2, msg3, term2, term3 = leaf_forward(far_placed, leaf_w, mid_w)
    near2 = partner(term3, "rep", 1)
    gather.relay(1, 0, term3)
    near2 = after(near2, *[gather.relay(level, 0, term1) for level in range(2, depth)])
    gather.exchange(0, near2)
    gather.relay(depth, depth - 1, term1)
    (pair,) = fused(pair_product, "pair_product", term2, near2)
    far_pair = partner(pair, "rep", 2)
    first_map = gather.weight(0)
    packed = [gather.relay(depth, stage, first_map) for stage in reversed(range(1, depth - 1))]
    far_pair = after(far_pair, gather.held[1][3][0], *packed)

    cotangents = {0: View(cotangent)}
    for stage in reversed(range(1, depth)):
        if stage == depth - 1:
            value = after(cotangent_sent, first_map)
        else:
            half = next(iter(cotangents.values())).shape[0] // 2
            (value,) = step(
                lambda: (),
                "stack",
                [],
                stacks=[[view.part(half, 2 * half) for view in cotangents.values()]],
                ids=ids,
            )
            far_pair = after(far_pair, value)
            cotangents = {key: view.part(0, half) for key, view in cotangents.items()}
        got = partner(value, "sub", 1 << stage)
        half = cotangents[0].shape[0]
        for place_at, key in enumerate(list(cotangents)):
            cotangents[key ^ (1 << stage)] = View(got, (place_at * half, (place_at + 1) * half))

    weights, messages, own_ups, other_ups = [], [], [], []
    for level in range(depth):
        if level == 1:
            for later in range(1, depth):
                gather.exchange(later, own_ups[0])
            weights += [gather.weight(later) for later in range(1, depth)]
            weights[1] = after(weights[1], weights[2])
        if level == 0:
            weights.append(first_map)
            outs = fused(mid_forward, "mid_forward", term0, near0, far_pair, weights[0])
        else:
            outs = fused(up_forward, "up_forward", own_ups[-1], other_ups[-1], weights[level])
        messages.append(outs[0])
        own_ups.append(outs[1])
        other_ups.append(partner(outs[2], "sub", 1 << level))
        if level == 0:
            early = partner(after(messages[0], other_ups[0]), "sub", 1)
        if level == 1:
            other_ups[1] = after(other_ups[1], early)
    gather.exchange(depth, other_ups[-1])
    (root,) = fused(top_forward, "top_forward", own_ups[-1], other_ups[-1])

    turns = [[[View(message)], []] for message in messages]

    def gather_turns(stage, value, levels):
        got = partner(value, "sub", 1 << stage)
        at = 0
        for level in levels:
            count = sum(view.shape[0] for view in turns[level][0])
            turns[level][0 if level > stage else 1].append(View(got, (at, at + count)))
            at += count
            if stage < level < depth:
                turns[level][1].append(View(got, (at, at + count)))
                at += count

    def to_stack(stage, levels):
        return [
            view
            for level in levels
            for view in turns[level][0] + (turns[level][1] if stage < level < depth else [])
        ]

    def stack_turns(stage, levels):
        (value,) = step(lambda: (), "stack", [], stacks=[to_stack(stage, levels)], ids=ids)
        gather_turns(stage, value, levels)

    turns[0][1].append(View(early))
    for level in range(1, depth):
        gather_turns(level, after(messages[level], own_ups[level]), [level])
    for stage in reversed(range(2, depth - 1)):
        stack_turns(stage, range(stage + 1, depth))

    head_maps = gather.head(head_left, head_right)
    root_high = partner(root, "sub", 1)
    root, grad_value, grad_gate, grad_msg, give, value = step(
        head_body,
        "head",
        [root, root_high, head_maps],
        parts=[cotangents[2 * i] for i in range(sub_count // 2)],
        stacks=[to_stack(1, range(2, depth))],
        ids=ids,
        limit=12,
    )
    got = partner(give, "sub", 1)
    gather_turns(1, value, range(2, depth))
    turns.append([[View(root)], []])
    gather_turns(depth - 1, root, [depth])
    low, high, value, root_value = step(
        top_back,
        "top_back",
        [own_ups[-1], other_ups[-1], grad_msg, got],
        stacks=[to_stack(0, range(1, depth)), to_stack(depth - 2, [depth])],
        ids=ids,
    )
    gather_turns(0, value, range(1, depth))
    gather_turns(depth - 2, root_value, [depth])
    for stage in reversed(range(1, depth - 2)):
        stack_turns(stage, [depth])
    turns[depth][1] = turns[depth][0]
    first_inputs = turns[0][0] + turns[0][1] + turns[depth][0]
    second_inputs = [view for entry in turns[1:depth] for turn in entry for view in turn]

    lows, highs = [None] * depth, [None] * depth
    lows[-1], highs[-1] = low, partner(high, "sub", 1 << (depth - 1))
    columns = [None] * depth + [[View(grad_value)], [View(grad_gate)]]

    def groups_of(stage):
        return [
            [View(lows[level]), View(highs[level])] if columns[level] is None else columns[level]
            for level in range(stage, depth)
        ]

    def spread(stage, keeps, send):
        got = partner(send, "sub", 1 << stage)
        at = 0
        for level, keep in zip(range(stage, depth + 2), keeps):
            span = keep.shape[1]
            columns[level] = [View(keep), View(got, None, (at, at + span))]
            at += span

    def columns_of(level, turn):
        if level == depth:
            return columns[depth + turn]
        if level == 0:
            return [columns[0][turn]]
        count = rows >> level
        return [
            view.part(i * count, (i + 1) * count)
            for view in columns[level]
            for i in range(turn, view.shape[0] // count, 2)
        ]

    far_got = []
    for level in reversed(range(depth - 1)):
        above = level + 1
        far = {depth - 2: first_inputs, 0: second_inputs}.get(level)
        low, high, *rest = step(
            down_back,
            "down_back",
            [own_ups[level], other_ups[level], weights[above], lows[above], highs[above]],
            halves=groups_of(above),
            fixed=columns[depth:],
            level=above,
            far=far,
            ids=ids,
            limit=12,
        )
        lows[level] = low
        highs[level] = partner(high, "sub", 1 << level)
        if far:
            far_got.append(partner(rest.pop(), "rep", 2))
        spread(above, rest[:-1], rest[-1])

    lows[0] = after(lows[0], far_got[0])
    back0, back1, pair_back, *rest = step(
        mid_back,
        "mid_back",
        [term0, near0, far_pair, weights[0], lows[0], highs[0]],
        halves=groups_of(0),
        level=0,
        ids=ids,
        limit=12,
    )
    back1 = partner(back1, "rep", 1)
    pair_back = partner(pair_back, "rep", 2)
    spread(0, rest[:-1], rest[-1])
    first = leaf_first(placed[:2], [back0, back1], leaf_w, mid_w)
    groups = [
        [view for turn in range(2) for view in columns_of(level, turn)]
        for level in range(depth + 1)
    ]
    groups[0][0] = groups[0][0].gated(first)
    own_grads = side_by_side(groups)
    far_grads = partner(own_grads, "rep", 2)
    near_grads = partner(own_grads, "rep", 1)
    back2, back3 = fused(far_back, "far_back", after(pair_back, own_grads), term2, near2)
    back3 = partner(back3, "rep", 1)
    inputs = first_inputs + second_inputs
    near_got = partner(near_inputs([inputs[0].gated(back2)] + inputs[1:], far_got, ids), "rep", 1)
    leaf_grad, mid_grad = leaf_backward(
        placed, [msg0, msg1, msg2, msg3], [back0, back1, back2, back3], leaf_w, mid_w, first
    )
    grads = [own_grads, far_grads, near_grads]
    grads.append(partner(after(far_grads, leaf_grad), "rep", 1))
    upper = upper_grads(turns, far_got, near_got, grads, ids)
    return leaf_grad[None], mid_grad[None, None], upper[None]


def solution(mesh):
    placed = (
        P("rep", "sub", None),
        P("sub"),
        P(("sub", "rep"), None, None, None),
        P("sub", "rep", None, None),
        P("sub", None, None, None),
        P("rep", "sub"),
    )
    return jax.shard_map(
        on_device,
        mesh=mesh,
        in_specs=placed,
        out_specs=(
            P(("sub", "rep"), None, None, None),
            P("sub", "rep", None, None),
            P("sub", "rep", None, None),
        ),
        check_vma=False,
    )
```

```python
import functools

import jax
import jax.numpy as jnp
from jax import lax
from jax.experimental import pallas as pl
from jax.experimental.pallas import tpu as pltpu
from jax.sharding import PartitionSpec as P

EPSILON = 1e-06
CHILDREN = 4
MIB = 1024 * 1024


def partner(value, axis, offset):
    return lax.ppermute(value, axis, [(i, i ^ offset) for i in range(lax.axis_size(axis))])


def rms_factor(values):
    return lax.rsqrt(jnp.mean(values * values, axis=-1, keepdims=True) + EPSILON)


def norm_back(gradient, normed, factor):
    return factor * (gradient - normed * jnp.mean(gradient * normed, axis=-1, keepdims=True))


def matmul(left_arr, right_arr):
    return jnp.dot(left_arr, right_arr, preferred_element_type=jnp.float32)


def matmul_t(left_arr, right_arr):
    return lax.dot_general(
        left_arr, right_arr, (((1,), (1,)), ((), ())), preferred_element_type=jnp.float32
    )


def inner_t(left_arr, right_arr):
    return lax.dot_general(
        left_arr, right_arr, (((0,), (0,)), ((), ())), preferred_element_type=jnp.float32
    )


def bf16(value):
    return value.astype(jnp.bfloat16)


def f32(value):
    return value.astype(jnp.float32)


def whole_block():
    return pl.BlockSpec(memory_space=pltpu.VMEM)


def smem_block():
    return pl.BlockSpec(memory_space=pltpu.SMEM)


def bit_of(value, level):
    return jnp.bitwise_and(jnp.right_shift(value, level), 1)


def place_kernel(slots, depth, ids_ref, map_ref, regions_ref, cotangent_ref, *rest):
    outs, keep_ref, send_ref, wide = rest[:CHILDREN], *rest[CHILDREN:]
    rows = regions_ref.shape[0] // slots
    parts = wide.shape[0]
    for part in range(parts):
        wide[part] = regions_ref[:, part * 128 : (part + 1) * 128].astype(jnp.float32)
    flip = 0
    for level in range(depth):
        flip = flip + bit_of(ids_ref[0], level) * (rows >> (level + 1))
    row = lax.broadcasted_iota(jnp.int32, (rows, rows), 0)
    col = lax.broadcasted_iota(jnp.int32, (rows, rows), 1)
    select = bf16(jnp.bitwise_xor(row, flip) == col)
    block = rows >> depth
    wanted = jnp.bitwise_and(row, block - 1)
    for level in range(depth):
        wanted = wanted + bit_of(row // block, level) * (block << (depth - 1 - level))
    pick = bf16(jnp.bitwise_xor(wanted, flip) == col)
    left = cotangent_ref[...]
    picked = 0.0
    for _ in range(3):
        top = bf16(left)
        left = left - f32(top)
        picked = picked + matmul(pick, top)
    keep_ref[...] = picked[: rows // 2]
    send_ref[...] = picked[rows // 2 :]
    for offset in range(CHILDREN):
        node = jnp.bitwise_xor(ids_ref[1], offset)
        for child in range(CHILDREN):
            region = map_ref[node * CHILDREN + child]
            for part in range(parts):
                values = bf16(wide[part, pl.ds(region, rows, stride=slots), :])
                outs[offset][child, :, part * 128 : (part + 1) * 128] = bf16(
                    matmul(select, values)
                )


def place(regions, leaf_map, cotangent, ids, depth):
    rows, slots, feats = regions.shape
    flat = regions.reshape(rows * slots, feats)
    return pl.pallas_call(
        functools.partial(place_kernel, slots, depth),
        out_shape=[jax.ShapeDtypeStruct((CHILDREN, rows, feats), jnp.bfloat16)] * CHILDREN
        + [jax.ShapeDtypeStruct((rows // 2, cotangent.shape[1]), cotangent.dtype)] * 2,
        in_specs=[smem_block(), smem_block(), whole_block(), whole_block()],
        out_specs=[whole_block()] * (CHILDREN + 2),
        scratch_shapes=[pltpu.VMEM((feats // 128, rows * slots, 128), jnp.float32)],
        compiler_params=pltpu.CompilerParams(vmem_limit_bytes=7 * MIB),
        name="place",
    )(ids, leaf_map, flat, cotangent)


def leaf_forward_kernel(count, *refs):
    placed, leaf_w, mid_w = refs[:count], refs[count], refs[count + 1]
    msgs, terms = refs[count + 2 : 2 * count + 2], refs[2 * count + 2 :]
    rows = placed[0].shape[1]
    product = None
    for child in range(CHILDREN):
        values = jnp.concatenate([ref[child] for ref in placed], axis=0)
        factor = 1.0 + matmul(values, leaf_w[child])
        product = factor if product is None else product * factor
    message = bf16(product * rms_factor(product))
    out = bf16(matmul(message, mid_w[...]))
    for i in range(count):
        msgs[i][...] = message[i * rows : (i + 1) * rows]
        terms[i][...] = out[i * rows : (i + 1) * rows]


def leaf_forward(placed, leaf_w, mid_w):
    count = len(placed)
    rows = placed[0].shape[1]
    width = mid_w.shape[0]
    return pl.pallas_call(
        functools.partial(leaf_forward_kernel, count),
        out_shape=[jax.ShapeDtypeStruct((rows, width), jnp.bfloat16)] * (2 * count),
        in_specs=[whole_block()] * (count + 2),
        out_specs=[whole_block()] * (2 * count),
        compiler_params=pltpu.CompilerParams(vmem_limit_bytes=14 * MIB),
        name="leaf_forward",
    )(*placed, leaf_w, mid_w)


def leaf_cotangents(placed, grads, leaf_w, mid_w):
    factors = [
        1.0 + matmul(jnp.concatenate([ref[child] for ref in placed], axis=0), leaf_w[child])
        for child in range(CHILDREN)
    ]
    low = factors[0] * factors[1]
    high = factors[2] * factors[3]
    product = low * high
    scale = rms_factor(product)
    back = matmul_t(jnp.concatenate([ref[...] for ref in grads], axis=0), mid_w[...])
    node = norm_back(back, product * scale, scale)
    high, low = node * high, node * low
    return [
        bf16(high * factors[1]),
        bf16(high * factors[0]),
        bf16(low * factors[3]),
        bf16(low * factors[2]),
    ]


def leaf_first_kernel(*refs):
    placed, grads, leaf_w, mid_w, out = refs[0:2], refs[2:4], refs[4], refs[5], refs[6]
    for child, value in enumerate(leaf_cotangents(placed, grads, leaf_w, mid_w)):
        out[child] = value


def leaf_first(placed, grads, leaf_w, mid_w):
    rows = placed[0].shape[1]
    return pl.pallas_call(
        leaf_first_kernel,
        out_shape=jax.ShapeDtypeStruct((CHILDREN, 2 * rows, mid_w.shape[0]), jnp.bfloat16),
        in_specs=[whole_block()] * 6,
        out_specs=whole_block(),
        compiler_params=pltpu.CompilerParams(vmem_limit_bytes=18 * MIB),
        name="leaf_first",
    )(*placed, *grads, leaf_w, mid_w)


def leaf_backward_kernel(*refs):
    placed, msgs, grads = refs[0:4], refs[4:8], refs[8:12]
    leaf_w, mid_w, first, leaf_out, mid_out = refs[12:17]
    all_grads = jnp.concatenate([ref[...] for ref in grads], axis=0)
    all_msgs = jnp.concatenate([ref[...] for ref in msgs], axis=0)
    mid_out[...] = bf16(inner_t(all_msgs, all_grads))
    second = leaf_cotangents(placed[2:], grads[2:], leaf_w, mid_w)
    for child in range(CHILDREN):
        values = jnp.concatenate([ref[child] for ref in placed], axis=0)
        cot = jnp.concatenate([first[child], second[child]], axis=0)
        leaf_out[child] = bf16(inner_t(values, cot))


def leaf_backward(placed, msgs, grads, leaf_w, mid_w, first):
    return pl.pallas_call(
        leaf_backward_kernel,
        out_shape=[
            jax.ShapeDtypeStruct(leaf_w.shape, jnp.bfloat16),
            jax.ShapeDtypeStruct(mid_w.shape, jnp.bfloat16),
        ],
        in_specs=[whole_block()] * 15,
        out_specs=[whole_block()] * 2,
        compiler_params=pltpu.CompilerParams(vmem_limit_bytes=30 * MIB),
        name="leaf_backward",
    )(*placed, *msgs, *grads, leaf_w, mid_w, first)


def fused(body, name, *args, limit=8, ids=None, plain=False):
    if plain or any(arg.shape[-2] % 16 or arg.shape[-1] % 128 for arg in args):
        return body(*args) if ids is None else body(ids, *args)
    count = len(args)
    if ids is None:
        shapes = jax.eval_shape(body, *args)
    else:
        shapes = jax.eval_shape(body, ids, *args)
        args = (ids, *args)

    def kernel(*refs):
        outs = refs[len(args) :]
        values = [ref[...] for ref in refs[len(args) - count : len(args)]]
        results = body(*values) if ids is None else body(refs[0], *values)
        for ref, result in zip(outs, results):
            ref[...] = result

    return pl.pallas_call(
        kernel,
        out_shape=shapes,
        in_specs=[smem_block()] * (len(args) - count) + [whole_block()] * count,
        out_specs=[whole_block()] * len(shapes),
        compiler_params=pltpu.CompilerParams(vmem_limit_bytes=limit * MIB),
        name=name,
    )(*args)


def join(pieces):
    if pieces[0].shape[0] % 16 == 0:
        return jnp.concatenate(pieces, axis=0)
    wide = lax.optimization_barrier(tuple(f32(piece) for piece in pieces))
    return bf16(lax.optimization_barrier(jnp.concatenate(wide, axis=0)))


def pack(pieces):
    arrays = []
    for array, _, _ in pieces:
        if not any(array is known for known in arrays):
            arrays.append(array)
    spots = [next(i for i, known in enumerate(arrays) if known is piece[0]) for piece in pieces]

    def body(*values):
        parts = [values[i][:, at : at + span] for i, (_, at, span) in zip(spots, pieces)]
        return (jnp.concatenate(parts, axis=1),)

    if any(piece[2] % 128 for piece in pieces):
        return body(*arrays)[0]
    return fused(body, "pack", *arrays, limit=6)[0]


def cut_kernel(depth, ids_ref, maps_ref, *refs):
    outs, split = refs[:-1], refs[-1]
    split[...] = jnp.swapaxes(maps_ref[...], 0, 1)
    width = maps_ref.shape[0]
    half = width // 2
    rows = pl.ds(pl.multiple_of(bit_of(ids_ref[1], 0) * half, half), half)
    for level in range(depth):
        span = width >> (level + 1)
        cols = pl.ds(width - 2 * span, span)
        side = bit_of(ids_ref[0], level)
        outs[3 * level][...] = split[side, :, cols]
        outs[3 * level + 1][...] = split[side, rows, cols]
        outs[3 * level + 2][...] = split[1 - side, rows, cols]
    span = width >> depth
    for side in range(2):
        outs[3 * depth + side][...] = split[side, :, width - span :]
        outs[3 * depth + 2][:, side * span : (side + 1) * span] = split[side, rows, width - span :]


def cut_maps(maps, ids, depth):
    width = maps.shape[0]
    half = width // 2
    spans = [width >> (level + 1) for level in range(depth)]
    if spans[-1] % 128 == 0:
        shapes = []
        for span in spans:
            shapes += [(width, span), (half, span), (half, span)]
        shapes += [(width, spans[-1])] * 2 + [(half, 2 * spans[-1])]
        outs = pl.pallas_call(
            functools.partial(cut_kernel, depth),
            out_shape=[jax.ShapeDtypeStruct(shape, maps.dtype) for shape in shapes],
            in_specs=[smem_block(), whole_block()],
            out_specs=[whole_block()] * len(shapes),
            scratch_shapes=[pltpu.VMEM((2, width, width), maps.dtype)],
            compiler_params=pltpu.CompilerParams(vmem_limit_bytes=18 * MIB),
            name="cut_maps",
        )(ids, maps)
    else:
        maps = jnp.transpose(maps, (1, 0, 2))
        outs = []
        core = bit_of(ids[1], 0)
        for level, span in enumerate(spans):
            side = bit_of(ids[0], level)
            first = width - 2 * span
            outs.append(lax.dynamic_slice(maps, (side, 0, first), (1, width, span))[0])
            for which in (side, 1 - side):
                outs.append(lax.dynamic_slice(maps, (which, core * half, first), (1, half, span))[0])
        outs += [maps[0, :, width - spans[-1] :], maps[1, :, width - spans[-1] :]]
        both = jnp.concatenate(outs[-2:], axis=1)
        outs.append(lax.dynamic_slice_in_dim(both, core * half, half, 0))
    return [outs[3 * i : 3 * i + 3] for i in range(depth)], outs[3 * depth :]


def assemble_kernel(spots, count, ids_ref, own_ref, *refs):
    out_ref = refs[-1]
    width, span = own_ref.shape
    half = width // 2
    block = jnp.bitwise_and(ids_ref[0], out_ref.shape[1] // span - 1)
    own_core = bit_of(ids_ref[1], 0)
    out_ref[:, pl.ds(pl.multiple_of(block * span, span), span)] = own_ref[...]
    for offset, index, at in spots:
        col = jnp.bitwise_xor(block, offset) * span
        for ref, core in ((refs[index], own_core), (refs[count + index], 1 - own_core)):
            out_ref[
                pl.ds(pl.multiple_of(core * half, half), half),
                pl.ds(pl.multiple_of(col, span), span),
            ] = ref[:, at : at + span]


def assemble(own, pieces, ids):
    width, span = own.shape
    count = len(pieces) + 1
    if span % 128 == 0:
        mine, other, spots = [], [], []
        for offset, (near_half, far_half, at) in pieces.items():
            known = [i for i, array in enumerate(mine) if array is near_half]
            if not known:
                mine.append(near_half)
                other.append(far_half)
                known = [len(mine) - 1]
            spots.append((offset, known[0], at))
        return pl.pallas_call(
            functools.partial(assemble_kernel, spots, len(mine)),
            out_shape=jax.ShapeDtypeStruct((width, span * count), own.dtype),
            in_specs=[smem_block()] + [whole_block()] * (2 * len(mine) + 1),
            out_specs=whole_block(),
            compiler_params=pltpu.CompilerParams(vmem_limit_bytes=8 * MIB),
            name="assemble",
        )(ids, own, *mine, *other)
    block = jnp.bitwise_and(ids[0], count - 1)
    core = bit_of(ids[1], 0)
    out = jnp.zeros((width, span * count), own.dtype)
    out = lax.dynamic_update_slice(out, own, (0, block * span))
    for offset, (near_half, far_half, at) in pieces.items():
        col = (block ^ offset) * span
        for array, which in ((near_half, core), (far_half, 1 - core)):
            part = array[:, at : at + span]
            out = lax.dynamic_update_slice(out, part, (which * (width // 2), col))
    return out


def assemble_head_kernel(spots, count, ids_ref, left_ref, right_ref, *refs):
    out_ref = refs[-1]
    width, span = left_ref.shape
    half, total = width // 2, out_ref.shape[1] // 2
    out_ref[:, :span] = left_ref[...]
    out_ref[:, total : total + span] = right_ref[...]
    own_core = bit_of(ids_ref[1], 0)
    for offset, index, at in spots:
        for ref, core in ((refs[index], own_core), (refs[count + index], 1 - own_core)):
            rows = pl.ds(pl.multiple_of(core * half, half), half)
            for side in range(2):
                col = side * total + (offset // 2) * span
                out_ref[rows, col : col + span] = ref[:, at + side * span : at + (side + 1) * span]


def assemble_head(left, right, pieces, ids):
    width, span = left.shape
    total = span * (len(pieces) + 1)
    mine, other, spots = [], [], []
    for offset, (near_half, far_half, at) in pieces.items():
        known = [i for i, array in enumerate(mine) if array is near_half]
        if not known:
            mine.append(near_half)
            other.append(far_half)
            known = [len(mine) - 1]
        spots.append((offset, known[0], at))
    if span % 128 == 0:
        return pl.pallas_call(
            functools.partial(assemble_head_kernel, spots, len(mine)),
            out_shape=jax.ShapeDtypeStruct((width, 2 * total), left.dtype),
            in_specs=[smem_block()] + [whole_block()] * (2 * len(mine) + 2),
            out_specs=whole_block(),
            compiler_params=pltpu.CompilerParams(vmem_limit_bytes=8 * MIB),
            name="assemble_head",
        )(ids, left, right, *mine, *other)
    core = bit_of(ids[1], 0)
    out = jnp.zeros((width, 2 * total), left.dtype)
    out = lax.dynamic_update_slice(out, left, (0, 0))
    out = lax.dynamic_update_slice(out, right, (0, total))
    for offset, index, at in spots:
        for array, which in ((mine[index], core), (other[index], 1 - core)):
            for side in range(2):
                part = array[:, at + side * span : at + (side + 1) * span]
                col = side * total + (offset // 2) * span
                out = lax.dynamic_update_slice(out, part, (which * (width // 2), col))
    return out


def after(value, *others):
    return lax.optimization_barrier((value, *others))[0]


class MapGather:
    def __init__(self, blocks, head_half, ids):
        self.blocks, self.ids = blocks + [(None, head_half, None)], ids
        self.depth = len(blocks)
        blocks = self.blocks
        self.spans = [block[1].shape[1] for block in blocks]
        self.held = [{0: (block[1], 0)} for block in blocks]
        self.other = {}
        pieces = [(blocks[0][2], 0, self.spans[0])]
        pieces += [(blocks[i][1], 0, self.spans[i]) for i in range(1, self.depth)]
        self.first = pack(pieces)
        got = partner(self.first, "sub", 1)
        self.received = got
        at = 0
        for level in range(self.depth):
            self.held[level][1] = (got, at)
            at += self.spans[level]

    def relay(self, level, stage, gate=None):
        if stage == level:
            offsets, value = [0], self.blocks[level][2]
            if gate is not None:
                value = after(value, gate)
        else:
            offsets = [i for i in self.held[level] if i % (2 << stage) == 0]
            if stage == 0:
                offsets = [i for i in offsets if i > 0]
            pieces = [(*self.held[level][i], self.spans[level]) for i in offsets]
            if gate is not None:
                pieces[-1] = (after(pieces[-1][0], gate), *pieces[-1][1:])
            if len(pieces) == 1 and pieces[0][0].shape[1] == pieces[0][2]:
                value = pieces[0][0]
            else:
                value = pack(pieces)
            if 0 not in offsets:
                for place, offset in enumerate(offsets):
                    self.held[level][offset] = (value, place * self.spans[level])
        got = partner(value, "sub", 1 << stage)
        for place, offset in enumerate(offsets):
            self.held[level][offset ^ (1 << stage)] = (got, place * self.spans[level])
        return value

    def exchange(self, level, gate):
        for offset, (array, _) in self.held[level].items():
            if offset > 0 and id(array) not in self.other:
                self.other[id(array)] = (array, partner(after(array, gate), "rep", 1))

    def head(self, left, right):
        return assemble_head(left, right, self.pieces(self.depth), self.ids)

    def weight(self, level):
        return assemble(self.blocks[level][0], self.pieces(level), self.ids)

    def pieces(self, level):
        pieces = {}
        for offset, (array, at) in self.held[level].items():
            if offset > 0:
                pieces[offset] = (array, self.other[id(array)][1], at)
        return pieces


class View:
    def __init__(self, array, rows=None, cols=None):
        self.array = array
        self.rows = (0, array.shape[0]) if rows is None else rows
        self.cols = (0, array.shape[1]) if cols is None else cols
        self.shape = (self.rows[1] - self.rows[0], self.cols[1] - self.cols[0])

    def value(self):
        return self.array[slice(*self.rows), slice(*self.cols)]

    def part(self, first, last):
        return View(self.array, (self.rows[0] + first, self.rows[0] + last), self.cols)

    def gated(self, *gates):
        return View(after(self.array, *gates), self.rows, self.cols)

    def aligned(self):
        edges = (*self.rows, *self.cols)
        return all(edge % unit == 0 for edge, unit in zip(edges, (16, 16, 128, 128)))


def spots_of(views):
    arrays, spots = [], []
    for view in views:
        known = [i for i, array in enumerate(arrays) if array is view.array]
        if not known:
            arrays.append(view.array)
            known = [len(arrays) - 1]
        spots.append((known[0], view.rows, view.cols))
    return arrays, spots


def join_all(pieces):
    if len(pieces) == 1:
        return pieces[0]
    if pieces[0].dtype == jnp.float32 or all(piece.shape[0] % 16 == 0 for piece in pieces):
        return jnp.concatenate(pieces, axis=0)
    wide = lax.optimization_barrier(tuple(f32(piece) for piece in pieces))
    return bf16(lax.optimization_barrier(jnp.concatenate(wide, axis=0)))


def step(body, name, args, parts=(), stacks=(), halves=(), fixed=(), level=0, far=None, **options):
    groups = [[view] for view in parts] + [list(group) for group in stacks]
    halved = [list(group) for group in (*halves, *fixed)]
    views = [view for group in (*groups, *halved, far or ()) for view in group]
    arrays = list(args)
    for view in views:
        if not any(array is view.array for array in arrays):
            arrays.append(view.array)

    def cut(values, group):
        pieces = []
        for view in group:
            index = next(i for i, array in enumerate(arrays) if array is view.array)
            pieces.append(values[index][slice(*view.rows), slice(*view.cols)])
        return join_all(pieces)

    def whole(ids, *values):
        given = [cut(values, group) for group in groups[: len(parts)]]
        results = list(body(*values[: len(args)], *given))
        results += [cut(values, group) for group in groups[len(parts) :]]
        sends = []
        for index, group in enumerate(halved):
            full = cut(values, group)
            half = full.shape[1] // 2
            low, high = full[:, :half], full[:, half:]
            if index < len(halves):
                own = bit_of(ids[0], level) == 1
                low, high = jnp.where(own, high, low), jnp.where(own, low, high)
            results.append(low)
            sends.append(high)
        if sends:
            results.append(jnp.concatenate(sends, axis=1))
        if far:
            full = cut(values, far)
            half = full.shape[1] // 2
            results.append(jnp.where(bit_of(ids[1], 1) == 1, full[:, :half], full[:, half:]))
        return results

    plain = not all(view.aligned() for view in views)
    return fused(whole, name, *arrays, plain=plain, **options)


def near_inputs_kernel(spots, ids_ref, first_ref, second_ref, *refs):
    out_ref = refs[-1]
    quarter = out_ref.shape[1]
    other = 1 - bit_of(ids_ref[1], 0)
    lanes = pl.ds(pl.multiple_of((bit_of(ids_ref[1], 1) * 2 + other) * quarter, quarter), quarter)
    at = 0
    for index, (first, last), _ in spots:
        out_ref[at : at + last - first] = refs[index][first:last, lanes]
        at += last - first
    for ref in (first_ref, second_ref):
        count = ref.shape[0]
        lanes = pl.ds(pl.multiple_of(other * quarter, quarter), quarter)
        out_ref[at : at + count] = ref[:, lanes]
        at += count


def near_inputs(views, got, ids):
    quarter = views[0].shape[1] // 4
    if not all(view.aligned() for view in views):
        full = join_all([view.value() for view in views])
        other = 1 - bit_of(ids[1], 0)
        where = (bit_of(ids[1], 1) * 2 + other) * quarter
        own = lax.dynamic_slice_in_dim(full, where, quarter, 1)
        far = jnp.concatenate(got, axis=0)
        return jnp.concatenate(
            [own, lax.dynamic_slice_in_dim(far, other * quarter, quarter, 1)], axis=0
        )
    arrays, spots = spots_of(views)
    return pl.pallas_call(
        functools.partial(near_inputs_kernel, spots),
        out_shape=jax.ShapeDtypeStruct(
            (2 * sum(array.shape[0] for array in got), quarter), jnp.bfloat16
        ),
        in_specs=[smem_block()] + [whole_block()] * (len(arrays) + 2),
        out_specs=whole_block(),
        compiler_params=pltpu.CompilerParams(vmem_limit_bytes=8 * MIB),
        name="near_inputs",
    )(ids, *got, *arrays)


def side_by_side_kernel(groups, *refs):
    out_ref = refs[-1]
    col = 0
    for spots in groups:
        at = 0
        for index, rows, cols in spots:
            span = cols[1] - cols[0]
            count = rows[1] - rows[0]
            out_ref[at : at + count, col : col + span] = refs[index][slice(*rows), slice(*cols)]
            at += count
        col += span


def side_by_side(groups):
    views = [view for group in groups for view in group]
    if not all(view.aligned() for view in views):
        return jnp.concatenate(
            [join_all([view.value() for view in group]) for group in groups], axis=1
        )
    arrays, spots = spots_of(views)
    by_group = [[spots.pop(0) for _ in group] for group in groups]
    shape = (
        sum(view.shape[0] for view in groups[0]),
        sum(group[0].shape[1] for group in groups),
    )
    return pl.pallas_call(
        functools.partial(side_by_side_kernel, by_group),
        out_shape=jax.ShapeDtypeStruct(shape, jnp.bfloat16),
        in_specs=[whole_block()] * len(arrays),
        out_specs=whole_block(),
        compiler_params=pltpu.CompilerParams(vmem_limit_bytes=6 * MIB),
        name="side_by_side",
    )(*arrays)


def upper_grads_kernel(spots, spans, rows, ids_ref, first_ref, second_ref, near_ref, *refs):
    grads, inputs, out_ref, both = refs[:4], refs[4:-2], refs[-2], refs[-1]
    quarter = out_ref.shape[0]
    core, far = bit_of(ids_ref[1], 0), bit_of(ids_ref[1], 1)
    lanes = pl.ds(pl.multiple_of((far * 2 + core) * quarter, quarter), quarter)
    far_lanes = pl.ds(pl.multiple_of(core * quarter, quarter), quarter)
    total = first_ref.shape[0] + second_ref.shape[0]
    col = 0
    for level, span in enumerate(spans):
        for turn in range(2):
            here, at = spots[level][turn]
            pieces = [inputs[i][slice(*edges), lanes] for i, edges, _ in here]
            if at < first_ref.shape[0]:
                pieces.append(first_ref[at : at + rows, far_lanes])
            else:
                there = at - first_ref.shape[0]
                pieces.append(second_ref[there : there + rows, far_lanes])
            pieces.append(near_ref[at : at + rows])
            pieces.append(near_ref[total + at : total + at + rows])
            grad = jnp.concatenate(
                [ref[turn * rows : (turn + 1) * rows, col : col + span] for ref in grads], axis=0
            )
            value = bf16(inner_t(jnp.concatenate(pieces, axis=0), grad))
            side = turn
            if level < len(spans) - 1:
                side = jnp.bitwise_xor(bit_of(ids_ref[0], level), turn)
            both[side, :, col : col + span] = value
        col += span
    out_ref[...] = jnp.swapaxes(both[...], 0, 1)


def upper_grads(entries, far_got, near_got, grads, ids):
    depth = len(entries) - 1
    width = entries[0][0][0].shape[1]
    rows = sum(view.shape[0] for view in entries[0][0])
    spans = [width >> (level + 1) for level in range(depth)] + [width >> depth]
    views = [view for entry in entries for turn in entry for view in turn]
    starts = [[0, rows]]
    starts += [[(2 * level + 1) * rows, (2 * level + 2) * rows] for level in range(1, depth)]
    starts.append([2 * rows, 2 * rows])
    if all(view.aligned() for view in views) and spans[-1] % 128 == 0:
        arrays, flat = spots_of(views)
        spots = [
            [([flat.pop(0) for _ in entry[turn]], starts[level][turn]) for turn in range(2)]
            for level, entry in enumerate(entries)
        ]
        return pl.pallas_call(
            functools.partial(upper_grads_kernel, spots, spans, rows),
            out_shape=jax.ShapeDtypeStruct((width // 4, 2, width), jnp.bfloat16),
            in_specs=[smem_block()] + [whole_block()] * (len(arrays) + 7),
            out_specs=whole_block(),
            scratch_shapes=[pltpu.VMEM((2, width // 4, width), jnp.bfloat16)],
            compiler_params=pltpu.CompilerParams(vmem_limit_bytes=16 * MIB),
            name="upper_grads",
        )(ids, *far_got, near_got, *grads, *arrays)
    quarter = width // 4
    core, far = bit_of(ids[1], 0), bit_of(ids[1], 1)
    far_got = jnp.concatenate(far_got, axis=0)
    total = far_got.shape[0]
    parts, col = [], 0
    for level, span in enumerate(spans):
        both = []
        for turn in range(2):
            at = starts[level][turn]
            own = join_all([view.value() for view in entries[level][turn]])
            pieces = [
                lax.dynamic_slice_in_dim(own, (far * 2 + core) * quarter, quarter, 1),
                lax.dynamic_slice_in_dim(far_got[at : at + rows], core * quarter, quarter, 1),
                near_got[at : at + rows],
                near_got[total + at : total + at + rows],
            ]
            grad = [part[turn * rows : (turn + 1) * rows, col : col + span] for part in grads]
            both.append(bf16(inner_t(jnp.concatenate(pieces), jnp.concatenate(grad))))
        if level < depth:
            swap = bit_of(ids[0], level) == 1
            both = [jnp.where(swap, both[1 - i], both[i]) for i in range(2)]
        parts.append(jnp.stack(both, axis=1))
        col += span
    return jnp.concatenate(parts, axis=2)


def mid_forward(term, near, far, weight):
    product = (1.0 + f32(term)) * (1.0 + f32(near)) * f32(far)
    return up_product(bf16(product * rms_factor(product)), weight)


def up_product(message, weight):
    up = matmul(message, weight)
    keep = up.shape[0] // 2
    return message, up[:keep], bf16(up[keep:])


def up_forward(own_up, other_up, weight):
    joined = (1.0 + own_up) * (1.0 + f32(other_up))
    return up_product(bf16(joined * rms_factor(joined)), weight)


def top_forward(own_up, other_up):
    joined = (1.0 + own_up) * (1.0 + f32(other_up))
    return (bf16(joined * rms_factor(joined)),)


def head_body(low, high, maps, *cotangents):
    root = join([low, high])
    cotangent = jnp.concatenate(cotangents, axis=1)
    half = maps.shape[1] // 2
    both = matmul(root, maps)
    value, gating = both[:, :half], jax.nn.sigmoid(both[:, half:])
    grad_value = bf16(cotangent * gating)
    grad_gate = bf16(cotangent * value * gating * (1.0 - gating))
    back = matmul_t(grad_value, maps[:, :half]) + matmul_t(grad_gate, maps[:, half:])
    rows = root.shape[0] // 2
    return root, grad_value, grad_gate, back[:rows], bf16(back[rows:])


def level_back(grad_msg, own_up, other_up):
    own_up, other_up = 1.0 + own_up, 1.0 + f32(other_up)
    joined = own_up * other_up
    scaling = rms_factor(joined)
    grad = norm_back(grad_msg, joined * scaling, scaling)
    return bf16(grad * other_up), bf16(grad * own_up)


def top_back(own_up, other_up, own_part, got):
    return level_back(own_part + f32(got), own_up, other_up)


def down_back(own_up, other_up, weight, low, high):
    return level_back(matmul_t(join([low, high]), weight), own_up, other_up)


def mid_back(term, near, far, weight, low, high):
    own, near, far = 1.0 + f32(term), 1.0 + f32(near), f32(far)
    pair = own * near
    product = pair * far
    scale = rms_factor(product)
    grad_msg = matmul_t(join([low, high]), weight)
    grad = norm_back(grad_msg, product * scale, scale)
    grad_pair = grad * far
    return bf16(grad_pair * near), bf16(grad_pair * own), bf16(grad * pair)


def far_back(grad_pair, term, near):
    grad_pair = f32(grad_pair)
    return bf16(grad_pair * (1.0 + f32(near))), bf16(grad_pair * (1.0 + f32(term)))


def pair_product(term, near):
    return (bf16((1.0 + f32(term)) * (1.0 + f32(near))),)


def on_device(regions, leaf_map, leaf_bond_weight, mid_weight, upper_weight, head_cotangent):
    rows = regions.shape[0]
    sub_count = lax.axis_size("sub")
    depth = sub_count.bit_length() - 1
    ids = jnp.stack([lax.axis_index("sub"), lax.axis_index("rep")]).astype(jnp.int32)
    leaf_w = leaf_bond_weight[0]
    mid_w = mid_weight[0, 0]

    blocks, (head_left, head_right, head_half) = cut_maps(upper_weight[0], ids, depth)
    gather = MapGather(blocks, head_half, ids)

    *sent, cotangent, cotangent_sent = place(after(regions, head_right), leaf_map, head_cotangent, ids, depth)
    near = partner(sent[1], "rep", 1)
    far_both = partner(sent[3], "rep", 3)
    far_one = partner(sent[2], "rep", 2)
    placed = [sent[0], near, far_one, far_both]
    for level in reversed(range(1, depth)):
        gather.relay(level, level, near)
    msg0, msg1, term0, term1 = leaf_forward(placed[:2], leaf_w, mid_w)
    near0 = partner(term1, "rep", 1)
    packed = []
    for level in range(2, depth):
        packed += [gather.relay(level, stage, term1) for stage in reversed(range(1, level))]
    far_placed = [after(far_one, term1, gather.held[1][2][0], *packed), far_both]
    msg2, msg3, term2, term3 = leaf_forward(far_placed, leaf_w, mid_w)
    near2 = partner(term3, "rep", 1)
    gather.relay(1, 0, term3)
    near2 = after(near2, *[gather.relay(level, 0, term1) for level in range(2, depth)])
    cotangents = {0: View(cotangent)}
    for stage in reversed(range(1, depth)):
        if stage == depth - 1:
            value = after(cotangent_sent, term1)
        else:
            half = next(iter(cotangents.values())).shape[0] // 2
            (value,) = step(
                lambda: (),
                "stack",
                [],
                stacks=[[view.part(half, 2 * half) for view in cotangents.values()]],
                ids=ids,
            )
            cotangents = {key: view.part(0, half) for key, view in cotangents.items()}
        got = partner(value, "sub", 1 << stage)
        half = cotangents[0].shape[0]
        for place_at, key in enumerate(list(cotangents)):
            cotangents[key ^ (1 << stage)] = View(got, (place_at * half, (place_at + 1) * half))
    near2 = after(near2, value)
    gather.exchange(0, near2)
    gather.relay(depth, depth - 1, term1)
    (pair,) = fused(pair_product, "pair_product", term2, near2)
    far_pair = partner(pair, "rep", 2)
    first_map = gather.weight(0)
    far_pair = after(far_pair, gather.held[1][3][0])

    packed = [gather.relay(depth, stage, first_map) for stage in reversed(range(1, depth - 1))]
    far_pair = after(far_pair, *packed)

    weights, messages, own_ups, other_ups = [], [], [], []
    for level in range(depth):
        if level == 1:
            for later in range(1, depth):
                gather.exchange(later, own_ups[0])
            weights += [gather.weight(later) for later in range(1, depth)]
            weights[1] = after(weights[1], weights[2])
        if level == 0:
            weights.append(first_map)
            outs = fused(mid_forward, "mid_forward", term0, near0, far_pair, weights[0])
        else:
            outs = fused(up_forward, "up_forward", own_ups[-1], other_ups[-1], weights[level])
        messages.append(outs[0])
        own_ups.append(outs[1])
        other_ups.append(partner(outs[2], "sub", 1 << level))
        if level == 0:
            early = partner(after(messages[0], other_ups[0]), "sub", 1)
        if level == 1:
            other_ups[1] = after(other_ups[1], early)
    gather.exchange(depth, other_ups[-1])
    (root,) = fused(top_forward, "top_forward", own_ups[-1], other_ups[-1])

    turns = [[[View(message)], []] for message in messages]

    def gather_turns(stage, value, levels):
        got = partner(value, "sub", 1 << stage)
        at = 0
        for level in levels:
            count = sum(view.shape[0] for view in turns[level][0])
            turns[level][0 if level > stage else 1].append(View(got, (at, at + count)))
            at += count
            if stage < level < depth:
                turns[level][1].append(View(got, (at, at + count)))
                at += count

    def to_stack(stage, levels):
        return [
            view
            for level in levels
            for view in turns[level][0] + (turns[level][1] if stage < level < depth else [])
        ]

    def stack_turns(stage, levels):
        (value,) = step(lambda: (), "stack", [], stacks=[to_stack(stage, levels)], ids=ids)
        gather_turns(stage, value, levels)

    turns[0][1].append(View(early))
    for level in range(1, depth):
        gather_turns(level, after(messages[level], own_ups[level]), [level])
    for stage in reversed(range(2, depth - 1)):
        stack_turns(stage, range(stage + 1, depth))

    head_maps = gather.head(head_left, head_right)
    root_high = partner(root, "sub", 1)
    root, grad_value, grad_gate, grad_msg, give, value = step(
        head_body,
        "head",
        [root, root_high, head_maps],
        parts=[cotangents[2 * i] for i in range(sub_count // 2)],
        stacks=[to_stack(1, range(2, depth))],
        ids=ids,
        limit=12,
    )
    got = partner(give, "sub", 1)
    gather_turns(1, value, range(2, depth))
    turns.append([[View(root)], []])
    gather_turns(depth - 1, root, [depth])
    low, high, value, root_value = step(
        top_back,
        "top_back",
        [own_ups[-1], other_ups[-1], grad_msg, got],
        stacks=[to_stack(0, range(1, depth)), to_stack(depth - 2, [depth])],
        ids=ids,
    )
    gather_turns(0, value, range(1, depth))
    gather_turns(depth - 2, root_value, [depth])
    for stage in reversed(range(1, depth - 2)):
        stack_turns(stage, [depth])
    turns[depth][1] = turns[depth][0]
    first_inputs = turns[0][0] + turns[0][1] + turns[depth][0]
    second_inputs = [view for entry in turns[1:depth] for turn in entry for view in turn]

    lows, highs = [None] * depth, [None] * depth
    lows[-1], highs[-1] = low, partner(high, "sub", 1 << (depth - 1))
    columns = [None] * depth + [[View(grad_value)], [View(grad_gate)]]

    def groups_of(stage):
        return [
            [View(lows[level]), View(highs[level])] if columns[level] is None else columns[level]
            for level in range(stage, depth)
        ]

    def spread(stage, keeps, send):
        got = partner(send, "sub", 1 << stage)
        at = 0
        for level, keep in zip(range(stage, depth + 2), keeps):
            span = keep.shape[1]
            columns[level] = [View(keep), View(got, None, (at, at + span))]
            at += span

    def columns_of(level, turn):
        if level == depth:
            return columns[depth + turn]
        if level == 0:
            return [columns[0][turn]]
        count = rows >> level
        return [
            view.part(i * count, (i + 1) * count)
            for view in columns[level]
            for i in range(turn, view.shape[0] // count, 2)
        ]

    far_got = []
    for level in reversed(range(depth - 1)):
        above = level + 1
        far = {depth - 2: first_inputs, 0: second_inputs}.get(level)
        low, high, *rest = step(
            down_back,
            "down_back",
            [own_ups[level], other_ups[level], weights[above], lows[above], highs[above]],
            halves=groups_of(above),
            fixed=columns[depth:],
            level=above,
            far=far,
            ids=ids,
            limit=12,
        )
        lows[level] = low
        highs[level] = partner(high, "sub", 1 << level)
        if far:
            far_got.append(partner(rest.pop(), "rep", 2))
        spread(above, rest[:-1], rest[-1])

    lows[0] = after(lows[0], far_got[0])
    back0, back1, pair_back, *rest = step(
        mid_back,
        "mid_back",
        [term0, near0, far_pair, weights[0], lows[0], highs[0]],
        halves=groups_of(0),
        level=0,
        ids=ids,
        limit=12,
    )
    back1 = partner(back1, "rep", 1)
    pair_back = partner(pair_back, "rep", 2)
    spread(0, rest[:-1], rest[-1])
    first = leaf_first(placed[:2], [back0, back1], leaf_w, mid_w)
    groups = [
        [view for turn in range(2) for view in columns_of(level, turn)]
        for level in range(depth + 1)
    ]
    groups[0][0] = groups[0][0].gated(first)
    own_grads = side_by_side(groups)
    far_grads = partner(own_grads, "rep", 2)
    near_grads = partner(own_grads, "rep", 1)
    back2, back3 = fused(far_back, "far_back", after(pair_back, own_grads), term2, near2)
    back3 = partner(back3, "rep", 1)
    inputs = first_inputs + second_inputs
    near_got = partner(near_inputs([inputs[0].gated(back2)] + inputs[1:], far_got, ids), "rep", 1)
    leaf_grad, mid_grad = leaf_backward(
        placed, [msg0, msg1, msg2, msg3], [back0, back1, back2, back3], leaf_w, mid_w, first
    )
    grads = [own_grads, far_grads, near_grads]
    grads.append(partner(after(far_grads, leaf_grad), "rep", 1))
    upper = upper_grads(turns, far_got, near_got, grads, ids)
    return leaf_grad[None], mid_grad[None, None], upper[None]


def solution(mesh):
    placed = (
        P("rep", "sub", None),
        P("sub"),
        P(("sub", "rep"), None, None, None),
        P("sub", "rep", None, None),
        P("sub", None, None, None),
        P("rep", "sub"),
    )
    return jax.shard_map(
        on_device,
        mesh=mesh,
        in_specs=placed,
        out_specs=(
            P(("sub", "rep"), None, None, None),
            P("sub", "rep", None, None),
            P("sub", "rep", None, None),
        ),
        check_vma=False,
    )
```

```python
import functools

import jax
import jax.numpy as jnp
from jax import lax
from jax.experimental import pallas as pl
from jax.experimental.pallas import tpu as pltpu
from jax.sharding import PartitionSpec as P

EPSILON = 1e-06
CHILDREN = 4
MIB = 1024 * 1024


def partner(value, axis, offset):
    return lax.ppermute(value, axis, [(i, i ^ offset) for i in range(lax.axis_size(axis))])


def rms_factor(values):
    return lax.rsqrt(jnp.mean(values * values, axis=-1, keepdims=True) + EPSILON)


def norm_back(gradient, normed, factor):
    return factor * (gradient - normed * jnp.mean(gradient * normed, axis=-1, keepdims=True))


def matmul(left_arr, right_arr):
    return jnp.dot(left_arr, right_arr, preferred_element_type=jnp.float32)


def matmul_t(left_arr, right_arr):
    return lax.dot_general(
        left_arr, right_arr, (((1,), (1,)), ((), ())), preferred_element_type=jnp.float32
    )


def inner_t(left_arr, right_arr):
    return lax.dot_general(
        left_arr, right_arr, (((0,), (0,)), ((), ())), preferred_element_type=jnp.float32
    )


def bf16(value):
    return value.astype(jnp.bfloat16)


def f32(value):
    return value.astype(jnp.float32)


def whole_block():
    return pl.BlockSpec(memory_space=pltpu.VMEM)


def smem_block():
    return pl.BlockSpec(memory_space=pltpu.SMEM)


def bit_of(value, level):
    return jnp.bitwise_and(jnp.right_shift(value, level), 1)


def place_kernel(slots, depth, ids_ref, map_ref, regions_ref, cotangent_ref, *rest):
    outs, keep_ref, send_ref, wide = rest[:CHILDREN], *rest[CHILDREN:]
    rows = regions_ref.shape[0] // slots
    parts = wide.shape[0]
    for part in range(parts):
        wide[part] = regions_ref[:, part * 128 : (part + 1) * 128].astype(jnp.float32)
    flip = 0
    for level in range(depth):
        flip = flip + bit_of(ids_ref[0], level) * (rows >> (level + 1))
    row = lax.broadcasted_iota(jnp.int32, (rows, rows), 0)
    col = lax.broadcasted_iota(jnp.int32, (rows, rows), 1)
    select = bf16(jnp.bitwise_xor(row, flip) == col)
    block = rows >> depth
    wanted = jnp.bitwise_and(row, block - 1)
    for level in range(depth):
        wanted = wanted + bit_of(row // block, level) * (block << (depth - 1 - level))
    pick = bf16(jnp.bitwise_xor(wanted, flip) == col)
    left = cotangent_ref[...]
    picked = 0.0
    for _ in range(3):
        top = bf16(left)
        left = left - f32(top)
        picked = picked + matmul(pick, top)
    keep_ref[...] = picked[: rows // 2]
    send_ref[...] = picked[rows // 2 :]
    for offset in range(CHILDREN):
        node = jnp.bitwise_xor(ids_ref[1], offset)
        for child in range(CHILDREN):
            region = map_ref[node * CHILDREN + child]
            for part in range(parts):
                values = bf16(wide[part, pl.ds(region, rows, stride=slots), :])
                outs[offset][child, :, part * 128 : (part + 1) * 128] = bf16(
                    matmul(select, values)
                )


def place(regions, leaf_map, cotangent, ids, depth):
    rows, slots, feats = regions.shape
    flat = regions.reshape(rows * slots, feats)
    return pl.pallas_call(
        functools.partial(place_kernel, slots, depth),
        out_shape=[jax.ShapeDtypeStruct((CHILDREN, rows, feats), jnp.bfloat16)] * CHILDREN
        + [jax.ShapeDtypeStruct((rows // 2, cotangent.shape[1]), cotangent.dtype)] * 2,
        in_specs=[smem_block(), smem_block(), whole_block(), whole_block()],
        out_specs=[whole_block()] * (CHILDREN + 2),
        scratch_shapes=[pltpu.VMEM((feats // 128, rows * slots, 128), jnp.float32)],
        compiler_params=pltpu.CompilerParams(vmem_limit_bytes=7 * MIB),
        name="place",
    )(ids, leaf_map, flat, cotangent)


def leaf_forward_kernel(count, *refs):
    placed, leaf_w, mid_w = refs[:count], refs[count], refs[count + 1]
    msgs, terms = refs[count + 2 : 2 * count + 2], refs[2 * count + 2 :]
    rows = placed[0].shape[1]
    product = None
    for child in range(CHILDREN):
        values = jnp.concatenate([ref[child] for ref in placed], axis=0)
        factor = 1.0 + matmul(values, leaf_w[child])
        product = factor if product is None else product * factor
    message = bf16(product * rms_factor(product))
    out = bf16(matmul(message, mid_w[...]))
    for i in range(count):
        msgs[i][...] = message[i * rows : (i + 1) * rows]
        terms[i][...] = out[i * rows : (i + 1) * rows]


def leaf_forward(placed, leaf_w, mid_w):
    count = len(placed)
    rows = placed[0].shape[1]
    width = mid_w.shape[0]
    return pl.pallas_call(
        functools.partial(leaf_forward_kernel, count),
        out_shape=[jax.ShapeDtypeStruct((rows, width), jnp.bfloat16)] * (2 * count),
        in_specs=[whole_block()] * (count + 2),
        out_specs=[whole_block()] * (2 * count),
        compiler_params=pltpu.CompilerParams(vmem_limit_bytes=14 * MIB),
        name="leaf_forward",
    )(*placed, leaf_w, mid_w)


def leaf_cotangents(placed, grads, leaf_w, mid_w):
    factors = [
        1.0 + matmul(jnp.concatenate([ref[child] for ref in placed], axis=0), leaf_w[child])
        for child in range(CHILDREN)
    ]
    low = factors[0] * factors[1]
    high = factors[2] * factors[3]
    product = low * high
    scale = rms_factor(product)
    back = matmul_t(jnp.concatenate([ref[...] for ref in grads], axis=0), mid_w[...])
    node = norm_back(back, product * scale, scale)
    high, low = node * high, node * low
    return [
        bf16(high * factors[1]),
        bf16(high * factors[0]),
        bf16(low * factors[3]),
        bf16(low * factors[2]),
    ]


def leaf_first_kernel(*refs):
    placed, grads, leaf_w, mid_w, out = refs[0:2], refs[2:4], refs[4], refs[5], refs[6]
    for child, value in enumerate(leaf_cotangents(placed, grads, leaf_w, mid_w)):
        out[child] = value


def leaf_first(placed, grads, leaf_w, mid_w):
    rows = placed[0].shape[1]
    return pl.pallas_call(
        leaf_first_kernel,
        out_shape=jax.ShapeDtypeStruct((CHILDREN, 2 * rows, mid_w.shape[0]), jnp.bfloat16),
        in_specs=[whole_block()] * 6,
        out_specs=whole_block(),
        compiler_params=pltpu.CompilerParams(vmem_limit_bytes=18 * MIB),
        name="leaf_first",
    )(*placed, *grads, leaf_w, mid_w)


def leaf_backward_kernel(*refs):
    placed, msgs, grads = refs[0:4], refs[4:8], refs[8:12]
    leaf_w, mid_w, first, leaf_out, mid_out = refs[12:17]
    all_grads = jnp.concatenate([ref[...] for ref in grads], axis=0)
    all_msgs = jnp.concatenate([ref[...] for ref in msgs], axis=0)
    mid_out[...] = bf16(inner_t(all_msgs, all_grads))
    second = leaf_cotangents(placed[2:], grads[2:], leaf_w, mid_w)
    for child in range(CHILDREN):
        values = jnp.concatenate([ref[child] for ref in placed], axis=0)
        cot = jnp.concatenate([first[child], second[child]], axis=0)
        leaf_out[child] = bf16(inner_t(values, cot))


def leaf_backward(placed, msgs, grads, leaf_w, mid_w, first):
    return pl.pallas_call(
        leaf_backward_kernel,
        out_shape=[
            jax.ShapeDtypeStruct(leaf_w.shape, jnp.bfloat16),
            jax.ShapeDtypeStruct(mid_w.shape, jnp.bfloat16),
        ],
        in_specs=[whole_block()] * 15,
        out_specs=[whole_block()] * 2,
        compiler_params=pltpu.CompilerParams(vmem_limit_bytes=30 * MIB),
        name="leaf_backward",
    )(*placed, *msgs, *grads, leaf_w, mid_w, first)


def fused(body, name, *args, limit=8, ids=None, plain=False):
    if plain or any(arg.shape[-2] % 16 or arg.shape[-1] % 128 for arg in args):
        return body(*args) if ids is None else body(ids, *args)
    count = len(args)
    if ids is None:
        shapes = jax.eval_shape(body, *args)
    else:
        shapes = jax.eval_shape(body, ids, *args)
        args = (ids, *args)

    def kernel(*refs):
        outs = refs[len(args) :]
        values = [ref[...] for ref in refs[len(args) - count : len(args)]]
        results = body(*values) if ids is None else body(refs[0], *values)
        for ref, result in zip(outs, results):
            ref[...] = result

    return pl.pallas_call(
        kernel,
        out_shape=shapes,
        in_specs=[smem_block()] * (len(args) - count) + [whole_block()] * count,
        out_specs=[whole_block()] * len(shapes),
        compiler_params=pltpu.CompilerParams(vmem_limit_bytes=limit * MIB),
        name=name,
    )(*args)


def join(pieces):
    if pieces[0].shape[0] % 16 == 0:
        return jnp.concatenate(pieces, axis=0)
    wide = lax.optimization_barrier(tuple(f32(piece) for piece in pieces))
    return bf16(lax.optimization_barrier(jnp.concatenate(wide, axis=0)))


def pack(pieces):
    arrays = []
    for array, _, _ in pieces:
        if not any(array is known for known in arrays):
            arrays.append(array)
    spots = [next(i for i, known in enumerate(arrays) if known is piece[0]) for piece in pieces]

    def body(*values):
        parts = [values[i][:, at : at + span] for i, (_, at, span) in zip(spots, pieces)]
        return (jnp.concatenate(parts, axis=1),)

    if any(piece[2] % 128 for piece in pieces):
        return body(*arrays)[0]
    return fused(body, "pack", *arrays, limit=6)[0]


def cut_kernel(depth, ids_ref, maps_ref, *refs):
    outs, split = refs[:-1], refs[-1]
    split[...] = jnp.swapaxes(maps_ref[...], 0, 1)
    width = maps_ref.shape[0]
    half = width // 2
    rows = pl.ds(pl.multiple_of(bit_of(ids_ref[1], 0) * half, half), half)
    for level in range(depth):
        span = width >> (level + 1)
        cols = pl.ds(width - 2 * span, span)
        side = bit_of(ids_ref[0], level)
        outs[3 * level][...] = split[side, :, cols]
        outs[3 * level + 1][...] = split[side, rows, cols]
        outs[3 * level + 2][...] = split[1 - side, rows, cols]
    span = width >> depth
    for side in range(2):
        outs[3 * depth + side][...] = split[side, :, width - span :]
        outs[3 * depth + 2][:, side * span : (side + 1) * span] = split[side, rows, width - span :]


def cut_maps(maps, ids, depth):
    width = maps.shape[0]
    half = width // 2
    spans = [width >> (level + 1) for level in range(depth)]
    if spans[-1] % 128 == 0:
        shapes = []
        for span in spans:
            shapes += [(width, span), (half, span), (half, span)]
        shapes += [(width, spans[-1])] * 2 + [(half, 2 * spans[-1])]
        outs = pl.pallas_call(
            functools.partial(cut_kernel, depth),
            out_shape=[jax.ShapeDtypeStruct(shape, maps.dtype) for shape in shapes],
            in_specs=[smem_block(), whole_block()],
            out_specs=[whole_block()] * len(shapes),
            scratch_shapes=[pltpu.VMEM((2, width, width), maps.dtype)],
            compiler_params=pltpu.CompilerParams(vmem_limit_bytes=18 * MIB),
            name="cut_maps",
        )(ids, maps)
    else:
        maps = jnp.transpose(maps, (1, 0, 2))
        outs = []
        core = bit_of(ids[1], 0)
        for level, span in enumerate(spans):
            side = bit_of(ids[0], level)
            first = width - 2 * span
            outs.append(lax.dynamic_slice(maps, (side, 0, first), (1, width, span))[0])
            for which in (side, 1 - side):
                outs.append(lax.dynamic_slice(maps, (which, core * half, first), (1, half, span))[0])
        outs += [maps[0, :, width - spans[-1] :], maps[1, :, width - spans[-1] :]]
        both = jnp.concatenate(outs[-2:], axis=1)
        outs.append(lax.dynamic_slice_in_dim(both, core * half, half, 0))
    return [outs[3 * i : 3 * i + 3] for i in range(depth)], outs[3 * depth :]


def assemble_kernel(spots, count, ids_ref, own_ref, *refs):
    out_ref = refs[-1]
    width, span = own_ref.shape
    half = width // 2
    block = jnp.bitwise_and(ids_ref[0], out_ref.shape[1] // span - 1)
    own_core = bit_of(ids_ref[1], 0)
    out_ref[:, pl.ds(pl.multiple_of(block * span, span), span)] = own_ref[...]
    for offset, index, at in spots:
        col = jnp.bitwise_xor(block, offset) * span
        for ref, core in ((refs[index], own_core), (refs[count + index], 1 - own_core)):
            out_ref[
                pl.ds(pl.multiple_of(core * half, half), half),
                pl.ds(pl.multiple_of(col, span), span),
            ] = ref[:, at : at + span]


def assemble(own, pieces, ids):
    width, span = own.shape
    count = len(pieces) + 1
    if span % 128 == 0:
        mine, other, spots = [], [], []
        for offset, (near_half, far_half, at) in pieces.items():
            known = [i for i, array in enumerate(mine) if array is near_half]
            if not known:
                mine.append(near_half)
                other.append(far_half)
                known = [len(mine) - 1]
            spots.append((offset, known[0], at))
        return pl.pallas_call(
            functools.partial(assemble_kernel, spots, len(mine)),
            out_shape=jax.ShapeDtypeStruct((width, span * count), own.dtype),
            in_specs=[smem_block()] + [whole_block()] * (2 * len(mine) + 1),
            out_specs=whole_block(),
            compiler_params=pltpu.CompilerParams(vmem_limit_bytes=8 * MIB),
            name="assemble",
        )(ids, own, *mine, *other)
    block = jnp.bitwise_and(ids[0], count - 1)
    core = bit_of(ids[1], 0)
    out = jnp.zeros((width, span * count), own.dtype)
    out = lax.dynamic_update_slice(out, own, (0, block * span))
    for offset, (near_half, far_half, at) in pieces.items():
        col = (block ^ offset) * span
        for array, which in ((near_half, core), (far_half, 1 - core)):
            part = array[:, at : at + span]
            out = lax.dynamic_update_slice(out, part, (which * (width // 2), col))
    return out


def assemble_head_kernel(spots, count, ids_ref, left_ref, right_ref, *refs):
    out_ref = refs[-1]
    width, span = left_ref.shape
    half, total = width // 2, out_ref.shape[1] // 2
    out_ref[:, :span] = left_ref[...]
    out_ref[:, total : total + span] = right_ref[...]
    own_core = bit_of(ids_ref[1], 0)
    for offset, index, at in spots:
        for ref, core in ((refs[index], own_core), (refs[count + index], 1 - own_core)):
            rows = pl.ds(pl.multiple_of(core * half, half), half)
            for side in range(2):
                col = side * total + (offset // 2) * span
                out_ref[rows, col : col + span] = ref[:, at + side * span : at + (side + 1) * span]


def assemble_head(left, right, pieces, ids):
    width, span = left.shape
    total = span * (len(pieces) + 1)
    mine, other, spots = [], [], []
    for offset, (near_half, far_half, at) in pieces.items():
        known = [i for i, array in enumerate(mine) if array is near_half]
        if not known:
            mine.append(near_half)
            other.append(far_half)
            known = [len(mine) - 1]
        spots.append((offset, known[0], at))
    if span % 128 == 0:
        return pl.pallas_call(
            functools.partial(assemble_head_kernel, spots, len(mine)),
            out_shape=jax.ShapeDtypeStruct((width, 2 * total), left.dtype),
            in_specs=[smem_block()] + [whole_block()] * (2 * len(mine) + 2),
            out_specs=whole_block(),
            compiler_params=pltpu.CompilerParams(vmem_limit_bytes=8 * MIB),
            name="assemble_head",
        )(ids, left, right, *mine, *other)
    core = bit_of(ids[1], 0)
    out = jnp.zeros((width, 2 * total), left.dtype)
    out = lax.dynamic_update_slice(out, left, (0, 0))
    out = lax.dynamic_update_slice(out, right, (0, total))
    for offset, index, at in spots:
        for array, which in ((mine[index], core), (other[index], 1 - core)):
            for side in range(2):
                part = array[:, at + side * span : at + (side + 1) * span]
                col = side * total + (offset // 2) * span
                out = lax.dynamic_update_slice(out, part, (which * (width // 2), col))
    return out


def after(value, *others):
    return lax.optimization_barrier((value, *others))[0]


class MapGather:
    def __init__(self, blocks, head_half, ids):
        self.blocks, self.ids = blocks + [(None, head_half, None)], ids
        self.depth = len(blocks)
        blocks = self.blocks
        self.spans = [block[1].shape[1] for block in blocks]
        self.held = [{0: (block[1], 0)} for block in blocks]
        self.other = {}
        pieces = [(blocks[0][2], 0, self.spans[0])]
        pieces += [(blocks[i][1], 0, self.spans[i]) for i in range(1, self.depth)]
        self.first = pack(pieces)
        got = partner(self.first, "sub", 1)
        self.received = got
        at = 0
        for level in range(self.depth):
            self.held[level][1] = (got, at)
            at += self.spans[level]

    def relay(self, level, stage, gate=None):
        if stage == level:
            offsets, value = [0], self.blocks[level][2]
            if gate is not None:
                value = after(value, gate)
        else:
            offsets = [i for i in self.held[level] if i % (2 << stage) == 0]
            if stage == 0:
                offsets = [i for i in offsets if i > 0]
            pieces = [(*self.held[level][i], self.spans[level]) for i in offsets]
            if gate is not None:
                pieces[-1] = (after(pieces[-1][0], gate), *pieces[-1][1:])
            if len(pieces) == 1 and pieces[0][0].shape[1] == pieces[0][2]:
                value = pieces[0][0]
            else:
                value = pack(pieces)
            if 0 not in offsets:
                for place, offset in enumerate(offsets):
                    self.held[level][offset] = (value, place * self.spans[level])
        got = partner(value, "sub", 1 << stage)
        for place, offset in enumerate(offsets):
            self.held[level][offset ^ (1 << stage)] = (got, place * self.spans[level])
        return value

    def exchange(self, level, gate):
        for offset, (array, _) in self.held[level].items():
            if offset > 0 and id(array) not in self.other:
                self.other[id(array)] = (array, partner(after(array, gate), "rep", 1))

    def head(self, left, right):
        return assemble_head(left, right, self.pieces(self.depth), self.ids)

    def weight(self, level):
        return assemble(self.blocks[level][0], self.pieces(level), self.ids)

    def pieces(self, level):
        pieces = {}
        for offset, (array, at) in self.held[level].items():
            if offset > 0:
                pieces[offset] = (array, self.other[id(array)][1], at)
        return pieces


class View:
    def __init__(self, array, rows=None, cols=None):
        self.array = array
        self.rows = (0, array.shape[0]) if rows is None else rows
        self.cols = (0, array.shape[1]) if cols is None else cols
        self.shape = (self.rows[1] - self.rows[0], self.cols[1] - self.cols[0])

    def value(self):
        return self.array[slice(*self.rows), slice(*self.cols)]

    def part(self, first, last):
        return View(self.array, (self.rows[0] + first, self.rows[0] + last), self.cols)

    def gated(self, *gates):
        return View(after(self.array, *gates), self.rows, self.cols)

    def aligned(self):
        edges = (*self.rows, *self.cols)
        return all(edge % unit == 0 for edge, unit in zip(edges, (16, 16, 128, 128)))


def spots_of(views):
    arrays, spots = [], []
    for view in views:
        known = [i for i, array in enumerate(arrays) if array is view.array]
        if not known:
            arrays.append(view.array)
            known = [len(arrays) - 1]
        spots.append((known[0], view.rows, view.cols))
    return arrays, spots


def join_all(pieces):
    if len(pieces) == 1:
        return pieces[0]
    if pieces[0].dtype == jnp.float32 or all(piece.shape[0] % 16 == 0 for piece in pieces):
        return jnp.concatenate(pieces, axis=0)
    wide = lax.optimization_barrier(tuple(f32(piece) for piece in pieces))
    return bf16(lax.optimization_barrier(jnp.concatenate(wide, axis=0)))


def step(body, name, args, parts=(), stacks=(), halves=(), fixed=(), level=0, far=None, **options):
    groups = [[view] for view in parts] + [list(group) for group in stacks]
    halved = [list(group) for group in (*halves, *fixed)]
    views = [view for group in (*groups, *halved, far or ()) for view in group]
    arrays = list(args)
    for view in views:
        if not any(array is view.array for array in arrays):
            arrays.append(view.array)

    def cut(values, group):
        pieces = []
        for view in group:
            index = next(i for i, array in enumerate(arrays) if array is view.array)
            pieces.append(values[index][slice(*view.rows), slice(*view.cols)])
        return join_all(pieces)

    def whole(ids, *values):
        given = [cut(values, group) for group in groups[: len(parts)]]
        results = list(body(*values[: len(args)], *given))
        results += [cut(values, group) for group in groups[len(parts) :]]
        sends = []
        for index, group in enumerate(halved):
            full = cut(values, group)
            half = full.shape[1] // 2
            low, high = full[:, :half], full[:, half:]
            if index < len(halves):
                own = bit_of(ids[0], level) == 1
                low, high = jnp.where(own, high, low), jnp.where(own, low, high)
            results.append(low)
            sends.append(high)
        if sends:
            results.append(jnp.concatenate(sends, axis=1))
        if far:
            full = cut(values, far)
            half = full.shape[1] // 2
            results.append(jnp.where(bit_of(ids[1], 1) == 1, full[:, :half], full[:, half:]))
        return results

    plain = not all(view.aligned() for view in views)
    return fused(whole, name, *arrays, plain=plain, **options)


def near_inputs_kernel(spots, ids_ref, first_ref, second_ref, *refs):
    out_ref = refs[-1]
    quarter = out_ref.shape[1]
    other = 1 - bit_of(ids_ref[1], 0)
    lanes = pl.ds(pl.multiple_of((bit_of(ids_ref[1], 1) * 2 + other) * quarter, quarter), quarter)
    at = 0
    for index, (first, last), _ in spots:
        out_ref[at : at + last - first] = refs[index][first:last, lanes]
        at += last - first
    for ref in (first_ref, second_ref):
        count = ref.shape[0]
        lanes = pl.ds(pl.multiple_of(other * quarter, quarter), quarter)
        out_ref[at : at + count] = ref[:, lanes]
        at += count


def near_inputs(views, got, ids):
    quarter = views[0].shape[1] // 4
    if not all(view.aligned() for view in views):
        full = join_all([view.value() for view in views])
        other = 1 - bit_of(ids[1], 0)
        where = (bit_of(ids[1], 1) * 2 + other) * quarter
        own = lax.dynamic_slice_in_dim(full, where, quarter, 1)
        far = jnp.concatenate(got, axis=0)
        return jnp.concatenate(
            [own, lax.dynamic_slice_in_dim(far, other * quarter, quarter, 1)], axis=0
        )
    arrays, spots = spots_of(views)
    return pl.pallas_call(
        functools.partial(near_inputs_kernel, spots),
        out_shape=jax.ShapeDtypeStruct(
            (2 * sum(array.shape[0] for array in got), quarter), jnp.bfloat16
        ),
        in_specs=[smem_block()] + [whole_block()] * (len(arrays) + 2),
        out_specs=whole_block(),
        compiler_params=pltpu.CompilerParams(vmem_limit_bytes=8 * MIB),
        name="near_inputs",
    )(ids, *got, *arrays)


def side_by_side_kernel(groups, *refs):
    out_ref = refs[-1]
    col = 0
    for spots in groups:
        at = 0
        for index, rows, cols in spots:
            span = cols[1] - cols[0]
            count = rows[1] - rows[0]
            out_ref[at : at + count, col : col + span] = refs[index][slice(*rows), slice(*cols)]
            at += count
        col += span


def side_by_side(groups):
    views = [view for group in groups for view in group]
    if not all(view.aligned() for view in views):
        return jnp.concatenate(
            [join_all([view.value() for view in group]) for group in groups], axis=1
        )
    arrays, spots = spots_of(views)
    by_group = [[spots.pop(0) for _ in group] for group in groups]
    shape = (
        sum(view.shape[0] for view in groups[0]),
        sum(group[0].shape[1] for group in groups),
    )
    return pl.pallas_call(
        functools.partial(side_by_side_kernel, by_group),
        out_shape=jax.ShapeDtypeStruct(shape, jnp.bfloat16),
        in_specs=[whole_block()] * len(arrays),
        out_specs=whole_block(),
        compiler_params=pltpu.CompilerParams(vmem_limit_bytes=6 * MIB),
        name="side_by_side",
    )(*arrays)


def upper_grads_kernel(spots, spans, rows, ids_ref, first_ref, second_ref, near_ref, *refs):
    grads, inputs, out_ref, both = refs[:4], refs[4:-2], refs[-2], refs[-1]
    quarter = out_ref.shape[0]
    core, far = bit_of(ids_ref[1], 0), bit_of(ids_ref[1], 1)
    lanes = pl.ds(pl.multiple_of((far * 2 + core) * quarter, quarter), quarter)
    far_lanes = pl.ds(pl.multiple_of(core * quarter, quarter), quarter)
    total = first_ref.shape[0] + second_ref.shape[0]
    col = 0
    for level, span in enumerate(spans):
        for turn in range(2):
            here, at = spots[level][turn]
            pieces = [inputs[i][slice(*edges), lanes] for i, edges, _ in here]
            if at < first_ref.shape[0]:
                pieces.append(first_ref[at : at + rows, far_lanes])
            else:
                there = at - first_ref.shape[0]
                pieces.append(second_ref[there : there + rows, far_lanes])
            pieces.append(near_ref[at : at + rows])
            pieces.append(near_ref[total + at : total + at + rows])
            grad = jnp.concatenate(
                [ref[turn * rows : (turn + 1) * rows, col : col + span] for ref in grads], axis=0
            )
            value = bf16(inner_t(jnp.concatenate(pieces, axis=0), grad))
            side = turn
            if level < len(spans) - 1:
                side = jnp.bitwise_xor(bit_of(ids_ref[0], level), turn)
            both[side, :, col : col + span] = value
        col += span
    out_ref[...] = jnp.swapaxes(both[...], 0, 1)


def upper_grads(entries, far_got, near_got, grads, ids):
    depth = len(entries) - 1
    width = entries[0][0][0].shape[1]
    rows = sum(view.shape[0] for view in entries[0][0])
    spans = [width >> (level + 1) for level in range(depth)] + [width >> depth]
    views = [view for entry in entries for turn in entry for view in turn]
    starts = [[0, rows]]
    starts += [[(2 * level + 1) * rows, (2 * level + 2) * rows] for level in range(1, depth)]
    starts.append([2 * rows, 2 * rows])
    if all(view.aligned() for view in views) and spans[-1] % 128 == 0:
        arrays, flat = spots_of(views)
        spots = [
            [([flat.pop(0) for _ in entry[turn]], starts[level][turn]) for turn in range(2)]
            for level, entry in enumerate(entries)
        ]
        return pl.pallas_call(
            functools.partial(upper_grads_kernel, spots, spans, rows),
            out_shape=jax.ShapeDtypeStruct((width // 4, 2, width), jnp.bfloat16),
            in_specs=[smem_block()] + [whole_block()] * (len(arrays) + 7),
            out_specs=whole_block(),
            scratch_shapes=[pltpu.VMEM((2, width // 4, width), jnp.bfloat16)],
            compiler_params=pltpu.CompilerParams(vmem_limit_bytes=16 * MIB),
            name="upper_grads",
        )(ids, *far_got, near_got, *grads, *arrays)
    quarter = width // 4
    core, far = bit_of(ids[1], 0), bit_of(ids[1], 1)
    far_got = jnp.concatenate(far_got, axis=0)
    total = far_got.shape[0]
    parts, col = [], 0
    for level, span in enumerate(spans):
        both = []
        for turn in range(2):
            at = starts[level][turn]
            own = join_all([view.value() for view in entries[level][turn]])
            pieces = [
                lax.dynamic_slice_in_dim(own, (far * 2 + core) * quarter, quarter, 1),
                lax.dynamic_slice_in_dim(far_got[at : at + rows], core * quarter, quarter, 1),
                near_got[at : at + rows],
                near_got[total + at : total + at + rows],
            ]
            grad = [part[turn * rows : (turn + 1) * rows, col : col + span] for part in grads]
            both.append(bf16(inner_t(jnp.concatenate(pieces), jnp.concatenate(grad))))
        if level < depth:
            swap = bit_of(ids[0], level) == 1
            both = [jnp.where(swap, both[1 - i], both[i]) for i in range(2)]
        parts.append(jnp.stack(both, axis=1))
        col += span
    return jnp.concatenate(parts, axis=2)


def mid_forward(term, near, far, weight):
    product = (1.0 + f32(term)) * (1.0 + f32(near)) * f32(far)
    return up_product(bf16(product * rms_factor(product)), weight)


def up_product(message, weight):
    up = matmul(message, weight)
    keep = up.shape[0] // 2
    return message, up[:keep], bf16(up[keep:])


def up_forward(own_up, other_up, weight):
    joined = (1.0 + own_up) * (1.0 + f32(other_up))
    return up_product(bf16(joined * rms_factor(joined)), weight)


def top_forward(own_up, other_up):
    joined = (1.0 + own_up) * (1.0 + f32(other_up))
    return (bf16(joined * rms_factor(joined)),)


def head_body(low, high, maps, *cotangents):
    root = join([low, high])
    cotangent = jnp.concatenate(cotangents, axis=1)
    half = maps.shape[1] // 2
    both = matmul(root, maps)
    value, gating = both[:, :half], jax.nn.sigmoid(both[:, half:])
    grad_value = bf16(cotangent * gating)
    grad_gate = bf16(cotangent * value * gating * (1.0 - gating))
    back = matmul_t(grad_value, maps[:, :half]) + matmul_t(grad_gate, maps[:, half:])
    rows = root.shape[0] // 2
    return root, grad_value, grad_gate, back[:rows], bf16(back[rows:])


def level_back(grad_msg, own_up, other_up):
    own_up, other_up = 1.0 + own_up, 1.0 + f32(other_up)
    joined = own_up * other_up
    scaling = rms_factor(joined)
    grad = norm_back(grad_msg, joined * scaling, scaling)
    return bf16(grad * other_up), bf16(grad * own_up)


def top_back(own_up, other_up, own_part, got):
    return level_back(own_part + f32(got), own_up, other_up)


def down_back(own_up, other_up, weight, low, high):
    return level_back(matmul_t(join([low, high]), weight), own_up, other_up)


def mid_back(term, near, far, weight, low, high):
    own, near, far = 1.0 + f32(term), 1.0 + f32(near), f32(far)
    pair = own * near
    product = pair * far
    scale = rms_factor(product)
    grad_msg = matmul_t(join([low, high]), weight)
    grad = norm_back(grad_msg, product * scale, scale)
    grad_pair = grad * far
    return bf16(grad_pair * near), bf16(grad_pair * own), bf16(grad * pair)


def far_back(grad_pair, term, near):
    grad_pair = f32(grad_pair)
    return bf16(grad_pair * (1.0 + f32(near))), bf16(grad_pair * (1.0 + f32(term)))


def pair_product(term, near):
    return (bf16((1.0 + f32(term)) * (1.0 + f32(near))),)


def on_device(regions, leaf_map, leaf_bond_weight, mid_weight, upper_weight, head_cotangent):
    rows = regions.shape[0]
    sub_count = lax.axis_size("sub")
    depth = sub_count.bit_length() - 1
    ids = jnp.stack([lax.axis_index("sub"), lax.axis_index("rep")]).astype(jnp.int32)
    leaf_w = leaf_bond_weight[0]
    mid_w = mid_weight[0, 0]

    blocks, (head_left, head_right, head_half) = cut_maps(upper_weight[0], ids, depth)
    gather = MapGather(blocks, head_half, ids)

    *sent, cotangent, cotangent_sent = place(after(regions, head_right), leaf_map, head_cotangent, ids, depth)
    near = partner(sent[1], "rep", 1)
    far_both = partner(sent[3], "rep", 3)
    far_one = partner(sent[2], "rep", 2)
    placed = [sent[0], near, far_one, far_both]
    for level in reversed(range(1, depth)):
        gather.relay(level, level, near)
    msg0, msg1, term0, term1 = leaf_forward(placed[:2], leaf_w, mid_w)
    near0 = partner(term1, "rep", 1)
    packed = []
    for level in range(2, depth):
        packed += [gather.relay(level, stage, term1) for stage in reversed(range(1, level))]
    far_placed = [after(far_one, term1, gather.held[1][2][0], *packed), far_both]
    msg2, msg3, term2, term3 = leaf_forward(far_placed, leaf_w, mid_w)
    near2 = partner(term3, "rep", 1)
    gather.relay(1, 0, term3)
    near2 = after(near2, *[gather.relay(level, 0, term1) for level in range(2, depth)])
    cotangents = {0: View(cotangent)}
    for stage in reversed(range(1, depth)):
        if stage == depth - 1:
            value = after(cotangent_sent, term1)
        else:
            half = next(iter(cotangents.values())).shape[0] // 2
            (value,) = step(
                lambda: (),
                "stack",
                [],
                stacks=[[view.part(half, 2 * half) for view in cotangents.values()]],
                ids=ids,
            )
            cotangents = {key: view.part(0, half) for key, view in cotangents.items()}
        got = partner(value, "sub", 1 << stage)
        half = cotangents[0].shape[0]
        for place_at, key in enumerate(list(cotangents)):
            cotangents[key ^ (1 << stage)] = View(got, (place_at * half, (place_at + 1) * half))
    near2 = after(near2, value)
    gather.exchange(0, near2)
    gather.relay(depth, depth - 1, term1)
    (pair,) = fused(pair_product, "pair_product", term2, near2)
    far_pair = partner(pair, "rep", 2)
    first_map = gather.weight(0)
    far_pair = after(far_pair, gather.held[1][3][0])

    weights, messages, own_ups, other_ups = [], [], [], []
    for level in range(depth):
        if level == 1:
            for later in range(1, depth):
                gather.exchange(later, own_ups[0])
            weights += [gather.weight(later) for later in range(1, depth)]
            last = reversed(range(1, depth - 1))
            packed = [gather.relay(depth, stage, other_ups[0]) for stage in last]
            weights[1] = after(weights[1], weights[2], *packed)
        if level == 0:
            weights.append(first_map)
            outs = fused(mid_forward, "mid_forward", term0, near0, far_pair, weights[0])
        else:
            outs = fused(up_forward, "up_forward", own_ups[-1], other_ups[-1], weights[level])
        messages.append(outs[0])
        own_ups.append(outs[1])
        other_ups.append(partner(outs[2], "sub", 1 << level))
        if level == 0:
            early = partner(after(messages[0], other_ups[0]), "sub", 1)
        if level == 1:
            other_ups[1] = after(other_ups[1], early)
    gather.exchange(depth, other_ups[-1])
    (root,) = fused(top_forward, "top_forward", own_ups[-1], other_ups[-1])

    turns = [[[View(message)], []] for message in messages]

    def gather_turns(stage, value, levels):
        got = partner(value, "sub", 1 << stage)
        at = 0
        for level in levels:
            count = sum(view.shape[0] for view in turns[level][0])
            turns[level][0 if level > stage else 1].append(View(got, (at, at + count)))
            at += count
            if stage < level < depth:
                turns[level][1].append(View(got, (at, at + count)))
                at += count

    def to_stack(stage, levels):
        return [
            view
            for level in levels
            for view in turns[level][0] + (turns[level][1] if stage < level < depth else [])
        ]

    def stack_turns(stage, levels):
        (value,) = step(lambda: (), "stack", [], stacks=[to_stack(stage, levels)], ids=ids)
        gather_turns(stage, value, levels)

    turns[0][1].append(View(early))
    for level in range(1, depth):
        gather_turns(level, after(messages[level], own_ups[level]), [level])
    for stage in reversed(range(2, depth - 1)):
        stack_turns(stage, range(stage + 1, depth))

    head_maps = gather.head(head_left, head_right)
    root_high = partner(root, "sub", 1)
    root, grad_value, grad_gate, grad_msg, give, value = step(
        head_body,
        "head",
        [root, root_high, head_maps],
        parts=[cotangents[2 * i] for i in range(sub_count // 2)],
        stacks=[to_stack(1, range(2, depth))],
        ids=ids,
        limit=12,
    )
    got = partner(give, "sub", 1)
    gather_turns(1, value, range(2, depth))
    turns.append([[View(root)], []])
    gather_turns(depth - 1, root, [depth])
    low, high, value, root_value = step(
        top_back,
        "top_back",
        [own_ups[-1], other_ups[-1], grad_msg, got],
        stacks=[to_stack(0, range(1, depth)), to_stack(depth - 2, [depth])],
        ids=ids,
    )
    gather_turns(0, value, range(1, depth))
    gather_turns(depth - 2, root_value, [depth])
    for stage in reversed(range(1, depth - 2)):
        stack_turns(stage, [depth])
    turns[depth][1] = turns[depth][0]
    first_inputs = turns[0][0] + turns[0][1] + turns[depth][0]
    second_inputs = [view for entry in turns[1:depth] for turn in entry for view in turn]

    lows, highs = [None] * depth, [None] * depth
    lows[-1], highs[-1] = low, partner(high, "sub", 1 << (depth - 1))
    columns = [None] * depth + [[View(grad_value)], [View(grad_gate)]]

    def groups_of(stage):
        return [
            [View(lows[level]), View(highs[level])] if columns[level] is None else columns[level]
            for level in range(stage, depth)
        ]

    def spread(stage, keeps, send):
        got = partner(send, "sub", 1 << stage)
        at = 0
        for level, keep in zip(range(stage, depth + 2), keeps):
            span = keep.shape[1]
            columns[level] = [View(keep), View(got, None, (at, at + span))]
            at += span

    def columns_of(level, turn):
        if level == depth:
            return columns[depth + turn]
        if level == 0:
            return [columns[0][turn]]
        count = rows >> level
        return [
            view.part(i * count, (i + 1) * count)
            for view in columns[level]
            for i in range(turn, view.shape[0] // count, 2)
        ]

    far_got = []
    for level in reversed(range(depth - 1)):
        above = level + 1
        far = {depth - 2: first_inputs, 0: second_inputs}.get(level)
        low, high, *rest = step(
            down_back,
            "down_back",
            [own_ups[level], other_ups[level], weights[above], lows[above], highs[above]],
            halves=groups_of(above),
            fixed=columns[depth:],
            level=above,
            far=far,
            ids=ids,
            limit=12,
        )
        lows[level] = low
        highs[level] = partner(high, "sub", 1 << level)
        if far:
            far_got.append(partner(rest.pop(), "rep", 2))
        spread(above, rest[:-1], rest[-1])

    lows[0] = after(lows[0], far_got[0])
    back0, back1, pair_back, *rest = step(
        mid_back,
        "mid_back",
        [term0, near0, far_pair, weights[0], lows[0], highs[0]],
        halves=groups_of(0),
        level=0,
        ids=ids,
        limit=12,
    )
    back1 = partner(back1, "rep", 1)
    pair_back = partner(pair_back, "rep", 2)
    spread(0, rest[:-1], rest[-1])
    first = leaf_first(placed[:2], [back0, back1], leaf_w, mid_w)
    groups = [
        [view for turn in range(2) for view in columns_of(level, turn)]
        for level in range(depth + 1)
    ]
    groups[0][0] = groups[0][0].gated(first)
    own_grads = side_by_side(groups)
    far_grads = partner(own_grads, "rep", 2)
    near_grads = partner(own_grads, "rep", 1)
    back2, back3 = fused(far_back, "far_back", after(pair_back, own_grads), term2, near2)
    back3 = partner(back3, "rep", 1)
    inputs = first_inputs + second_inputs
    near_got = partner(near_inputs([inputs[0].gated(back2)] + inputs[1:], far_got, ids), "rep", 1)
    leaf_grad, mid_grad = leaf_backward(
        placed, [msg0, msg1, msg2, msg3], [back0, back1, back2, back3], leaf_w, mid_w, first
    )
    grads = [own_grads, far_grads, near_grads]
    grads.append(partner(after(far_grads, leaf_grad), "rep", 1))
    upper = upper_grads(turns, far_got, near_got, grads, ids)
    return leaf_grad[None], mid_grad[None, None], upper[None]


def solution(mesh):
    placed = (
        P("rep", "sub", None),
        P("sub"),
        P(("sub", "rep"), None, None, None),
        P("sub", "rep", None, None),
        P("sub", None, None, None),
        P("rep", "sub"),
    )
    return jax.shard_map(
        on_device,
        mesh=mesh,
        in_specs=placed,
        out_specs=(
            P(("sub", "rep"), None, None, None),
            P("sub", "rep", None, None),
            P("sub", "rep", None, None),
        ),
        check_vma=False,
    )
```
